32 devices in a mesh: dp: 8 (over z, x), ctx: 2 (over y), tensor: 2 (over core).
Axes of the slice: x: 2, y: 2, z: 4, core: 2. Of those that a mesh axis runs over, the one named last changes fastest.
Arguments:
- tokens: bfloat16 [8, 1024, 1024], P('dp', ('ctx', 'tensor')), may hold values from -6 to 6
- places: int32 [8, 1024], P('dp', 'ctx'), may hold values from 0 to 1023, as said below
- attn_gain: float32 [1024], P('dp'), may hold values from 0.25 to 1.75
- w_query: float32 [1024, 2048], P('dp', 'tensor'), may hold values from -0.1875 to 0.1875
- w_key: float32 [1024, 1024], P('dp', 'tensor'), may hold values from -0.1875 to 0.1875
- w_value: float32 [1024, 1024], P('dp', 'tensor'), may hold values from -0.1875 to 0.1875
- q_gain: float32 [128], P('dp'), may hold values from 1 to 2
- k_gain: float32 [128], P('dp'), may hold values from 1 to 2
- w_out: float32 [2048, 1024], P('tensor', 'dp'), may hold values from -1 to 1
- mlp_gain: float32 [1024], P('dp'), may hold values from 0.25 to 1.75
- w_gate: float32 [1024, 3072], P('dp', 'tensor'), may hold values from -0.1875 to 0.1875
- w_up: float32 [1024, 3072], P('dp', 'tensor'), may hold values from -0.1875 to 0.1875
- w_down: float32 [3072, 1024], P('tensor', 'dp'), may hold values from -0.109375 to 0.109375
- cotangent: bfloat16 [8, 1024, 1024], P('dp', ('ctx', 'tensor')), may hold values from -6 to 6
Outputs:
- out: float32 [8, 1024, 1024], P('dp', ('ctx', 'tensor'))
- grad_in: float32 [8, 1024, 1024], P('dp', ('ctx', 'tensor'))
- grad_attn_gain: float32 [1024], replicated
- grad_w_query: float32 [1024, 2048], P(('dp', 'ctx'), 'tensor')
- grad_w_key: float32 [1024, 1024], P(('dp', 'ctx'), 'tensor')
- grad_w_value: float32 [1024, 1024], P(('dp', 'ctx'), 'tensor')
- grad_q_gain: float32 [128], replicated
- grad_k_gain: float32 [128], replicated
- grad_w_out: float32 [2048, 1024], P('tensor', ('dp', 'ctx'))
- grad_mlp_gain: float32 [1024], replicated
- grad_w_gate: float32 [1024, 3072], P(('dp', 'ctx'), 'tensor')
- grad_w_up: float32 [1024, 3072], P(('dp', 'ctx'), 'tensor')
- grad_w_down: float32 [3072, 1024], P('tensor', ('dp', 'ctx'))
The draws below stay inside these ranges and needn't reach their ends.
Inputs may be any that keep to these rules, and one draw needn't show every extreme that they name: Each row of places is a permutation of 0 to 1023: with n the number of ctx devices, the positions fall into 2 n runs of 1024 / (2 n) in a row, run k covering k * 1024 / (2 n) to (k + 1) * 1024 / (2 n) - 1; the stored tokens of ctx device c hold run c in their first half and run 2 n - 1 - c in their second half, in a drawn order within each run.
All inputs are finite; a program needn't handle non-finite values.
Results may differ from the reference program's by a relative error of at most 0.015.
The reference program's roundings to bfloat16 on the way count: a program that leaves them out, or rounds other values in their place, can miss the bound.
Values may be sent and summed in bfloat16 or wider, within the bound.
No kernel may reach another device: no remote copies, remote signals or barrier semaphores. Data moves between devices by JAX's collectives and lax.ppermute only.
A program may use at most 192 MiB of HBM per device.

```python
import math
import jax
import jax.numpy as jnp
from jax import lax

D = 1024
HQ = 16
KVH = 8
HD = 128
FF = 3072
LEN = 1024
SEQ_ALL = 8
N_CTX = 2


def draw_places(key, part):
    run_length = LEN // (2 * N_CTX)
    run_keys = jax.random.split(key, SEQ_ALL * 2 * N_CTX)
    shuffled = jax.vmap(lambda one_key: jax.random.permutation(one_key, run_length))(run_keys)
    shuffled = shuffled.astype(jnp.int32).reshape(SEQ_ALL, 2 * N_CTX, run_length)
    ranks = jnp.arange(N_CTX, dtype=jnp.int32)
    run_order = jnp.stack([ranks, 2 * N_CTX - 1 - ranks], axis=1).reshape(2 * N_CTX)
    placed = run_order[None, :, None] * run_length + shuffled
    return placed.reshape(SEQ_ALL, LEN).astype(jnp.int32)


def raised(array, rng, source, target, parts, factor):
    owner, partner = [(jnp.arange(array.shape[position]) // (array.shape[position] // parts)).reshape([-1 if axis == position else 1 for axis in range(array.ndim)]) for position in (source, target)]
    chosen = jax.random.permutation(rng, parts)[partner]
    strong = (owner == chosen) | (owner == (partner + parts // 2) % parts)
    return jnp.where(strong, factor * array, array)


def shard_levels(rng, extent, cuts, least, top_value):
    factor_of = 1.0
    for dim, shards_of in cuts:
        heights = jax.random.uniform(jax.random.fold_in(jax.random.fold_in(rng, 6), dim), (shards_of,), jnp.float32, least / len(cuts), top_value / len(cuts))
        factor_of = factor_of * jnp.repeat(jnp.exp(heights), extent[dim] // shards_of).reshape((-1,) + (1,) * (len(extent) - 1 - dim))
    return factor_of


def noise(key, shape, deviation, limit, cuts=(), kind=jnp.bfloat16):
    entries = jax.random.normal(key, shape, jnp.float32) * deviation
    if len(cuts) > 0:
        entries = shard_levels(key, shape, cuts, -0.22, 0.18) * entries
    return jnp.clip(entries, min=-limit, max=limit).astype(kind)


def bell_draw_with(stream_key, shape, spread, reach, cuts, heavy, kind=jnp.bfloat16):
    result = spread * jax.random.normal(stream_key, shape, jnp.float32)
    if cuts:
        result = result * shard_levels(stream_key, shape, cuts, -0.22, 0.18)
    return jnp.clip(raised(result, jax.random.fold_in(stream_key, 3), *heavy), -reach, reach).astype(kind)


def setup_inputs(seed: int = 0) -> dict:
    arg_keys = jax.random.split(jax.random.key(seed), 15)
    return {
        "tokens": noise(arg_keys[0], (SEQ_ALL, LEN, D), 1.0, 6.0, ((0, 8), (1, 4))),
        "places": draw_places(jax.random.fold_in(arg_keys[14], 71), 0),
        "attn_gain": jnp.clip(1.0 + 0.15 * jax.random.normal(arg_keys[2], (D,), jnp.float32), 0.25, 1.75),
        "w_query": noise(arg_keys[3], (D, HQ * HD), D ** -0.5, 0.1875, ((0, 8), (1, 2)), jnp.float32),
        "w_key": noise(arg_keys[4], (D, KVH * HD), D ** -0.5, 0.1875, ((0, 8), (1, 2)), jnp.float32),
        "w_value": noise(arg_keys[5], (D, KVH * HD), D ** -0.5, 0.1875, ((0, 8), (1, 2)), jnp.float32),
        "q_gain": jnp.clip(1.0 + 1.0 * jax.random.uniform(arg_keys[6], (HD,), jnp.float32) ** shard_levels(arg_keys[6], (HD,), ((0, 8),), -0.2, 0.2), 1.0, 2.0),
        "k_gain": jnp.clip(1.0 + 1.0 * jax.random.uniform(arg_keys[7], (HD,), jnp.float32) ** shard_levels(arg_keys[7], (HD,), ((0, 8),), -0.2, 0.2), 1.0, 2.0),
        "w_out": noise(arg_keys[8], (HQ * HD, D), (HQ * HD // 64) ** -0.5, 1.0, ((0, 2), (1, 8)), jnp.float32),
        "mlp_gain": jnp.clip(1.0 + 0.15 * jax.random.normal(arg_keys[9], (D,), jnp.float32), 0.25, 1.75),
        "w_gate": noise(arg_keys[10], (D, FF), D ** -0.5, 0.1875, ((0, 8), (1, 2)), jnp.float32),
        "w_up": noise(arg_keys[11], (D, FF), D ** -0.5, 0.1875, ((0, 8), (1, 2)), jnp.float32),
        "w_down": noise(arg_keys[12], (FF, D), FF ** -0.5, 0.109375, ((0, 2), (1, 8)), jnp.float32),
        "cotangent": bell_draw_with(arg_keys[13], (SEQ_ALL, LEN, D), 1.0, 6.0, ((0, 8), (1, 4)), (0, 2, 8, 2.0)),
    }


@jax.custom_vjp
def low(v):
    return lax.optimization_barrier(v.astype(jnp.bfloat16)).astype(jnp.float32)

@jax.custom_vjp
def low_back(v):
    return v

def low_keep(v):
    return (low(v), None)

def low_pass(kept, grad):
    return (grad,)

def back_keep(v):
    return (v, None)

def back_low(kept, grad):
    return (low(grad),)
low.defvjp(low_keep, low_pass)
low_back.defvjp(back_keep, back_low)
EPSILON = 1e-06
ROPE_BASE = 1000000.0
NEGATIVE = -1e+30
PRECISE = lax.Precision.HIGHEST

def matmul(left, right):
    return jnp.dot(left, right, precision=PRECISE, preferred_element_type=jnp.float32)

def row_norm(source, gain):
    factor = lax.rsqrt(lax.optimization_barrier(jnp.mean(source * source, axis=-1, keepdims=True)) + EPSILON)
    return source * factor * gain

def rope_tables(positions):
    freq_index = jnp.arange(HD // 2, dtype=jnp.float32)
    inverse = ROPE_BASE ** (-2.0 * freq_index / HD)
    angles = positions.astype(jnp.float32)[:, None] * inverse[None, :]
    cosine = jnp.concatenate([jnp.cos(angles), jnp.cos(angles)], axis=-1)
    sine_table = jnp.concatenate([jnp.sin(angles), jnp.sin(angles)], axis=-1)
    return (cosine[:, None, :], sine_table[:, None, :])

def rotate(source, cosine, sine_table):
    half_width = source.shape[-1] // 2
    turned = jnp.concatenate([-source[..., half_width:], source[..., :half_width]], axis=-1)
    return source * cosine + turned * sine_table

def attention(queries, key_rows, value_rows, positions):
    group_size = HQ // KVH
    keys_all = jnp.repeat(key_rows, group_size, axis=1)
    values_all = jnp.repeat(value_rows, group_size, axis=1)
    block_rows = math.gcd(LEN, 512)
    score_scale = HD ** (-0.5)

    def one_block(pieces):
        query_rows, row_places = pieces
        scores = low_back(jnp.einsum('qhd,khd->hqk', query_rows, keys_all, precision=PRECISE) * score_scale)
        visible = positions[None, None, :] <= row_places[None, :, None]
        attn_probs = jax.nn.softmax(jnp.where(visible, scores, NEGATIVE), axis=-1)
        return jnp.einsum('hqk,khd->qhd', low(attn_probs), values_all, precision=PRECISE)
    blocks = lax.map(jax.checkpoint(one_block), (queries.reshape(LEN // block_rows, block_rows, HQ, HD), positions.reshape(LEN // block_rows, block_rows)))
    return blocks.reshape(LEN, HQ, HD)

def block_layer(source, positions, params):
    attn_g, query_w, key_w, value_w, qnorm_g, knorm_g, out_w, mlp_g, gate_w, up_w, down_w = [low(weight) for weight in params]
    normed = low(row_norm(source, attn_g))
    query_raw = low_back(matmul(normed, query_w)).reshape(LEN, HQ, HD)
    key_raw = low_back(matmul(normed, key_w)).reshape(LEN, KVH, HD)
    value_rows = low(low_back(matmul(normed, value_w))).reshape(LEN, KVH, HD)
    cosine, sine_table = rope_tables(positions)
    queries = low(rotate(row_norm(query_raw, qnorm_g), cosine, sine_table))
    key_rows = low(rotate(row_norm(key_raw, knorm_g), cosine, sine_table))
    mixed = attention(queries, key_rows, value_rows, positions)
    mixed = low(low_back(mixed.reshape(LEN, HQ * HD)))
    middle = source + low_back(matmul(mixed, out_w))
    normed_two = low(row_norm(middle, mlp_g))
    gate_act = low_back(matmul(normed_two, gate_w))
    up_act = low_back(matmul(normed_two, up_w))
    hidden = low(jax.nn.silu(gate_act) * up_act)
    return middle + low_back(matmul(hidden, down_w))

def reference(tokens, places, attn_gain, w_query, w_key, w_value, q_gain, k_gain, w_out, mlp_gain, w_gate, w_up, w_down, cotangent):
    params = (attn_gain, w_query, w_key, w_value, q_gain, k_gain, w_out, mlp_gain, w_gate, w_up, w_down)

    def one_sequence(totals, pieces):
        seq_tokens, seq_places, seq_grad = pieces

        def forward(source, weights):
            return block_layer(source, seq_places, weights)
        layer_out, pullback = jax.vjp(forward, seq_tokens.astype(jnp.float32), params)
        grad_tokens, grad_params = pullback(seq_grad.astype(jnp.float32))
        totals = jax.tree.map(jnp.add, totals, grad_params)
        return (totals, (layer_out, grad_tokens))
    zero_grads = jax.tree.map(jnp.zeros_like, params)
    totals, results = lax.scan(one_sequence, zero_grads, (tokens, places, cotangent))
    return (results[0], results[1], totals[0], totals[1], totals[2], totals[3], totals[4], totals[5], totals[6], totals[7], totals[8], totals[9], totals[10])
```

```python
import functools

import jax
import jax.numpy as jnp
from jax import lax
from jax.experimental import pallas as pl
from jax.experimental.pallas import tpu as pltpu
from jax.sharding import PartitionSpec as P

HD = 128


EPSILON = 1e-06
ROPE_BASE = 1000000.0
NEGATIVE = -1e30


def gather_rows(source):
    return lax.all_gather(source, "tensor", axis=1, tiled=True)


def reduce_rows(partial_sum):
    return lax.psum_scatter(partial_sum, "tensor", scatter_dimension=1, tiled=True)


def norm_forward(source, gain):
    factor = lax.rsqrt(jnp.mean(source * source, axis=-1, keepdims=True) + EPSILON)
    unit = source * factor
    return (unit * gain, unit, factor)


def norm_backward(grad_normed, unit, factor, gain):
    grad_unit = grad_normed * gain
    grad_gain = jnp.sum((grad_normed * unit).reshape(-1, unit.shape[-1]), axis=0)
    grad_source = factor * (grad_unit - unit * jnp.mean(grad_unit * unit, axis=-1, keepdims=True))
    return (grad_source, grad_gain)


def rope_tables(positions):
    freq_index = jnp.arange(HD // 2, dtype=jnp.float32)
    inverse = ROPE_BASE ** (-2.0 * freq_index / HD)
    angles = positions.astype(jnp.float32)[..., None] * inverse
    cosine = jnp.concatenate([jnp.cos(angles), jnp.cos(angles)], axis=-1)
    sine_table = jnp.concatenate([jnp.sin(angles), jnp.sin(angles)], axis=-1)
    return (cosine[..., None, :], sine_table[..., None, :])


def rotate(source, cosine, sine_table):
    half_width = source.shape[-1] // 2
    turned = jnp.concatenate([-source[..., half_width:], source[..., :half_width]], axis=-1)
    return source * cosine + turned * sine_table


def rotate_back(grad_rotated, cosine, sine_table):
    half_width = grad_rotated.shape[-1] // 2
    sined = grad_rotated * sine_table
    turned = jnp.concatenate([sined[..., half_width:], -sined[..., :half_width]], axis=-1)
    return grad_rotated * cosine + turned


def to_blocks(heads_last, kv_heads):
    seqs, row_count, width = heads_last.shape
    group_size = width // (kv_heads * HD)
    shaped = heads_last.reshape(seqs, row_count, kv_heads, group_size, HD)
    return shaped.transpose(0, 2, 3, 1, 4).reshape(seqs * kv_heads, group_size, row_count, HD)


def from_blocks(blocked, seqs):
    count, group_size, row_count, width = blocked.shape
    kv_heads = count // seqs
    shaped = blocked.reshape(seqs, kv_heads, group_size, row_count, width)
    return shaped.transpose(0, 3, 1, 2, 4).reshape(seqs, row_count, kv_heads * group_size * width)


def masked_scores(queries, key_rows, query_places, key_places):
    scores = jnp.einsum(
        "hqd,kd->hqk", queries, key_rows, preferred_element_type=jnp.float32
    ) * HD ** (-0.5)
    visible = key_places[None, None, :] <= query_places[None, :, None]
    return jnp.where(visible, scores, NEGATIVE)


def recompute(queries, key_rows, lse_rows, query_places, key_places):
    return jnp.exp(masked_scores(queries, key_rows, query_places, key_places) - lse_rows[..., None])


def forward_block(pieces):
    queries, key_rows, value_rows, query_places, key_places = pieces
    scores = masked_scores(queries, key_rows, query_places, key_places)
    row_max = jnp.max(scores, axis=-1, keepdims=True)
    raised = jnp.exp(scores - row_max)
    row_total = jnp.sum(raised, axis=-1, keepdims=True)
    attn_probs = raised / row_total
    mixed = jnp.einsum(
        "hqk,kd->hqd",
        attn_probs.astype(jnp.bfloat16),
        value_rows,
        preferred_element_type=jnp.float32,
    )
    return (mixed, (row_max + jnp.log(row_total))[..., 0])


def full_block(pieces):
    queries, grad_mixed, lse_rows, query_places, key_rows, value_rows, key_places = pieces
    attn_probs = recompute(queries, key_rows, lse_rows, query_places, key_places)
    grad_probs = jnp.einsum(
        "hqd,kd->hqk", grad_mixed, value_rows, preferred_element_type=jnp.float32
    )
    row_delta = jnp.sum(attn_probs * grad_probs, axis=-1)
    grad_scores = (attn_probs * (grad_probs - row_delta[..., None])).astype(jnp.bfloat16)
    grad_queries = jnp.einsum(
        "hqk,kd->hqd", grad_scores, key_rows, preferred_element_type=jnp.float32
    ) * HD ** (-0.5)
    grad_keys = jnp.einsum(
        "hqk,hqd->kd", grad_scores, queries, preferred_element_type=jnp.float32
    ) * HD ** (-0.5)
    grad_values = jnp.einsum(
        "hqk,hqd->kd",
        attn_probs.astype(jnp.bfloat16),
        grad_mixed,
        preferred_element_type=jnp.float32,
    )
    return (grad_queries, grad_keys, grad_values)


def split_body(
    tokens,
    places,
    attn_gain,
    w_query,
    w_key,
    w_value,
    q_gain,
    k_gain,
    w_out,
    mlp_gain,
    w_gate,
    w_up,
    w_down,
    cotangent,
):
    seqs, local_rows, width = tokens.shape
    attn_set = (
        lax.all_gather(attn_gain.astype(jnp.bfloat16), "dp", axis=0, tiled=True),
        lax.all_gather(w_query.astype(jnp.bfloat16), "dp", axis=0, tiled=True),
        lax.all_gather(w_key.astype(jnp.bfloat16), "dp", axis=0, tiled=True),
        lax.all_gather(w_value.astype(jnp.bfloat16), "dp", axis=0, tiled=True),
        lax.all_gather(q_gain.astype(jnp.bfloat16), "dp", axis=0, tiled=True),
        lax.all_gather(k_gain.astype(jnp.bfloat16), "dp", axis=0, tiled=True),
        lax.all_gather(w_out.astype(jnp.bfloat16), "dp", axis=1, tiled=True),
    )
    gain_one, query_weight, key_weight, value_weight, query_gain, key_gain, out_weight = attn_set
    mlp_set = (
        lax.all_gather(mlp_gain.astype(jnp.bfloat16), "dp", axis=0, tiled=True),
        lax.all_gather(w_gate.astype(jnp.bfloat16), "dp", axis=0, tiled=True),
        lax.all_gather(w_up.astype(jnp.bfloat16), "dp", axis=0, tiled=True),
        lax.all_gather(w_down.astype(jnp.bfloat16), "dp", axis=1, tiled=True),
    )
    gain_two, gate_weight, up_weight, down_weight = mlp_set
    gain_one = gain_one.astype(jnp.float32)
    gain_two = gain_two.astype(jnp.float32)
    query_gain = query_gain.astype(jnp.float32)
    key_gain = key_gain.astype(jnp.float32)
    source = tokens.astype(jnp.float32)
    normed_one, unit_one, factor_one = norm_forward(source, gain_one)
    rows_one = gather_rows(normed_one.astype(jnp.bfloat16))
    group_rows = rows_one.shape[1]
    flat_one = rows_one.reshape(seqs * group_rows, width)
    query_raw = jnp.dot(flat_one, query_weight, preferred_element_type=jnp.float32).reshape(
        seqs, group_rows, -1, HD
    )
    key_raw = jnp.dot(flat_one, key_weight, preferred_element_type=jnp.float32).reshape(
        seqs, group_rows, -1, HD
    )
    value_rows = (
        jnp.dot(flat_one, value_weight, preferred_element_type=jnp.float32)
        .astype(jnp.bfloat16)
        .reshape(seqs, group_rows, -1)
    )
    kv_heads = key_raw.shape[2]
    cosine, sine_table = rope_tables(places)
    query_normed, query_unit, query_factor = norm_forward(query_raw, query_gain)
    queries = (
        rotate(query_normed, cosine, sine_table).astype(jnp.bfloat16).reshape(seqs, group_rows, -1)
    )
    key_normed, key_unit, key_factor = norm_forward(key_raw, key_gain)
    key_rows = (
        rotate(key_normed, cosine, sine_table).astype(jnp.bfloat16).reshape(seqs, group_rows, -1)
    )
    key_all, value_all, places_all = (
        lax.all_gather(key_rows, "ctx", axis=1, tiled=True),
        lax.all_gather(value_rows, "ctx", axis=1, tiled=True),
        lax.all_gather(places, "ctx", axis=1, tiled=True),
    )
    query_blocks = to_blocks(queries, kv_heads)
    key_blocks = to_blocks(key_all, kv_heads)[:, 0]
    value_blocks = to_blocks(value_all, kv_heads)[:, 0]
    query_places = jnp.repeat(places, kv_heads, axis=0)
    key_places = jnp.repeat(places_all, kv_heads, axis=0)
    mixed_blocks, lse_blocks = lax.map(
        forward_block, (query_blocks, key_blocks, value_blocks, query_places, key_places)
    )
    mixed = from_blocks(mixed_blocks, seqs).astype(jnp.bfloat16).reshape(seqs * group_rows, -1)
    attn_part = jnp.dot(mixed, out_weight, preferred_element_type=jnp.float32).reshape(
        seqs, group_rows, width
    )
    middle = source + reduce_rows(attn_part)
    normed_two, unit_two, factor_two = norm_forward(middle, gain_two)
    rows_two = gather_rows(normed_two.astype(jnp.bfloat16)).reshape(seqs * group_rows, width)
    gate_act = jnp.dot(rows_two, gate_weight, preferred_element_type=jnp.float32)
    up_act = jnp.dot(rows_two, up_weight, preferred_element_type=jnp.float32)
    sigmoid_gate = jax.nn.sigmoid(gate_act)
    silu_gate = gate_act * sigmoid_gate
    hidden = (silu_gate * up_act).astype(jnp.bfloat16)
    mlp_part = jnp.dot(hidden, down_weight, preferred_element_type=jnp.float32).reshape(
        seqs, group_rows, width
    )
    layer_out = middle + reduce_rows(mlp_part)
    grad_rows = gather_rows(cotangent).reshape(seqs * group_rows, width)
    down_grad = jnp.einsum("tf,td->fd", hidden, grad_rows, preferred_element_type=jnp.float32)
    grad_hidden = jnp.einsum(
        "td,fd->tf", grad_rows, down_weight, preferred_element_type=jnp.float32
    )
    grad_gate = (
        grad_hidden * up_act * sigmoid_gate * (1.0 + gate_act * (1.0 - sigmoid_gate))
    ).astype(jnp.bfloat16)
    grad_up = (grad_hidden * silu_gate).astype(jnp.bfloat16)
    gate_grad = jnp.einsum("td,tf->df", rows_two, grad_gate, preferred_element_type=jnp.float32)
    up_grad = jnp.einsum("td,tf->df", rows_two, grad_up, preferred_element_type=jnp.float32)
    grad_normed_two = jnp.einsum(
        "tf,df->td", grad_gate, gate_weight, preferred_element_type=jnp.float32
    ) + jnp.einsum("tf,df->td", grad_up, up_weight, preferred_element_type=jnp.float32)
    grad_normed_two = reduce_rows(grad_normed_two.reshape(seqs, group_rows, width))
    grad_source_two, grad_gain_two = norm_backward(grad_normed_two, unit_two, factor_two, gain_two)
    grad_middle = cotangent.astype(jnp.float32) + grad_source_two
    grad_branch = gather_rows(grad_middle.astype(jnp.bfloat16)).reshape(seqs * group_rows, width)
    out_grad = jnp.einsum("tc,td->cd", mixed, grad_branch, preferred_element_type=jnp.float32)
    grad_mixed = (
        jnp.einsum("td,cd->tc", grad_branch, out_weight, preferred_element_type=jnp.float32)
        .astype(jnp.bfloat16)
        .reshape(seqs, group_rows, -1)
    )
    grad_blocks = to_blocks(grad_mixed, kv_heads)
    grad_query_blocks, grad_key_blocks, grad_value_blocks = lax.map(
        full_block,
        (query_blocks, grad_blocks, lse_blocks, query_places, key_blocks, value_blocks, key_places),
    )
    key_terms = jnp.concatenate(
        [
            from_blocks(grad_key_blocks[:, None], seqs),
            from_blocks(grad_value_blocks[:, None], seqs),
        ],
        axis=-1,
    )
    key_sums = lax.psum_scatter(
        key_terms.astype(jnp.bfloat16), "ctx", scatter_dimension=1, tiled=True
    ).astype(jnp.float32)
    half_width = key_sums.shape[-1] // 2
    grad_keys = key_sums[..., :half_width]
    grad_values = key_sums[..., half_width:]
    grad_query_rot = from_blocks(grad_query_blocks, seqs).reshape(seqs, group_rows, -1, HD)
    grad_query_raw, grad_q_part = norm_backward(
        rotate_back(grad_query_rot, cosine, sine_table), query_unit, query_factor, query_gain
    )
    grad_query_raw = grad_query_raw.astype(jnp.bfloat16).reshape(seqs * group_rows, -1)
    grad_key_rot = grad_keys.reshape(seqs, group_rows, kv_heads, HD)
    grad_key_raw, grad_k_part = norm_backward(
        rotate_back(grad_key_rot, cosine, sine_table), key_unit, key_factor, key_gain
    )
    grad_key_raw = grad_key_raw.astype(jnp.bfloat16).reshape(seqs * group_rows, -1)
    grad_value_raw = grad_values.astype(jnp.bfloat16).reshape(seqs * group_rows, -1)
    query_grad = jnp.einsum(
        "td,tc->dc", flat_one, grad_query_raw, preferred_element_type=jnp.float32
    )
    key_grad = jnp.einsum("td,tc->dc", flat_one, grad_key_raw, preferred_element_type=jnp.float32)
    value_grad = jnp.einsum(
        "td,tc->dc", flat_one, grad_value_raw, preferred_element_type=jnp.float32
    )
    grad_normed_one = jnp.einsum(
        "tc,dc->td", grad_query_raw, query_weight, preferred_element_type=jnp.float32
    )
    grad_normed_one = grad_normed_one + jnp.einsum(
        "tc,dc->td", grad_key_raw, key_weight, preferred_element_type=jnp.float32
    )
    grad_normed_one = grad_normed_one + jnp.einsum(
        "tc,dc->td", grad_value_raw, value_weight, preferred_element_type=jnp.float32
    )
    grad_normed_one = reduce_rows(grad_normed_one.reshape(seqs, group_rows, width))
    grad_source_one, grad_gain_one = norm_backward(grad_normed_one, unit_one, factor_one, gain_one)
    grad_tokens = grad_middle + grad_source_one
    weight_grads = (
        lax.psum_scatter(query_grad, ("dp", "ctx"), scatter_dimension=0, tiled=True),
        lax.psum_scatter(key_grad, ("dp", "ctx"), scatter_dimension=0, tiled=True),
        lax.psum_scatter(value_grad, ("dp", "ctx"), scatter_dimension=0, tiled=True),
        lax.psum_scatter(out_grad, ("dp", "ctx"), scatter_dimension=1, tiled=True),
        lax.psum_scatter(gate_grad, ("dp", "ctx"), scatter_dimension=0, tiled=True),
        lax.psum_scatter(up_grad, ("dp", "ctx"), scatter_dimension=0, tiled=True),
        lax.psum_scatter(down_grad, ("dp", "ctx"), scatter_dimension=1, tiled=True),
    )
    gain_grads = lax.psum(
        (grad_gain_one, grad_q_part, grad_k_part, grad_gain_two), ("dp", "ctx", "tensor")
    )
    return (
        layer_out,
        grad_tokens,
        gain_grads[0],
        weight_grads[0],
        weight_grads[1],
        weight_grads[2],
        gain_grads[1],
        gain_grads[2],
        weight_grads[3],
        gain_grads[3],
        weight_grads[4],
        weight_grads[5],
        weight_grads[6],
    )


NT = (((1,), (1,)), ((), ()))
TN = (((0,), (0,)), ((), ()))
NN = (((1,), (0,)), ((), ()))
SCALE = HD ** (-0.5)


def dot(left, right, dims=NN):
    return lax.dot_general(left, right, dims, preferred_element_type=jnp.float32)


def sort_runs(block_of, run, *pairs):
    for index in range(4):
        source = pl.multiple_of(block_of[index] * run, run)
        for target, origin in pairs:
            target[pl.ds(index * run, run), :] = origin[pl.ds(source, run), :]


def raw_scores(keys, query, visible, run):
    scores = dot(keys, query, NT) * SCALE
    count = scores.shape[0]
    last = jnp.where(visible, scores[count - run :], NEGATIVE)
    if count == run:
        return last
    return jnp.concatenate([scores[: count - run], last], axis=0)


def forward_kernel(
    block_of, q_ref, k_ref, v_ref, column_ref, row_ref, mixed_ref, lse_ref, keys, values, columns
):
    run = q_ref.shape[0] // 4
    sort_runs(block_of, run, (keys, k_ref), (values, v_ref), (columns, column_ref))
    for index in range(4):
        count = run * (index + 1)
        rows = pl.ds(pl.multiple_of(block_of[index] * run, run), run)
        visible = columns[pl.ds(count - run, run), :] <= row_ref[:, rows]
        for head in range(q_ref.shape[1] // HD):
            lanes = pl.ds(head * HD, HD)
            scores = raw_scores(keys[:count], q_ref[rows, lanes], visible, run)
            row_max = jnp.max(scores, axis=0, keepdims=True)
            raised = jnp.exp(scores - row_max)
            row_total = jnp.sum(raised, axis=0, keepdims=True)
            probs = (raised * (1.0 / row_total)).astype(jnp.bfloat16)
            mixed_ref[rows, lanes] = dot(probs, values[:count], TN).astype(jnp.bfloat16)
            lse_ref[pl.ds(head, 1), rows] = row_max + jnp.log(row_total)


def backward_kernel(
    block_of,
    q_ref,
    k_ref,
    v_ref,
    g_ref,
    lse_ref,
    column_ref,
    row_ref,
    dq_ref,
    dk_ref,
    dv_ref,
    keys,
    values,
    columns,
    key_sum,
    value_sum,
):
    run = q_ref.shape[0] // 4
    sort_runs(block_of, run, (keys, k_ref), (values, v_ref), (columns, column_ref))
    key_sum[...] = jnp.zeros_like(key_sum)
    value_sum[...] = jnp.zeros_like(value_sum)
    for index in range(4):
        count = run * (index + 1)
        rows = pl.ds(pl.multiple_of(block_of[index] * run, run), run)
        visible = columns[pl.ds(count - run, run), :] <= row_ref[:, rows]
        for head in range(q_ref.shape[1] // HD):
            lanes = pl.ds(head * HD, HD)
            query = q_ref[rows, lanes]
            grad = g_ref[rows, lanes]
            scores = raw_scores(keys[:count], query, visible, run)
            probs = jnp.exp(scores - lse_ref[pl.ds(head, 1), rows])
            grad_probs = dot(values[:count], grad, NT)
            delta = jnp.sum(probs * grad_probs, axis=0, keepdims=True)
            grad_scores = (probs * (grad_probs - delta)).astype(jnp.bfloat16)
            value_sum[:count, :] += dot(probs.astype(jnp.bfloat16), grad)
            key_sum[:count, :] += dot(grad_scores, query)
            dq_ref[rows, lanes] = dot(grad_scores, keys[:count], TN) * SCALE
    for index in range(4):
        rows = pl.ds(pl.multiple_of(block_of[index] * run, run), run)
        dk_ref[rows, :] = key_sum[pl.ds(index * run, run), :] * SCALE
        dv_ref[rows, :] = value_sum[pl.ds(index * run, run), :]


def head_spec(rows, width):
    return pl.BlockSpec((rows, width), lambda group, order: (0, group))


def attend(block_of, queries, keys, values, place_column, place_row):
    rows, width = keys.shape
    groups = width // HD
    pair = queries.shape[1] // groups
    fixed_column = pl.BlockSpec((rows, 1), lambda group, order: (0, 0))
    fixed_row = pl.BlockSpec((1, rows), lambda group, order: (0, 0))
    lse_spec = pl.BlockSpec((None, pair // HD, rows), lambda group, order: (group, 0, 0))
    return pl.pallas_call(
        forward_kernel,
        grid_spec=pltpu.PrefetchScalarGridSpec(
            num_scalar_prefetch=1,
            grid=(groups,),
            in_specs=[
                head_spec(rows, pair),
                head_spec(rows, HD),
                head_spec(rows, HD),
                fixed_column,
                fixed_row,
            ],
            out_specs=[head_spec(rows, pair), lse_spec],
            scratch_shapes=[
                pltpu.VMEM((rows, HD), jnp.bfloat16),
                pltpu.VMEM((rows, HD), jnp.bfloat16),
                pltpu.VMEM((rows, 1), jnp.int32),
            ],
        ),
        out_shape=[
            jax.ShapeDtypeStruct(queries.shape, jnp.bfloat16),
            jax.ShapeDtypeStruct((groups, pair // HD, rows), jnp.float32),
        ],
        compiler_params=pltpu.CompilerParams(vmem_limit_bytes=40 * 1024 * 1024),
        cost_estimate=pl.CostEstimate(
            flops=3 * rows * rows * queries.shape[1],
            bytes_accessed=8 * rows * queries.shape[1],
            transcendentals=rows * rows * queries.shape[1] // HD,
        ),
    )(block_of, queries, keys, values, place_column, place_row)


def attend_back(block_of, queries, keys, values, grad_mixed, lse_rows, place_column, place_row):
    rows, width = keys.shape
    groups = width // HD
    pair = queries.shape[1] // groups
    fixed_column = pl.BlockSpec((rows, 1), lambda group, order: (0, 0))
    fixed_row = pl.BlockSpec((1, rows), lambda group, order: (0, 0))
    lse_spec = pl.BlockSpec((None, pair // HD, rows), lambda group, order: (group, 0, 0))
    return pl.pallas_call(
        backward_kernel,
        grid_spec=pltpu.PrefetchScalarGridSpec(
            num_scalar_prefetch=1,
            grid=(groups,),
            in_specs=[
                head_spec(rows, pair),
                head_spec(rows, HD),
                head_spec(rows, HD),
                head_spec(rows, pair),
                lse_spec,
                fixed_column,
                fixed_row,
            ],
            out_specs=[head_spec(rows, pair), head_spec(rows, HD), head_spec(rows, HD)],
            scratch_shapes=[
                pltpu.VMEM((rows, HD), jnp.bfloat16),
                pltpu.VMEM((rows, HD), jnp.bfloat16),
                pltpu.VMEM((rows, 1), jnp.int32),
                pltpu.VMEM((rows, HD), jnp.float32),
                pltpu.VMEM((rows, HD), jnp.float32),
            ],
        ),
        out_shape=[
            jax.ShapeDtypeStruct(queries.shape, jnp.float32),
            jax.ShapeDtypeStruct(keys.shape, jnp.float32),
            jax.ShapeDtypeStruct(keys.shape, jnp.float32),
        ],
        compiler_params=pltpu.CompilerParams(vmem_limit_bytes=40 * 1024 * 1024),
        cost_estimate=pl.CostEstimate(
            flops=7 * rows * rows * queries.shape[1],
            bytes_accessed=16 * rows * queries.shape[1],
            transcendentals=rows * rows * queries.shape[1] // HD,
        ),
    )(block_of, queries, keys, values, grad_mixed, lse_rows, place_column, place_row)


def swap(source, axis, size, bit=1):
    return lax.ppermute(source, axis, [(i, i ^ bit) for i in range(size)])


def group_body(
    dp_size,
    tokens,
    places,
    attn_gain,
    w_query,
    w_key,
    w_value,
    q_gain,
    k_gain,
    w_out,
    mlp_gain,
    w_gate,
    w_up,
    w_down,
    cotangent,
):
    bf16, f32 = jnp.bfloat16, jnp.float32
    run, width = tokens.shape[1:]
    side = lax.axis_index("ctx")
    core = lax.axis_index("tensor")
    member = lax.axis_index("dp")

    def over_core(source):
        return swap(source, "tensor", 2)

    def over_ctx(source):
        return swap(source, "ctx", 2)

    def spread(own):
        half = jnp.concatenate([own, over_ctx(own)], axis=0)
        return jnp.concatenate([half, over_core(half)], axis=0)

    def core_sum(parts):
        half = parts.shape[0] // 2
        return parts[:half] + over_core(parts[half:].astype(bf16)).astype(f32)

    def own_sum(parts):
        summed = core_sum(parts)
        return summed[:run] + over_ctx(summed[run:].astype(bf16)).astype(f32)

    def half_sum(parts):
        summed = core_sum(parts)
        other = over_ctx(summed.astype(bf16)).astype(f32)
        return summed + jnp.concatenate([other[run:], other[:run]], axis=0)

    def mine(source, axis):
        size = source.shape[axis] // 2
        return lax.dynamic_slice_in_dim(source, side * size, size, axis).astype(bf16)

    def gather_small(source):
        bit = 1
        while bit < dp_size:
            other = swap(source, "dp", dp_size, bit)
            first = (member // bit) % 2 == 0
            source = jnp.where(
                first,
                jnp.concatenate([source, other], axis=0),
                jnp.concatenate([other, source], axis=0),
            )
            bit *= 2
        return source

    def sum_small(source):
        source = source + over_core(source)
        source = source + over_ctx(source)
        bit = 1
        while bit < dp_size:
            source = source + swap(source, "dp", dp_size, bit)
            bit *= 2
        return source

    gain_block = attn_gain.shape[0]
    head_block = q_gain.shape[0]
    gains = gather_small(
        jnp.concatenate([attn_gain, mlp_gain, q_gain, k_gain]).astype(bf16)[None]
    ).astype(f32)
    gain_one = gains[:, :gain_block].reshape(-1)
    gain_two = gains[:, gain_block : 2 * gain_block].reshape(-1)
    query_gain = gains[:, 2 * gain_block : 2 * gain_block + head_block].reshape(-1)
    key_gain = gains[:, 2 * gain_block + head_block :].reshape(-1)

    attn_shard = jnp.concatenate(
        [mine(w_query, 1), mine(w_key, 1), mine(w_value, 1), mine(w_out, 0).T], axis=1
    )
    mlp_shard = jnp.concatenate([mine(w_gate, 1), mine(w_up, 1), mine(w_down, 0).T], axis=1)
    attn_weight = lax.all_gather(attn_shard, "dp", axis=0, tiled=True)
    mlp_weight = lax.all_gather(mlp_shard, "dp", axis=0, tiled=True)
    q_width = w_query.shape[1] // 2
    k_width = w_key.shape[1] // 2
    kv_end = q_width + 2 * k_width
    hidden_width = w_gate.shape[1] // 2
    qkv_weight = attn_weight[:, :kv_end]
    out_weight = attn_weight[:, kv_end:]
    gate_up_weight = mlp_weight[:, : 2 * hidden_width]
    down_weight = mlp_weight[:, 2 * hidden_width :]

    rows_all = spread(tokens[0])
    source = rows_all.astype(f32)
    grad_rows = spread(cotangent[0])
    other_places = over_ctx(places)[0].reshape(2, run)
    own_places = places[0].reshape(2, run)
    place_blocks = jnp.stack([own_places, other_places], axis=1)
    place_blocks = jnp.where(core == 0, place_blocks, place_blocks[::-1]).reshape(-1)
    place_column = place_blocks[:, None]
    place_row = place_blocks[None, :]
    home_side = jnp.array([0, 1, 1, 0], jnp.int32)
    home_core = jnp.array([0, 0, 1, 1], jnp.int32)
    block_of = (home_core ^ core) * 2 + (home_side ^ side)

    normed_one, unit_one, factor_one = norm_forward(source, gain_one)
    normed_one = normed_one.astype(bf16)
    projected = dot(normed_one, qkv_weight)
    row_count = projected.shape[0]
    query_raw = projected[:, :q_width].reshape(row_count, -1, HD)
    key_raw = projected[:, q_width : q_width + k_width].reshape(row_count, -1, HD)
    value_rows = projected[:, q_width + k_width :].astype(bf16)
    cosine, sine_table = rope_tables(place_blocks)
    query_normed, query_unit, query_factor = norm_forward(query_raw, query_gain)
    queries = rotate(query_normed, cosine, sine_table).astype(bf16).reshape(row_count, -1)
    key_normed, key_unit, key_factor = norm_forward(key_raw, key_gain)
    key_rows = rotate(key_normed, cosine, sine_table).astype(bf16).reshape(row_count, -1)
    mixed, lse_rows = attend(block_of, queries, key_rows, value_rows, place_column, place_row)

    middle = source[: 2 * run] + half_sum(dot(mixed, out_weight, NT))
    normed_two, unit_two, factor_two = norm_forward(middle, gain_two)
    normed_two = normed_two.astype(bf16)
    rows_two = jnp.concatenate([normed_two, over_core(normed_two)], axis=0)
    gate_up = dot(rows_two, gate_up_weight)
    gate_act = gate_up[:, :hidden_width]
    up_act = gate_up[:, hidden_width:]
    sigmoid_gate = jax.nn.sigmoid(gate_act)
    silu_gate = gate_act * sigmoid_gate
    hidden = (silu_gate * up_act).astype(bf16)
    grad_hidden = dot(grad_rows, down_weight)
    grad_gate = (
        grad_hidden * up_act * sigmoid_gate * (1.0 + gate_act * (1.0 - sigmoid_gate))
    ).astype(bf16)
    grad_up = (grad_hidden * silu_gate).astype(bf16)
    grad_gate_up = jnp.concatenate([grad_gate, grad_up], axis=1)
    layer_out = middle[:run] + own_sum(dot(hidden, down_weight, NT))

    grad_normed_two = half_sum(dot(grad_gate_up, gate_up_weight, NT))
    mlp_grad = jnp.concatenate(
        [
            dot(rows_two, grad_gate_up, TN).astype(bf16),
            dot(grad_rows, hidden, TN).astype(bf16),
        ],
        axis=1,
    )
    grad_source_two, _ = norm_backward(grad_normed_two, unit_two, factor_two, gain_two)
    grad_gain_two = jnp.sum(grad_normed_two[:run] * unit_two[:run], axis=0)
    grad_middle = grad_rows[: 2 * run].astype(f32) + grad_source_two
    branch_half = grad_middle.astype(bf16)
    grad_branch = jnp.concatenate([branch_half, over_core(branch_half)], axis=0)
    grad_mixed = dot(grad_branch, out_weight).astype(bf16)
    grad_query_rot, grad_key_rot, grad_values = attend_back(
        block_of, queries, key_rows, value_rows, grad_mixed, lse_rows, place_column, place_row
    )
    grad_query_raw, grad_q_part = norm_backward(
        rotate_back(grad_query_rot.reshape(row_count, -1, HD), cosine, sine_table),
        query_unit,
        query_factor,
        query_gain,
    )
    grad_key_raw, grad_k_part = norm_backward(
        rotate_back(grad_key_rot.reshape(row_count, -1, HD), cosine, sine_table),
        key_unit,
        key_factor,
        key_gain,
    )
    grad_qkv = jnp.concatenate(
        [
            grad_query_raw.astype(bf16).reshape(row_count, -1),
            grad_key_raw.astype(bf16).reshape(row_count, -1),
            grad_values.astype(bf16),
        ],
        axis=1,
    )
    attn_grad = jnp.concatenate(
        [dot(normed_one, grad_qkv, TN).astype(bf16), dot(grad_branch, mixed, TN).astype(bf16)],
        axis=1,
    )
    grad_normed_one = own_sum(dot(grad_qkv, qkv_weight, NT))
    grad_source_one, grad_gain_one = norm_backward(
        grad_normed_one, unit_one[:run], factor_one[:run], gain_one
    )
    grad_tokens = grad_middle[:run] + grad_source_one

    def owned(grad):
        block = lax.psum_scatter(grad, "dp", scatter_dimension=0, tiled=True)
        size = block.shape[0] // 2
        kept = lax.dynamic_slice_in_dim(block, side * size, size, 0)
        sent = lax.dynamic_slice_in_dim(block, (1 - side) * size, size, 0)
        return kept.astype(f32), over_ctx(sent).astype(f32)

    def joined(kept, other):
        return jnp.where(
            side == 0,
            jnp.concatenate([kept, other], axis=1),
            jnp.concatenate([other, kept], axis=1),
        )

    mlp_kept, mlp_other = owned(mlp_grad)
    attn_kept, attn_other = owned(attn_grad)

    def part(pair, start, stop):
        return joined(pair[0][:, start:stop], pair[1][:, start:stop])

    attn_pair = (attn_kept, attn_other)
    mlp_pair = (mlp_kept, mlp_other)
    gain_grads = sum_small(
        jnp.concatenate([grad_gain_one, grad_gain_two, grad_q_part, grad_k_part])
    )
    return (
        layer_out[None],
        grad_tokens[None],
        gain_grads[:width],
        part(attn_pair, 0, q_width),
        part(attn_pair, q_width, q_width + k_width),
        part(attn_pair, q_width + k_width, kv_end),
        gain_grads[2 * width : 2 * width + HD],
        gain_grads[2 * width + HD :],
        part(attn_pair, kv_end, attn_kept.shape[1]).T,
        gain_grads[width : 2 * width],
        part(mlp_pair, 0, hidden_width),
        part(mlp_pair, hidden_width, 2 * hidden_width),
        part(mlp_pair, 2 * hidden_width, mlp_kept.shape[1]).T,
    )


def plan(mesh):
    sizes = dict(mesh.shape)
    if sizes["ctx"] == 2 and sizes["tensor"] == 2 and sizes["dp"] & (sizes["dp"] - 1) == 0:
        return functools.partial(group_body, sizes["dp"])
    return split_body


def solution(mesh):
    in_specs = (
        P("dp", ("ctx", "tensor"), None),
        P("dp", "ctx"),
        P("dp"),
        P("dp", "tensor"),
        P("dp", "tensor"),
        P("dp", "tensor"),
        P("dp"),
        P("dp"),
        P("tensor", "dp"),
        P("dp"),
        P("dp", "tensor"),
        P("dp", "tensor"),
        P("tensor", "dp"),
        P("dp", ("ctx", "tensor"), None),
    )
    out_specs = (
        P("dp", ("ctx", "tensor"), None),
        P("dp", ("ctx", "tensor"), None),
        P(),
        P(("dp", "ctx"), "tensor"),
        P(("dp", "ctx"), "tensor"),
        P(("dp", "ctx"), "tensor"),
        P(),
        P(),
        P("tensor", ("dp", "ctx")),
        P(),
        P(("dp", "ctx"), "tensor"),
        P(("dp", "ctx"), "tensor"),
        P("tensor", ("dp", "ctx")),
    )
    return jax.shard_map(plan(mesh), mesh=mesh, in_specs=in_specs, out_specs=out_specs, check_vma=False)
```

```python
import functools

import jax
import jax.numpy as jnp
from jax import lax
from jax.experimental import pallas as pl
from jax.experimental.pallas import tpu as pltpu
from jax.sharding import PartitionSpec as P

HD = 128


EPSILON = 1e-06
ROPE_BASE = 1000000.0
NEGATIVE = -1e30


def gather_rows(source):
    return lax.all_gather(source, "tensor", axis=1, tiled=True)


def reduce_rows(partial_sum):
    return lax.psum_scatter(partial_sum, "tensor", scatter_dimension=1, tiled=True)


def norm_forward(source, gain):
    factor = lax.rsqrt(jnp.mean(source * source, axis=-1, keepdims=True) + EPSILON)
    unit = source * factor
    return (unit * gain, unit, factor)


def norm_backward(grad_normed, unit, factor, gain):
    grad_unit = grad_normed * gain
    grad_gain = jnp.sum((grad_normed * unit).reshape(-1, unit.shape[-1]), axis=0)
    grad_source = factor * (grad_unit - unit * jnp.mean(grad_unit * unit, axis=-1, keepdims=True))
    return (grad_source, grad_gain)


def rope_tables(positions):
    freq_index = jnp.arange(HD // 2, dtype=jnp.float32)
    inverse = ROPE_BASE ** (-2.0 * freq_index / HD)
    angles = positions.astype(jnp.float32)[..., None] * inverse
    cosine = jnp.concatenate([jnp.cos(angles), jnp.cos(angles)], axis=-1)
    sine_table = jnp.concatenate([jnp.sin(angles), jnp.sin(angles)], axis=-1)
    return (cosine[..., None, :], sine_table[..., None, :])


def rotate(source, cosine, sine_table):
    half_width = source.shape[-1] // 2
    turned = jnp.concatenate([-source[..., half_width:], source[..., :half_width]], axis=-1)
    return source * cosine + turned * sine_table


def rotate_back(grad_rotated, cosine, sine_table):
    half_width = grad_rotated.shape[-1] // 2
    sined = grad_rotated * sine_table
    turned = jnp.concatenate([sined[..., half_width:], -sined[..., :half_width]], axis=-1)
    return grad_rotated * cosine + turned


def to_blocks(heads_last, kv_heads):
    seqs, row_count, width = heads_last.shape
    group_size = width // (kv_heads * HD)
    shaped = heads_last.reshape(seqs, row_count, kv_heads, group_size, HD)
    return shaped.transpose(0, 2, 3, 1, 4).reshape(seqs * kv_heads, group_size, row_count, HD)


def from_blocks(blocked, seqs):
    count, group_size, row_count, width = blocked.shape
    kv_heads = count // seqs
    shaped = blocked.reshape(seqs, kv_heads, group_size, row_count, width)
    return shaped.transpose(0, 3, 1, 2, 4).reshape(seqs, row_count, kv_heads * group_size * width)


def masked_scores(queries, key_rows, query_places, key_places):
    scores = jnp.einsum(
        "hqd,kd->hqk", queries, key_rows, preferred_element_type=jnp.float32
    ) * HD ** (-0.5)
    visible = key_places[None, None, :] <= query_places[None, :, None]
    return jnp.where(visible, scores, NEGATIVE)


def recompute(queries, key_rows, lse_rows, query_places, key_places):
    return jnp.exp(masked_scores(queries, key_rows, query_places, key_places) - lse_rows[..., None])


def forward_block(pieces):
    queries, key_rows, value_rows, query_places, key_places = pieces
    scores = masked_scores(queries, key_rows, query_places, key_places)
    row_max = jnp.max(scores, axis=-1, keepdims=True)
    raised = jnp.exp(scores - row_max)
    row_total = jnp.sum(raised, axis=-1, keepdims=True)
    attn_probs = raised / row_total
    mixed = jnp.einsum(
        "hqk,kd->hqd",
        attn_probs.astype(jnp.bfloat16),
        value_rows,
        preferred_element_type=jnp.float32,
    )
    return (mixed, (row_max + jnp.log(row_total))[..., 0])


def full_block(pieces):
    queries, grad_mixed, lse_rows, query_places, key_rows, value_rows, key_places = pieces
    attn_probs = recompute(queries, key_rows, lse_rows, query_places, key_places)
    grad_probs = jnp.einsum(
        "hqd,kd->hqk", grad_mixed, value_rows, preferred_element_type=jnp.float32
    )
    row_delta = jnp.sum(attn_probs * grad_probs, axis=-1)
    grad_scores = (attn_probs * (grad_probs - row_delta[..., None])).astype(jnp.bfloat16)
    grad_queries = jnp.einsum(
        "hqk,kd->hqd", grad_scores, key_rows, preferred_element_type=jnp.float32
    ) * HD ** (-0.5)
    grad_keys = jnp.einsum(
        "hqk,hqd->kd", grad_scores, queries, preferred_element_type=jnp.float32
    ) * HD ** (-0.5)
    grad_values = jnp.einsum(
        "hqk,hqd->kd",
        attn_probs.astype(jnp.bfloat16),
        grad_mixed,
        preferred_element_type=jnp.float32,
    )
    return (grad_queries, grad_keys, grad_values)


def split_body(
    tokens,
    places,
    attn_gain,
    w_query,
    w_key,
    w_value,
    q_gain,
    k_gain,
    w_out,
    mlp_gain,
    w_gate,
    w_up,
    w_down,
    cotangent,
):
    seqs, local_rows, width = tokens.shape
    attn_set = (
        lax.all_gather(attn_gain.astype(jnp.bfloat16), "dp", axis=0, tiled=True),
        lax.all_gather(w_query.astype(jnp.bfloat16), "dp", axis=0, tiled=True),
        lax.all_gather(w_key.astype(jnp.bfloat16), "dp", axis=0, tiled=True),
        lax.all_gather(w_value.astype(jnp.bfloat16), "dp", axis=0, tiled=True),
        lax.all_gather(q_gain.astype(jnp.bfloat16), "dp", axis=0, tiled=True),
        lax.all_gather(k_gain.astype(jnp.bfloat16), "dp", axis=0, tiled=True),
        lax.all_gather(w_out.astype(jnp.bfloat16), "dp", axis=1, tiled=True),
    )
    gain_one, query_weight, key_weight, value_weight, query_gain, key_gain, out_weight = attn_set
    mlp_set = (
        lax.all_gather(mlp_gain.astype(jnp.bfloat16), "dp", axis=0, tiled=True),
        lax.all_gather(w_gate.astype(jnp.bfloat16), "dp", axis=0, tiled=True),
        lax.all_gather(w_up.astype(jnp.bfloat16), "dp", axis=0, tiled=True),
        lax.all_gather(w_down.astype(jnp.bfloat16), "dp", axis=1, tiled=True),
    )
    gain_two, gate_weight, up_weight, down_weight = mlp_set
    gain_one = gain_one.astype(jnp.float32)
    gain_two = gain_two.astype(jnp.float32)
    query_gain = query_gain.astype(jnp.float32)
    key_gain = key_gain.astype(jnp.float32)
    source = tokens.astype(jnp.float32)
    normed_one, unit_one, factor_one = norm_forward(source, gain_one)
    rows_one = gather_rows(normed_one.astype(jnp.bfloat16))
    group_rows = rows_one.shape[1]
    flat_one = rows_one.reshape(seqs * group_rows, width)
    query_raw = jnp.dot(flat_one, query_weight, preferred_element_type=jnp.float32).reshape(
        seqs, group_rows, -1, HD
    )
    key_raw = jnp.dot(flat_one, key_weight, preferred_element_type=jnp.float32).reshape(
        seqs, group_rows, -1, HD
    )
    value_rows = (
        jnp.dot(flat_one, value_weight, preferred_element_type=jnp.float32)
        .astype(jnp.bfloat16)
        .reshape(seqs, group_rows, -1)
    )
    kv_heads = key_raw.shape[2]
    cosine, sine_table = rope_tables(places)
    query_normed, query_unit, query_factor = norm_forward(query_raw, query_gain)
    queries = (
        rotate(query_normed, cosine, sine_table).astype(jnp.bfloat16).reshape(seqs, group_rows, -1)
    )
    key_normed, key_unit, key_factor = norm_forward(key_raw, key_gain)
    key_rows = (
        rotate(key_normed, cosine, sine_table).astype(jnp.bfloat16).reshape(seqs, group_rows, -1)
    )
    key_all, value_all, places_all = (
        lax.all_gather(key_rows, "ctx", axis=1, tiled=True),
        lax.all_gather(value_rows, "ctx", axis=1, tiled=True),
        lax.all_gather(places, "ctx", axis=1, tiled=True),
    )
    query_blocks = to_blocks(queries, kv_heads)
    key_blocks = to_blocks(key_all, kv_heads)[:, 0]
    value_blocks = to_blocks(value_all, kv_heads)[:, 0]
    query_places = jnp.repeat(places, kv_heads, axis=0)
    key_places = jnp.repeat(places_all, kv_heads, axis=0)
    mixed_blocks, lse_blocks = lax.map(
        forward_block, (query_blocks, key_blocks, value_blocks, query_places, key_places)
    )
    mixed = from_blocks(mixed_blocks, seqs).astype(jnp.bfloat16).reshape(seqs * group_rows, -1)
    attn_part = jnp.dot(mixed, out_weight, preferred_element_type=jnp.float32).reshape(
        seqs, group_rows, width
    )
    middle = source + reduce_rows(attn_part)
    normed_two, unit_two, factor_two = norm_forward(middle, gain_two)
    rows_two = gather_rows(normed_two.astype(jnp.bfloat16)).reshape(seqs * group_rows, width)
    gate_act = jnp.dot(rows_two, gate_weight, preferred_element_type=jnp.float32)
    up_act = jnp.dot(rows_two, up_weight, preferred_element_type=jnp.float32)
    sigmoid_gate = jax.nn.sigmoid(gate_act)
    silu_gate = gate_act * sigmoid_gate
    hidden = (silu_gate * up_act).astype(jnp.bfloat16)
    mlp_part = jnp.dot(hidden, down_weight, preferred_element_type=jnp.float32).reshape(
        seqs, group_rows, width
    )
    layer_out = middle + reduce_rows(mlp_part)
    grad_rows = gather_rows(cotangent).reshape(seqs * group_rows, width)
    down_grad = jnp.einsum("tf,td->fd", hidden, grad_rows, preferred_element_type=jnp.float32)
    grad_hidden = jnp.einsum(
        "td,fd->tf", grad_rows, down_weight, preferred_element_type=jnp.float32
    )
    grad_gate = (
        grad_hidden * up_act * sigmoid_gate * (1.0 + gate_act * (1.0 - sigmoid_gate))
    ).astype(jnp.bfloat16)
    grad_up = (grad_hidden * silu_gate).astype(jnp.bfloat16)
    gate_grad = jnp.einsum("td,tf->df", rows_two, grad_gate, preferred_element_type=jnp.float32)
    up_grad = jnp.einsum("td,tf->df", rows_two, grad_up, preferred_element_type=jnp.float32)
    grad_normed_two = jnp.einsum(
        "tf,df->td", grad_gate, gate_weight, preferred_element_type=jnp.float32
    ) + jnp.einsum("tf,df->td", grad_up, up_weight, preferred_element_type=jnp.float32)
    grad_normed_two = reduce_rows(grad_normed_two.reshape(seqs, group_rows, width))
    grad_source_two, grad_gain_two = norm_backward(grad_normed_two, unit_two, factor_two, gain_two)
    grad_middle = cotangent.astype(jnp.float32) + grad_source_two
    grad_branch = gather_rows(grad_middle.astype(jnp.bfloat16)).reshape(seqs * group_rows, width)
    out_grad = jnp.einsum("tc,td->cd", mixed, grad_branch, preferred_element_type=jnp.float32)
    grad_mixed = (
        jnp.einsum("td,cd->tc", grad_branch, out_weight, preferred_element_type=jnp.float32)
        .astype(jnp.bfloat16)
        .reshape(seqs, group_rows, -1)
    )
    grad_blocks = to_blocks(grad_mixed, kv_heads)
    grad_query_blocks, grad_key_blocks, grad_value_blocks = lax.map(
        full_block,
        (query_blocks, grad_blocks, lse_blocks, query_places, key_blocks, value_blocks, key_places),
    )
    key_terms = jnp.concatenate(
        [
            from_blocks(grad_key_blocks[:, None], seqs),
            from_blocks(grad_value_blocks[:, None], seqs),
        ],
        axis=-1,
    )
    key_sums = lax.psum_scatter(
        key_terms.astype(jnp.bfloat16), "ctx", scatter_dimension=1, tiled=True
    ).astype(jnp.float32)
    half_width = key_sums.shape[-1] // 2
    grad_keys = key_sums[..., :half_width]
    grad_values = key_sums[..., half_width:]
    grad_query_rot = from_blocks(grad_query_blocks, seqs).reshape(seqs, group_rows, -1, HD)
    grad_query_raw, grad_q_part = norm_backward(
        rotate_back(grad_query_rot, cosine, sine_table), query_unit, query_factor, query_gain
    )
    grad_query_raw = grad_query_raw.astype(jnp.bfloat16).reshape(seqs * group_rows, -1)
    grad_key_rot = grad_keys.reshape(seqs, group_rows, kv_heads, HD)
    grad_key_raw, grad_k_part = norm_backward(
        rotate_back(grad_key_rot, cosine, sine_table), key_unit, key_factor, key_gain
    )
    grad_key_raw = grad_key_raw.astype(jnp.bfloat16).reshape(seqs * group_rows, -1)
    grad_value_raw = grad_values.astype(jnp.bfloat16).reshape(seqs * group_rows, -1)
    query_grad = jnp.einsum(
        "td,tc->dc", flat_one, grad_query_raw, preferred_element_type=jnp.float32
    )
    key_grad = jnp.einsum("td,tc->dc", flat_one, grad_key_raw, preferred_element_type=jnp.float32)
    value_grad = jnp.einsum(
        "td,tc->dc", flat_one, grad_value_raw, preferred_element_type=jnp.float32
    )
    grad_normed_one = jnp.einsum(
        "tc,dc->td", grad_query_raw, query_weight, preferred_element_type=jnp.float32
    )
    grad_normed_one = grad_normed_one + jnp.einsum(
        "tc,dc->td", grad_key_raw, key_weight, preferred_element_type=jnp.float32
    )
    grad_normed_one = grad_normed_one + jnp.einsum(
        "tc,dc->td", grad_value_raw, value_weight, preferred_element_type=jnp.float32
    )
    grad_normed_one = reduce_rows(grad_normed_one.reshape(seqs, group_rows, width))
    grad_source_one, grad_gain_one = norm_backward(grad_normed_one, unit_one, factor_one, gain_one)
    grad_tokens = grad_middle + grad_source_one
    weight_grads = (
        lax.psum_scatter(query_grad, ("dp", "ctx"), scatter_dimension=0, tiled=True),
        lax.psum_scatter(key_grad, ("dp", "ctx"), scatter_dimension=0, tiled=True),
        lax.psum_scatter(value_grad, ("dp", "ctx"), scatter_dimension=0, tiled=True),
        lax.psum_scatter(out_grad, ("dp", "ctx"), scatter_dimension=1, tiled=True),
        lax.psum_scatter(gate_grad, ("dp", "ctx"), scatter_dimension=0, tiled=True),
        lax.psum_scatter(up_grad, ("dp", "ctx"), scatter_dimension=0, tiled=True),
        lax.psum_scatter(down_grad, ("dp", "ctx"), scatter_dimension=1, tiled=True),
    )
    gain_grads = lax.psum(
        (grad_gain_one, grad_q_part, grad_k_part, grad_gain_two), ("dp", "ctx", "tensor")
    )
    return (
        layer_out,
        grad_tokens,
        gain_grads[0],
        weight_grads[0],
        weight_grads[1],
        weight_grads[2],
        gain_grads[1],
        gain_grads[2],
        weight_grads[3],
        gain_grads[3],
        weight_grads[4],
        weight_grads[5],
        weight_grads[6],
    )


NT = (((1,), (1,)), ((), ()))
TN = (((0,), (0,)), ((), ()))
NN = (((1,), (0,)), ((), ()))
SCALE = HD ** (-0.5)


def dot(left, right, dims=NN):
    return lax.dot_general(left, right, dims, preferred_element_type=jnp.float32)


def sort_runs(block_of, run, *pairs):
    for index in range(4):
        source = pl.multiple_of(block_of[index] * run, run)
        for target, origin in pairs:
            target[pl.ds(index * run, run), :] = origin[pl.ds(source, run), :]


def raw_scores(keys, query, visible, run):
    scores = dot(keys, query, NT) * SCALE
    count = scores.shape[0]
    last = jnp.where(visible, scores[count - run :], NEGATIVE)
    if count == run:
        return last
    return jnp.concatenate([scores[: count - run], last], axis=0)


def forward_kernel(
    block_of, q_ref, k_ref, v_ref, column_ref, row_ref, mixed_ref, lse_ref, keys, values, columns
):
    run = q_ref.shape[0] // 4
    sort_runs(block_of, run, (keys, k_ref), (values, v_ref), (columns, column_ref))
    for index in range(4):
        count = run * (index + 1)
        rows = pl.ds(pl.multiple_of(block_of[index] * run, run), run)
        visible = columns[pl.ds(count - run, run), :] <= row_ref[:, rows]
        for head in range(q_ref.shape[1] // HD):
            lanes = pl.ds(head * HD, HD)
            scores = raw_scores(keys[:count], q_ref[rows, lanes], visible, run)
            row_max = jnp.max(scores, axis=0, keepdims=True)
            raised = jnp.exp(scores - row_max)
            row_total = jnp.sum(raised, axis=0, keepdims=True)
            probs = (raised * (1.0 / row_total)).astype(jnp.bfloat16)
            mixed_ref[rows, lanes] = dot(probs, values[:count], TN).astype(jnp.bfloat16)
            lse_ref[pl.ds(head, 1), rows] = row_max + jnp.log(row_total)


def turn(source):
    return pltpu.roll(source, HD // 2, 1)


def unit_of(raw):
    factor = lax.rsqrt(jnp.mean(raw * raw, axis=-1, keepdims=True) + EPSILON)
    return (raw * factor, factor)


def project_kernel(
    x_ref, w_ref, cos_ref, sin_ref, q_gain_ref, k_gain_ref, q_ref, k_ref, v_ref, raw_ref
):
    product = dot(x_ref[...], w_ref[...])
    raw_width = raw_ref.shape[1]
    raw_ref[...] = product[:, :raw_width]
    v_ref[...] = product[:, raw_width:].astype(jnp.bfloat16)
    cosine = cos_ref[...]
    sine = sin_ref[...]
    q_heads = q_ref.shape[1] // HD
    for head in range(raw_width // HD):
        unit, _ = unit_of(product[:, head * HD : (head + 1) * HD])
        target = (q_ref, head) if head < q_heads else (k_ref, head - q_heads)
        gain_ref = q_gain_ref if head < q_heads else k_gain_ref
        normed = unit * gain_ref[...]
        rotated = normed * cosine + turn(normed) * sine
        target[0][:, target[1] * HD : (target[1] + 1) * HD] = rotated.astype(jnp.bfloat16)


def norm_rope_back(grad, raw, cosine, sine, gain):
    grad_normed = grad * cosine - turn(grad) * sine
    unit, factor = unit_of(raw)
    gain_part = jnp.sum(grad_normed * unit, axis=0, keepdims=True)
    grad_unit = grad_normed * gain
    projected = jnp.mean(grad_unit * unit, axis=-1, keepdims=True)
    return ((factor * (grad_unit - unit * projected)).astype(jnp.bfloat16), gain_part)


def backward_kernel(
    block_of,
    q_ref,
    k_ref,
    v_ref,
    g_ref,
    lse_ref,
    column_ref,
    row_ref,
    raw_q_ref,
    raw_k_ref,
    cos_ref,
    sin_ref,
    q_gain_ref,
    k_gain_ref,
    dq_ref,
    dk_ref,
    dv_ref,
    q_part_ref,
    k_part_ref,
    keys,
    values,
    columns,
    key_sum,
    value_sum,
):
    run = q_ref.shape[0] // 4
    sort_runs(block_of, run, (keys, k_ref), (values, v_ref), (columns, column_ref))
    key_sum[...] = jnp.zeros_like(key_sum)
    value_sum[...] = jnp.zeros_like(value_sum)
    q_part = jnp.zeros((1, HD), jnp.float32)
    k_part = jnp.zeros((1, HD), jnp.float32)
    for index in range(4):
        count = run * (index + 1)
        rows = pl.ds(pl.multiple_of(block_of[index] * run, run), run)
        visible = columns[pl.ds(count - run, run), :] <= row_ref[:, rows]
        for head in range(q_ref.shape[1] // HD):
            lanes = pl.ds(head * HD, HD)
            query = q_ref[rows, lanes]
            grad = g_ref[rows, lanes]
            scores = raw_scores(keys[:count], query, visible, run)
            probs = jnp.exp(scores - lse_ref[pl.ds(head, 1), rows])
            grad_probs = dot(values[:count], grad, NT)
            delta = jnp.sum(probs * grad_probs, axis=0, keepdims=True)
            grad_scores = (probs * (grad_probs - delta)).astype(jnp.bfloat16)
            value_sum[:count, :] += dot(probs.astype(jnp.bfloat16), grad)
            key_sum[:count, :] += dot(grad_scores, query)
            grad_query = dot(grad_scores, keys[:count], TN) * SCALE
            dq_ref[rows, lanes], part = norm_rope_back(
                grad_query,
                raw_q_ref[rows, lanes],
                cos_ref[rows, :],
                sin_ref[rows, :],
                q_gain_ref[...],
            )
            q_part += part
    for index in range(4):
        rows = pl.ds(pl.multiple_of(block_of[index] * run, run), run)
        sorted_rows = pl.ds(index * run, run)
        dk_ref[rows, :], part = norm_rope_back(
            key_sum[sorted_rows, :] * SCALE,
            raw_k_ref[rows, :],
            cos_ref[rows, :],
            sin_ref[rows, :],
            k_gain_ref[...],
        )
        k_part += part
        dv_ref[rows, :] = value_sum[sorted_rows, :].astype(jnp.bfloat16)
    q_part_ref[...] = q_part
    k_part_ref[...] = k_part


def mlp_kernel(x_ref, g_ref, gate_up_ref, down_ref, hidden_ref, grad_ref, kept_ref, sent_ref):
    bf16 = jnp.bfloat16
    width = down_ref.shape[1]
    gate_up = dot(x_ref[...], gate_up_ref[...])
    grad_hidden = dot(g_ref[...], down_ref[...])
    gate = gate_up[:, :width]
    up = gate_up[:, width:]
    sigmoid = jax.nn.sigmoid(gate)
    silu = gate * sigmoid
    hidden_ref[...] = (silu * up).astype(bf16)
    grad_gate = (grad_hidden * up * sigmoid * (1.0 + gate * (1.0 - sigmoid))).astype(bf16)
    grad_up = (grad_hidden * silu).astype(bf16)
    grad_ref[:, :width] = grad_gate
    grad_ref[:, width:] = grad_up
    grad_x = dot(grad_gate, gate_up_ref[:, :width], NT) + dot(
        grad_up, gate_up_ref[:, width:], NT
    )
    half = pl.num_programs(0) // 2

    @pl.when(pl.program_id(0) < half)
    def _():
        kept_ref[...] = grad_x

    @pl.when(pl.program_id(0) >= half)
    def _():
        sent_ref[...] = grad_x.astype(bf16)


VMEM_LIMIT = 44 * 1024 * 1024


def project(normed, weight, cosine, sine, q_gain, k_gain, q_width, k_width):
    rows, width = normed.shape
    block = rows // 4
    total = q_width + 2 * k_width

    def by_rows(columns):
        return pl.BlockSpec((block, columns), lambda i: (i, 0))

    def fixed(*shape):
        return pl.BlockSpec(shape, lambda i: (0, 0))

    return pl.pallas_call(
        project_kernel,
        grid=(4,),
        in_specs=[
            by_rows(width),
            fixed(width, total),
            by_rows(HD),
            by_rows(HD),
            fixed(1, HD),
            fixed(1, HD),
        ],
        out_specs=[by_rows(q_width), by_rows(k_width), by_rows(k_width), by_rows(q_width + k_width)],
        out_shape=[
            jax.ShapeDtypeStruct((rows, q_width), jnp.bfloat16),
            jax.ShapeDtypeStruct((rows, k_width), jnp.bfloat16),
            jax.ShapeDtypeStruct((rows, k_width), jnp.bfloat16),
            jax.ShapeDtypeStruct((rows, q_width + k_width), jnp.float32),
        ],
        compiler_params=pltpu.CompilerParams(vmem_limit_bytes=VMEM_LIMIT),
        cost_estimate=pl.CostEstimate(
            flops=2 * rows * width * total,
            bytes_accessed=2 * rows * width + 2 * width * total + 6 * rows * total,
            transcendentals=0,
        ),
    )(normed, weight, cosine, sine, q_gain, k_gain)


def feed(rows_two, grad_rows, weight):
    rows, width = rows_two.shape
    hidden_width = weight.shape[1] // 3
    block = rows // 4

    def by_rows(columns):
        return pl.BlockSpec((block, columns), lambda i: (i, 0))

    return pl.pallas_call(
        mlp_kernel,
        grid=(4,),
        in_specs=[
            by_rows(width),
            by_rows(width),
            pl.BlockSpec((width, 2 * hidden_width), lambda i: (0, 0)),
            pl.BlockSpec((width, hidden_width), lambda i: (0, 2)),
        ],
        out_specs=[
            by_rows(hidden_width),
            by_rows(2 * hidden_width),
            pl.BlockSpec((block, width), lambda i: (jnp.minimum(i, 1), 0)),
            pl.BlockSpec((block, width), lambda i: (jnp.maximum(i - 2, 0), 0)),
        ],
        out_shape=[
            jax.ShapeDtypeStruct((rows, hidden_width), jnp.bfloat16),
            jax.ShapeDtypeStruct((rows, 2 * hidden_width), jnp.bfloat16),
            jax.ShapeDtypeStruct((rows // 2, width), jnp.float32),
            jax.ShapeDtypeStruct((rows // 2, width), jnp.bfloat16),
        ],
        compiler_params=pltpu.CompilerParams(vmem_limit_bytes=VMEM_LIMIT),
        cost_estimate=pl.CostEstimate(
            flops=10 * rows * width * hidden_width,
            bytes_accessed=6 * width * hidden_width + 10 * rows * width,
            transcendentals=rows * hidden_width,
        ),
    )(rows_two, grad_rows, weight, weight)


def head_spec(rows, width):
    return pl.BlockSpec((rows, width), lambda group, order: (0, group))


def attend(block_of, queries, keys, values, place_column, place_row):
    rows, width = keys.shape
    groups = width // HD
    pair = queries.shape[1] // groups
    fixed_column = pl.BlockSpec((rows, 1), lambda group, order: (0, 0))
    fixed_row = pl.BlockSpec((1, rows), lambda group, order: (0, 0))
    lse_spec = pl.BlockSpec((None, pair // HD, rows), lambda group, order: (group, 0, 0))
    return pl.pallas_call(
        forward_kernel,
        grid_spec=pltpu.PrefetchScalarGridSpec(
            num_scalar_prefetch=1,
            grid=(groups,),
            in_specs=[
                head_spec(rows, pair),
                head_spec(rows, HD),
                head_spec(rows, HD),
                fixed_column,
                fixed_row,
            ],
            out_specs=[head_spec(rows, pair), lse_spec],
            scratch_shapes=[
                pltpu.VMEM((rows, HD), jnp.bfloat16),
                pltpu.VMEM((rows, HD), jnp.bfloat16),
                pltpu.VMEM((rows, 1), jnp.int32),
            ],
        ),
        out_shape=[
            jax.ShapeDtypeStruct(queries.shape, jnp.bfloat16),
            jax.ShapeDtypeStruct((groups, pair // HD, rows), jnp.float32),
        ],
        compiler_params=pltpu.CompilerParams(vmem_limit_bytes=40 * 1024 * 1024),
        cost_estimate=pl.CostEstimate(
            flops=3 * rows * rows * queries.shape[1],
            bytes_accessed=8 * rows * queries.shape[1],
            transcendentals=rows * rows * queries.shape[1] // HD,
        ),
    )(block_of, queries, keys, values, place_column, place_row)


def attend_back(
    block_of, queries, keys, values, grad_mixed, lse_rows, column, row, raw, cosine, sine, q_gain, k_gain
):
    rows, width = keys.shape
    groups = width // HD
    pair = queries.shape[1] // groups
    first_key = queries.shape[1] // HD

    def fixed(*shape):
        return pl.BlockSpec(shape, lambda group, order: (0, 0))

    lse_spec = pl.BlockSpec((None, pair // HD, rows), lambda group, order: (group, 0, 0))
    part_spec = pl.BlockSpec((None, 1, HD), lambda group, order: (group, 0, 0))
    return pl.pallas_call(
        backward_kernel,
        grid_spec=pltpu.PrefetchScalarGridSpec(
            num_scalar_prefetch=1,
            grid=(groups,),
            in_specs=[
                head_spec(rows, pair),
                head_spec(rows, HD),
                head_spec(rows, HD),
                head_spec(rows, pair),
                lse_spec,
                fixed(rows, 1),
                fixed(1, rows),
                head_spec(rows, pair),
                pl.BlockSpec((rows, HD), lambda group, order: (0, first_key + group)),
                fixed(rows, HD),
                fixed(rows, HD),
                fixed(1, HD),
                fixed(1, HD),
            ],
            out_specs=[
                head_spec(rows, pair),
                head_spec(rows, HD),
                head_spec(rows, HD),
                part_spec,
                part_spec,
            ],
            scratch_shapes=[
                pltpu.VMEM((rows, HD), jnp.bfloat16),
                pltpu.VMEM((rows, HD), jnp.bfloat16),
                pltpu.VMEM((rows, 1), jnp.int32),
                pltpu.VMEM((rows, HD), jnp.float32),
                pltpu.VMEM((rows, HD), jnp.float32),
            ],
        ),
        out_shape=[
            jax.ShapeDtypeStruct(queries.shape, jnp.bfloat16),
            jax.ShapeDtypeStruct(keys.shape, jnp.bfloat16),
            jax.ShapeDtypeStruct(keys.shape, jnp.bfloat16),
            jax.ShapeDtypeStruct((groups, 1, HD), jnp.float32),
            jax.ShapeDtypeStruct((groups, 1, HD), jnp.float32),
        ],
        compiler_params=pltpu.CompilerParams(vmem_limit_bytes=VMEM_LIMIT),
        cost_estimate=pl.CostEstimate(
            flops=7 * rows * rows * queries.shape[1],
            bytes_accessed=16 * rows * queries.shape[1],
            transcendentals=rows * rows * queries.shape[1] // HD,
        ),
    )(
        block_of,
        queries,
        keys,
        values,
        grad_mixed,
        lse_rows,
        column,
        row,
        raw,
        raw,
        cosine,
        sine,
        q_gain,
        k_gain,
    )


def swap(source, axis, size, bit=1):
    return lax.ppermute(source, axis, [(i, i ^ bit) for i in range(size)])


def group_body(
    dp_size,
    tokens,
    places,
    attn_gain,
    w_query,
    w_key,
    w_value,
    q_gain,
    k_gain,
    w_out,
    mlp_gain,
    w_gate,
    w_up,
    w_down,
    cotangent,
):
    bf16, f32 = jnp.bfloat16, jnp.float32
    run, width = tokens.shape[1:]
    side = lax.axis_index("ctx")
    core = lax.axis_index("tensor")
    member = lax.axis_index("dp")

    def over_core(source):
        return swap(source, "tensor", 2)

    def over_ctx(source):
        return swap(source, "ctx", 2)

    def spread(own):
        half = jnp.concatenate([own, over_ctx(own)], axis=0)
        return jnp.concatenate([half, over_core(half)], axis=0)

    def core_sum(parts):
        half = parts.shape[0] // 2
        return parts[:half] + over_core(parts[half:].astype(bf16)).astype(f32)

    def own_sum(parts):
        summed = core_sum(parts)
        return summed[:run] + over_ctx(summed[run:].astype(bf16)).astype(f32)

    def half_sum(parts):
        return ctx_sum(core_sum(parts))

    def ctx_sum(summed):
        other = over_ctx(summed.astype(bf16)).astype(f32)
        return summed + jnp.concatenate([other[run:], other[:run]], axis=0)

    def mine(source, axis):
        size = source.shape[axis] // 2
        return lax.dynamic_slice_in_dim(source, side * size, size, axis).astype(bf16)

    def gather_small(source):
        bit = 1
        while bit < dp_size:
            other = swap(source, "dp", dp_size, bit)
            first = (member // bit) % 2 == 0
            source = jnp.where(
                first,
                jnp.concatenate([source, other], axis=0),
                jnp.concatenate([other, source], axis=0),
            )
            bit *= 2
        return source

    def sum_small(source):
        source = source + over_core(source)
        source = source + over_ctx(source)
        bit = 1
        while bit < dp_size:
            source = source + swap(source, "dp", dp_size, bit)
            bit *= 2
        return source

    gain_block = attn_gain.shape[0]
    head_block = q_gain.shape[0]
    gains = gather_small(
        jnp.concatenate([attn_gain, mlp_gain, q_gain, k_gain]).astype(bf16)[None]
    ).astype(f32)
    gain_one = gains[:, :gain_block].reshape(-1)
    gain_two = gains[:, gain_block : 2 * gain_block].reshape(-1)
    query_gain = gains[:, 2 * gain_block : 2 * gain_block + head_block].reshape(1, -1)
    key_gain = gains[:, 2 * gain_block + head_block :].reshape(1, -1)

    attn_shard = jnp.concatenate(
        [mine(w_query, 1), mine(w_key, 1), mine(w_value, 1), mine(w_out, 0).T], axis=1
    )
    mlp_shard = jnp.concatenate([mine(w_gate, 1), mine(w_up, 1), mine(w_down, 0).T], axis=1)
    attn_weight = lax.all_gather(attn_shard, "dp", axis=0, tiled=True)
    mlp_weight = lax.all_gather(mlp_shard, "dp", axis=0, tiled=True)
    q_width = w_query.shape[1] // 2
    k_width = w_key.shape[1] // 2
    kv_end = q_width + 2 * k_width
    hidden_width = w_gate.shape[1] // 2
    qkv_weight = attn_weight[:, :kv_end]
    out_weight = attn_weight[:, kv_end:]
    down_weight = mlp_weight[:, 2 * hidden_width :]

    rows_all = spread(tokens[0])
    source = rows_all.astype(f32)
    grad_rows = spread(cotangent[0])
    other_places = over_ctx(places)[0].reshape(2, run)
    own_places = places[0].reshape(2, run)
    place_blocks = jnp.stack([own_places, other_places], axis=1)
    place_blocks = jnp.where(core == 0, place_blocks, place_blocks[::-1]).reshape(-1)
    place_column = place_blocks[:, None]
    place_row = place_blocks[None, :]
    home_side = jnp.array([0, 1, 1, 0], jnp.int32)
    home_core = jnp.array([0, 0, 1, 1], jnp.int32)
    block_of = (home_core ^ core) * 2 + (home_side ^ side)

    normed_one, unit_one, factor_one = norm_forward(source, gain_one)
    normed_one = normed_one.astype(bf16)
    row_count = source.shape[0]
    cosine, sine_table = (table[:, 0] for table in rope_tables(place_blocks))
    signs = jnp.where(jnp.arange(HD) < HD // 2, -1.0, 1.0).astype(f32)
    sine_table = sine_table * signs
    queries, key_rows, value_rows, raw = project(
        normed_one, attn_weight, cosine, sine_table, query_gain, key_gain, q_width, k_width
    )
    mixed, lse_rows = attend(block_of, queries, key_rows, value_rows, place_column, place_row)

    middle = source[: 2 * run] + half_sum(dot(mixed, out_weight, NT))
    normed_two, unit_two, factor_two = norm_forward(middle, gain_two)
    normed_two = normed_two.astype(bf16)
    rows_two = jnp.concatenate([normed_two, over_core(normed_two)], axis=0)
    hidden, grad_gate_up, grad_kept, grad_sent = feed(rows_two, grad_rows, mlp_weight)
    layer_out = middle[:run] + own_sum(dot(hidden, down_weight, NT))

    grad_normed_two = ctx_sum(grad_kept + over_core(grad_sent).astype(f32))
    mlp_grad = jnp.concatenate(
        [
            dot(rows_two, grad_gate_up, TN).astype(bf16),
            dot(grad_rows, hidden, TN).astype(bf16),
        ],
        axis=1,
    )
    grad_source_two, _ = norm_backward(grad_normed_two, unit_two, factor_two, gain_two)
    grad_gain_two = jnp.sum(grad_normed_two[:run] * unit_two[:run], axis=0)
    grad_middle = grad_rows[: 2 * run].astype(f32) + grad_source_two
    branch_half = grad_middle.astype(bf16)
    grad_branch = jnp.concatenate([branch_half, over_core(branch_half)], axis=0)
    grad_mixed = dot(grad_branch, out_weight).astype(bf16)
    grad_query, grad_key, grad_value, grad_q_part, grad_k_part = attend_back(
        block_of,
        queries,
        key_rows,
        value_rows,
        grad_mixed,
        lse_rows,
        place_column,
        place_row,
        raw,
        cosine,
        sine_table,
        query_gain,
        key_gain,
    )
    grad_q_part = jnp.sum(grad_q_part, axis=(0, 1))
    grad_k_part = jnp.sum(grad_k_part, axis=(0, 1))
    grad_qkv = jnp.concatenate([grad_query, grad_key, grad_value], axis=1)
    attn_grad = jnp.concatenate(
        [dot(normed_one, grad_qkv, TN).astype(bf16), dot(grad_branch, mixed, TN).astype(bf16)],
        axis=1,
    )
    grad_normed_one = own_sum(dot(grad_qkv, qkv_weight, NT))
    grad_source_one, grad_gain_one = norm_backward(
        grad_normed_one, unit_one[:run], factor_one[:run], gain_one
    )
    grad_tokens = grad_middle[:run] + grad_source_one

    def owned(grad):
        block = lax.psum_scatter(grad, "dp", scatter_dimension=0, tiled=True)
        size = block.shape[0] // 2
        kept = lax.dynamic_slice_in_dim(block, side * size, size, 0)
        sent = lax.dynamic_slice_in_dim(block, (1 - side) * size, size, 0)
        return kept.astype(f32), over_ctx(sent).astype(f32)

    def joined(kept, other):
        return jnp.where(
            side == 0,
            jnp.concatenate([kept, other], axis=1),
            jnp.concatenate([other, kept], axis=1),
        )

    mlp_kept, mlp_other = owned(mlp_grad)
    attn_kept, attn_other = owned(attn_grad)

    def part(pair, start, stop):
        return joined(pair[0][:, start:stop], pair[1][:, start:stop])

    attn_pair = (attn_kept, attn_other)
    mlp_pair = (mlp_kept, mlp_other)
    gain_grads = sum_small(
        jnp.concatenate([grad_gain_one, grad_gain_two, grad_q_part, grad_k_part])
    )
    return (
        layer_out[None],
        grad_tokens[None],
        gain_grads[:width],
        part(attn_pair, 0, q_width),
        part(attn_pair, q_width, q_width + k_width),
        part(attn_pair, q_width + k_width, kv_end),
        gain_grads[2 * width : 2 * width + HD],
        gain_grads[2 * width + HD :],
        part(attn_pair, kv_end, attn_kept.shape[1]).T,
        gain_grads[width : 2 * width],
        part(mlp_pair, 0, hidden_width),
        part(mlp_pair, hidden_width, 2 * hidden_width),
        part(mlp_pair, 2 * hidden_width, mlp_kept.shape[1]).T,
    )


def plan(mesh):
    sizes = dict(mesh.shape)
    if sizes["ctx"] == 2 and sizes["tensor"] == 2 and sizes["dp"] & (sizes["dp"] - 1) == 0:
        return functools.partial(group_body, sizes["dp"])
    return split_body


def solution(mesh):
    in_specs = (
        P("dp", ("ctx", "tensor"), None),
        P("dp", "ctx"),
        P("dp"),
        P("dp", "tensor"),
        P("dp", "tensor"),
        P("dp", "tensor"),
        P("dp"),
        P("dp"),
        P("tensor", "dp"),
        P("dp"),
        P("dp", "tensor"),
        P("dp", "tensor"),
        P("tensor", "dp"),
        P("dp", ("ctx", "tensor"), None),
    )
    out_specs = (
        P("dp", ("ctx", "tensor"), None),
        P("dp", ("ctx", "tensor"), None),
        P(),
        P(("dp", "ctx"), "tensor"),
        P(("dp", "ctx"), "tensor"),
        P(("dp", "ctx"), "tensor"),
        P(),
        P(),
        P("tensor", ("dp", "ctx")),
        P(),
        P(("dp", "ctx"), "tensor"),
        P(("dp", "ctx"), "tensor"),
        P("tensor", ("dp", "ctx")),
    )
    return jax.shard_map(plan(mesh), mesh=mesh, in_specs=in_specs, out_specs=out_specs, check_vma=False)
```

```python
import functools

import jax
import jax.numpy as jnp
from jax import lax
from jax.experimental import pallas as pl
from jax.experimental.pallas import tpu as pltpu
from jax.sharding import PartitionSpec as P

HD = 128


EPSILON = 1e-06
ROPE_BASE = 1000000.0
NEGATIVE = -1e30


def gather_rows(source):
    return lax.all_gather(source, "tensor", axis=1, tiled=True)


def reduce_rows(partial_sum):
    return lax.psum_scatter(partial_sum, "tensor", scatter_dimension=1, tiled=True)


def norm_forward(source, gain):
    factor = lax.rsqrt(jnp.mean(source * source, axis=-1, keepdims=True) + EPSILON)
    unit = source * factor
    return (unit * gain, unit, factor)


def norm_backward(grad_normed, unit, factor, gain):
    grad_unit = grad_normed * gain
    grad_gain = jnp.sum((grad_normed * unit).reshape(-1, unit.shape[-1]), axis=0)
    grad_source = factor * (grad_unit - unit * jnp.mean(grad_unit * unit, axis=-1, keepdims=True))
    return (grad_source, grad_gain)


def rope_tables(positions):
    freq_index = jnp.arange(HD // 2, dtype=jnp.float32)
    inverse = ROPE_BASE ** (-2.0 * freq_index / HD)
    angles = positions.astype(jnp.float32)[..., None] * inverse
    cosine = jnp.concatenate([jnp.cos(angles), jnp.cos(angles)], axis=-1)
    sine_table = jnp.concatenate([jnp.sin(angles), jnp.sin(angles)], axis=-1)
    return (cosine[..., None, :], sine_table[..., None, :])


def rotate(source, cosine, sine_table):
    half_width = source.shape[-1] // 2
    turned = jnp.concatenate([-source[..., half_width:], source[..., :half_width]], axis=-1)
    return source * cosine + turned * sine_table


def rotate_back(grad_rotated, cosine, sine_table):
    half_width = grad_rotated.shape[-1] // 2
    sined = grad_rotated * sine_table
    turned = jnp.concatenate([sined[..., half_width:], -sined[..., :half_width]], axis=-1)
    return grad_rotated * cosine + turned


def to_blocks(heads_last, kv_heads):
    seqs, row_count, width = heads_last.shape
    group_size = width // (kv_heads * HD)
    shaped = heads_last.reshape(seqs, row_count, kv_heads, group_size, HD)
    return shaped.transpose(0, 2, 3, 1, 4).reshape(seqs * kv_heads, group_size, row_count, HD)


def from_blocks(blocked, seqs):
    count, group_size, row_count, width = blocked.shape
    kv_heads = count // seqs
    shaped = blocked.reshape(seqs, kv_heads, group_size, row_count, width)
    return shaped.transpose(0, 3, 1, 2, 4).reshape(seqs, row_count, kv_heads * group_size * width)


def masked_scores(queries, key_rows, query_places, key_places):
    scores = jnp.einsum(
        "hqd,kd->hqk", queries, key_rows, preferred_element_type=jnp.float32
    ) * HD ** (-0.5)
    visible = key_places[None, None, :] <= query_places[None, :, None]
    return jnp.where(visible, scores, NEGATIVE)


def recompute(queries, key_rows, lse_rows, query_places, key_places):
    return jnp.exp(masked_scores(queries, key_rows, query_places, key_places) - lse_rows[..., None])


def forward_block(pieces):
    queries, key_rows, value_rows, query_places, key_places = pieces
    scores = masked_scores(queries, key_rows, query_places, key_places)
    row_max = jnp.max(scores, axis=-1, keepdims=True)
    raised = jnp.exp(scores - row_max)
    row_total = jnp.sum(raised, axis=-1, keepdims=True)
    attn_probs = raised / row_total
    mixed = jnp.einsum(
        "hqk,kd->hqd",
        attn_probs.astype(jnp.bfloat16),
        value_rows,
        preferred_element_type=jnp.float32,
    )
    return (mixed, (row_max + jnp.log(row_total))[..., 0])


def full_block(pieces):
    queries, grad_mixed, lse_rows, query_places, key_rows, value_rows, key_places = pieces
    attn_probs = recompute(queries, key_rows, lse_rows, query_places, key_places)
    grad_probs = jnp.einsum(
        "hqd,kd->hqk", grad_mixed, value_rows, preferred_element_type=jnp.float32
    )
    row_delta = jnp.sum(attn_probs * grad_probs, axis=-1)
    grad_scores = (attn_probs * (grad_probs - row_delta[..., None])).astype(jnp.bfloat16)
    grad_queries = jnp.einsum(
        "hqk,kd->hqd", grad_scores, key_rows, preferred_element_type=jnp.float32
    ) * HD ** (-0.5)
    grad_keys = jnp.einsum(
        "hqk,hqd->kd", grad_scores, queries, preferred_element_type=jnp.float32
    ) * HD ** (-0.5)
    grad_values = jnp.einsum(
        "hqk,hqd->kd",
        attn_probs.astype(jnp.bfloat16),
        grad_mixed,
        preferred_element_type=jnp.float32,
    )
    return (grad_queries, grad_keys, grad_values)


def split_body(
    tokens,
    places,
    attn_gain,
    w_query,
    w_key,
    w_value,
    q_gain,
    k_gain,
    w_out,
    mlp_gain,
    w_gate,
    w_up,
    w_down,
    cotangent,
):
    seqs, local_rows, width = tokens.shape
    attn_set = (
        lax.all_gather(attn_gain.astype(jnp.bfloat16), "dp", axis=0, tiled=True),
        lax.all_gather(w_query.astype(jnp.bfloat16), "dp", axis=0, tiled=True),
        lax.all_gather(w_key.astype(jnp.bfloat16), "dp", axis=0, tiled=True),
        lax.all_gather(w_value.astype(jnp.bfloat16), "dp", axis=0, tiled=True),
        lax.all_gather(q_gain.astype(jnp.bfloat16), "dp", axis=0, tiled=True),
        lax.all_gather(k_gain.astype(jnp.bfloat16), "dp", axis=0, tiled=True),
        lax.all_gather(w_out.astype(jnp.bfloat16), "dp", axis=1, tiled=True),
    )
    gain_one, query_weight, key_weight, value_weight, query_gain, key_gain, out_weight = attn_set
    mlp_set = (
        lax.all_gather(mlp_gain.astype(jnp.bfloat16), "dp", axis=0, tiled=True),
        lax.all_gather(w_gate.astype(jnp.bfloat16), "dp", axis=0, tiled=True),
        lax.all_gather(w_up.astype(jnp.bfloat16), "dp", axis=0, tiled=True),
        lax.all_gather(w_down.astype(jnp.bfloat16), "dp", axis=1, tiled=True),
    )
    gain_two, gate_weight, up_weight, down_weight = mlp_set
    gain_one = gain_one.astype(jnp.float32)
    gain_two = gain_two.astype(jnp.float32)
    query_gain = query_gain.astype(jnp.float32)
    key_gain = key_gain.astype(jnp.float32)
    source = tokens.astype(jnp.float32)
    normed_one, unit_one, factor_one = norm_forward(source, gain_one)
    rows_one = gather_rows(normed_one.astype(jnp.bfloat16))
    group_rows = rows_one.shape[1]
    flat_one = rows_one.reshape(seqs * group_rows, width)
    query_raw = jnp.dot(flat_one, query_weight, preferred_element_type=jnp.float32).reshape(
        seqs, group_rows, -1, HD
    )
    key_raw = jnp.dot(flat_one, key_weight, preferred_element_type=jnp.float32).reshape(
        seqs, group_rows, -1, HD
    )
    value_rows = (
        jnp.dot(flat_one, value_weight, preferred_element_type=jnp.float32)
        .astype(jnp.bfloat16)
        .reshape(seqs, group_rows, -1)
    )
    kv_heads = key_raw.shape[2]
    cosine, sine_table = rope_tables(places)
    query_normed, query_unit, query_factor = norm_forward(query_raw, query_gain)
    queries = (
        rotate(query_normed, cosine, sine_table).astype(jnp.bfloat16).reshape(seqs, group_rows, -1)
    )
    key_normed, key_unit, key_factor = norm_forward(key_raw, key_gain)
    key_rows = (
        rotate(key_normed, cosine, sine_table).astype(jnp.bfloat16).reshape(seqs, group_rows, -1)
    )
    key_all, value_all, places_all = (
        lax.all_gather(key_rows, "ctx", axis=1, tiled=True),
        lax.all_gather(value_rows, "ctx", axis=1, tiled=True),
        lax.all_gather(places, "ctx", axis=1, tiled=True),
    )
    query_blocks = to_blocks(queries, kv_heads)
    key_blocks = to_blocks(key_all, kv_heads)[:, 0]
    value_blocks = to_blocks(value_all, kv_heads)[:, 0]
    query_places = jnp.repeat(places, kv_heads, axis=0)
    key_places = jnp.repeat(places_all, kv_heads, axis=0)
    mixed_blocks, lse_blocks = lax.map(
        forward_block, (query_blocks, key_blocks, value_blocks, query_places, key_places)
    )
    mixed = from_blocks(mixed_blocks, seqs).astype(jnp.bfloat16).reshape(seqs * group_rows, -1)
    attn_part = jnp.dot(mixed, out_weight, preferred_element_type=jnp.float32).reshape(
        seqs, group_rows, width
    )
    middle = source + reduce_rows(attn_part)
    normed_two, unit_two, factor_two = norm_forward(middle, gain_two)
    rows_two = gather_rows(normed_two.astype(jnp.bfloat16)).reshape(seqs * group_rows, width)
    gate_act = jnp.dot(rows_two, gate_weight, preferred_element_type=jnp.float32)
    up_act = jnp.dot(rows_two, up_weight, preferred_element_type=jnp.float32)
    sigmoid_gate = jax.nn.sigmoid(gate_act)
    silu_gate = gate_act * sigmoid_gate
    hidden = (silu_gate * up_act).astype(jnp.bfloat16)
    mlp_part = jnp.dot(hidden, down_weight, preferred_element_type=jnp.float32).reshape(
        seqs, group_rows, width
    )
    layer_out = middle + reduce_rows(mlp_part)
    grad_rows = gather_rows(cotangent).reshape(seqs * group_rows, width)
    down_grad = jnp.einsum("tf,td->fd", hidden, grad_rows, preferred_element_type=jnp.float32)
    grad_hidden = jnp.einsum(
        "td,fd->tf", grad_rows, down_weight, preferred_element_type=jnp.float32
    )
    grad_gate = (
        grad_hidden * up_act * sigmoid_gate * (1.0 + gate_act * (1.0 - sigmoid_gate))
    ).astype(jnp.bfloat16)
    grad_up = (grad_hidden * silu_gate).astype(jnp.bfloat16)
    gate_grad = jnp.einsum("td,tf->df", rows_two, grad_gate, preferred_element_type=jnp.float32)
    up_grad = jnp.einsum("td,tf->df", rows_two, grad_up, preferred_element_type=jnp.float32)
    grad_normed_two = jnp.einsum(
        "tf,df->td", grad_gate, gate_weight, preferred_element_type=jnp.float32
    ) + jnp.einsum("tf,df->td", grad_up, up_weight, preferred_element_type=jnp.float32)
    grad_normed_two = reduce_rows(grad_normed_two.reshape(seqs, group_rows, width))
    grad_source_two, grad_gain_two = norm_backward(grad_normed_two, unit_two, factor_two, gain_two)
    grad_middle = cotangent.astype(jnp.float32) + grad_source_two
    grad_branch = gather_rows(grad_middle.astype(jnp.bfloat16)).reshape(seqs * group_rows, width)
    out_grad = jnp.einsum("tc,td->cd", mixed, grad_branch, preferred_element_type=jnp.float32)
    grad_mixed = (
        jnp.einsum("td,cd->tc", grad_branch, out_weight, preferred_element_type=jnp.float32)
        .astype(jnp.bfloat16)
        .reshape(seqs, group_rows, -1)
    )
    grad_blocks = to_blocks(grad_mixed, kv_heads)
    grad_query_blocks, grad_key_blocks, grad_value_blocks = lax.map(
        full_block,
        (query_blocks, grad_blocks, lse_blocks, query_places, key_blocks, value_blocks, key_places),
    )
    key_terms = jnp.concatenate(
        [
            from_blocks(grad_key_blocks[:, None], seqs),
            from_blocks(grad_value_blocks[:, None], seqs),
        ],
        axis=-1,
    )
    key_sums = lax.psum_scatter(
        key_terms.astype(jnp.bfloat16), "ctx", scatter_dimension=1, tiled=True
    ).astype(jnp.float32)
    half_width = key_sums.shape[-1] // 2
    grad_keys = key_sums[..., :half_width]
    grad_values = key_sums[..., half_width:]
    grad_query_rot = from_blocks(grad_query_blocks, seqs).reshape(seqs, group_rows, -1, HD)
    grad_query_raw, grad_q_part = norm_backward(
        rotate_back(grad_query_rot, cosine, sine_table), query_unit, query_factor, query_gain
    )
    grad_query_raw = grad_query_raw.astype(jnp.bfloat16).reshape(seqs * group_rows, -1)
    grad_key_rot = grad_keys.reshape(seqs, group_rows, kv_heads, HD)
    grad_key_raw, grad_k_part = norm_backward(
        rotate_back(grad_key_rot, cosine, sine_table), key_unit, key_factor, key_gain
    )
    grad_key_raw = grad_key_raw.astype(jnp.bfloat16).reshape(seqs * group_rows, -1)
    grad_value_raw = grad_values.astype(jnp.bfloat16).reshape(seqs * group_rows, -1)
    query_grad = jnp.einsum(
        "td,tc->dc", flat_one, grad_query_raw, preferred_element_type=jnp.float32
    )
    key_grad = jnp.einsum("td,tc->dc", flat_one, grad_key_raw, preferred_element_type=jnp.float32)
    value_grad = jnp.einsum(
        "td,tc->dc", flat_one, grad_value_raw, preferred_element_type=jnp.float32
    )
    grad_normed_one = jnp.einsum(
        "tc,dc->td", grad_query_raw, query_weight, preferred_element_type=jnp.float32
    )
    grad_normed_one = grad_normed_one + jnp.einsum(
        "tc,dc->td", grad_key_raw, key_weight, preferred_element_type=jnp.float32
    )
    grad_normed_one = grad_normed_one + jnp.einsum(
        "tc,dc->td", grad_value_raw, value_weight, preferred_element_type=jnp.float32
    )
    grad_normed_one = reduce_rows(grad_normed_one.reshape(seqs, group_rows, width))
    grad_source_one, grad_gain_one = norm_backward(grad_normed_one, unit_one, factor_one, gain_one)
    grad_tokens = grad_middle + grad_source_one
    weight_grads = (
        lax.psum_scatter(query_grad, ("dp", "ctx"), scatter_dimension=0, tiled=True),
        lax.psum_scatter(key_grad, ("dp", "ctx"), scatter_dimension=0, tiled=True),
        lax.psum_scatter(value_grad, ("dp", "ctx"), scatter_dimension=0, tiled=True),
        lax.psum_scatter(out_grad, ("dp", "ctx"), scatter_dimension=1, tiled=True),
        lax.psum_scatter(gate_grad, ("dp", "ctx"), scatter_dimension=0, tiled=True),
        lax.psum_scatter(up_grad, ("dp", "ctx"), scatter_dimension=0, tiled=True),
        lax.psum_scatter(down_grad, ("dp", "ctx"), scatter_dimension=1, tiled=True),
    )
    gain_grads = lax.psum(
        (grad_gain_one, grad_q_part, grad_k_part, grad_gain_two), ("dp", "ctx", "tensor")
    )
    return (
        layer_out,
        grad_tokens,
        gain_grads[0],
        weight_grads[0],
        weight_grads[1],
        weight_grads[2],
        gain_grads[1],
        gain_grads[2],
        weight_grads[3],
        gain_grads[3],
        weight_grads[4],
        weight_grads[5],
        weight_grads[6],
    )


NT = (((1,), (1,)), ((), ()))
TN = (((0,), (0,)), ((), ()))
NN = (((1,), (0,)), ((), ()))
SCALE = HD ** (-0.5)


def dot(left, right, dims=NN):
    return lax.dot_general(left, right, dims, preferred_element_type=jnp.float32)


def sort_runs(block_of, run, *pairs):
    for index in range(4):
        source = pl.multiple_of(block_of[index] * run, run)
        for target, origin in pairs:
            target[pl.ds(index * run, run), :] = origin[pl.ds(source, run), :]


def raw_scores(keys, query, visible, run):
    scores = dot(keys, query, NT) * SCALE
    count = scores.shape[0]
    last = jnp.where(visible, scores[count - run :], NEGATIVE)
    if count == run:
        return last
    return jnp.concatenate([scores[: count - run], last], axis=0)


def forward_kernel(
    block_of, q_ref, k_ref, v_ref, column_ref, row_ref, mixed_ref, lse_ref, keys, values, columns
):
    run = q_ref.shape[0] // 4
    sort_runs(block_of, run, (keys, k_ref), (values, v_ref), (columns, column_ref))
    for index in range(4):
        count = run * (index + 1)
        rows = pl.ds(pl.multiple_of(block_of[index] * run, run), run)
        visible = columns[pl.ds(count - run, run), :] <= row_ref[:, rows]
        for head in range(q_ref.shape[1] // HD):
            lanes = pl.ds(head * HD, HD)
            scores = raw_scores(keys[:count], q_ref[rows, lanes], visible, run)
            row_max = jnp.max(scores, axis=0, keepdims=True)
            raised = jnp.exp(scores - row_max)
            row_total = jnp.sum(raised, axis=0, keepdims=True)
            probs = (raised * (1.0 / row_total)).astype(jnp.bfloat16)
            mixed_ref[rows, lanes] = dot(probs, values[:count], TN).astype(jnp.bfloat16)
            lse_ref[pl.ds(head, 1), rows] = row_max + jnp.log(row_total)


def turn(source):
    return pltpu.roll(source, HD // 2, 1)


def unit_of(raw):
    factor = lax.rsqrt(jnp.mean(raw * raw, axis=-1, keepdims=True) + EPSILON)
    return (raw * factor, factor)


def place_pieces(member, target, pieces):
    for index, piece in enumerate(pieces):
        size = piece.shape[0]
        start = pl.multiple_of((member ^ index) * size, size)
        target[pl.ds(start, size), :] = piece[...]


def project_kernel(member_ref, *refs):
    (x_ref, cos_ref, sin_ref, q_gain_ref, k_gain_ref), refs = refs[:5], refs[5:]
    pieces, (q_ref, k_ref, v_ref, raw_ref, weight_ref) = refs[:-5], refs[-5:]

    @pl.when(pl.program_id(0) == 0)
    def _():
        place_pieces(member_ref[0], weight_ref, pieces)

    product = dot(x_ref[...], weight_ref[...])
    raw_width = raw_ref.shape[1]
    raw_ref[...] = product[:, :raw_width]
    v_ref[...] = product[:, raw_width:].astype(jnp.bfloat16)
    cosine = cos_ref[...]
    sine = sin_ref[...]
    q_heads = q_ref.shape[1] // HD
    for head in range(raw_width // HD):
        unit, _ = unit_of(product[:, head * HD : (head + 1) * HD])
        target = (q_ref, head) if head < q_heads else (k_ref, head - q_heads)
        gain_ref = q_gain_ref if head < q_heads else k_gain_ref
        normed = unit * gain_ref[...]
        rotated = normed * cosine + turn(normed) * sine
        target[0][:, target[1] * HD : (target[1] + 1) * HD] = rotated.astype(jnp.bfloat16)


def norm_rope_back(grad, raw, cosine, sine, gain):
    grad_normed = grad * cosine - turn(grad) * sine
    unit, factor = unit_of(raw)
    gain_part = jnp.sum(grad_normed * unit, axis=0, keepdims=True)
    grad_unit = grad_normed * gain
    projected = jnp.mean(grad_unit * unit, axis=-1, keepdims=True)
    return ((factor * (grad_unit - unit * projected)).astype(jnp.bfloat16), gain_part)


def backward_kernel(
    block_of,
    q_ref,
    k_ref,
    v_ref,
    g_ref,
    lse_ref,
    column_ref,
    row_ref,
    raw_q_ref,
    raw_k_ref,
    cos_ref,
    sin_ref,
    q_gain_ref,
    k_gain_ref,
    dq_ref,
    dk_ref,
    dv_ref,
    q_part_ref,
    k_part_ref,
    keys,
    values,
    columns,
    key_sum,
    value_sum,
):
    run = q_ref.shape[0] // 4
    sort_runs(block_of, run, (keys, k_ref), (values, v_ref), (columns, column_ref))
    key_sum[...] = jnp.zeros_like(key_sum)
    value_sum[...] = jnp.zeros_like(value_sum)
    q_part = jnp.zeros((1, HD), jnp.float32)
    k_part = jnp.zeros((1, HD), jnp.float32)
    for index in range(4):
        count = run * (index + 1)
        rows = pl.ds(pl.multiple_of(block_of[index] * run, run), run)
        visible = columns[pl.ds(count - run, run), :] <= row_ref[:, rows]
        for head in range(q_ref.shape[1] // HD):
            lanes = pl.ds(head * HD, HD)
            query = q_ref[rows, lanes]
            grad = g_ref[rows, lanes]
            scores = raw_scores(keys[:count], query, visible, run)
            probs = jnp.exp(scores - lse_ref[pl.ds(head, 1), rows])
            grad_probs = dot(values[:count], grad, NT)
            delta = jnp.sum(probs * grad_probs, axis=0, keepdims=True)
            grad_scores = (probs * (grad_probs - delta)).astype(jnp.bfloat16)
            value_sum[:count, :] += dot(probs.astype(jnp.bfloat16), grad)
            key_sum[:count, :] += dot(grad_scores, query)
            grad_query = dot(grad_scores, keys[:count], TN) * SCALE
            dq_ref[rows, lanes], part = norm_rope_back(
                grad_query,
                raw_q_ref[rows, lanes],
                cos_ref[rows, :],
                sin_ref[rows, :],
                q_gain_ref[...],
            )
            q_part += part
    for index in range(4):
        rows = pl.ds(pl.multiple_of(block_of[index] * run, run), run)
        sorted_rows = pl.ds(index * run, run)
        dk_ref[rows, :], part = norm_rope_back(
            key_sum[sorted_rows, :] * SCALE,
            raw_k_ref[rows, :],
            cos_ref[rows, :],
            sin_ref[rows, :],
            k_gain_ref[...],
        )
        k_part += part
        dv_ref[rows, :] = value_sum[sorted_rows, :].astype(jnp.bfloat16)
    q_part_ref[...] = q_part
    k_part_ref[...] = k_part


def mlp_kernel(x_ref, g_ref, gate_up_ref, down_ref, hidden_ref, grad_ref, kept_ref, sent_ref):
    bf16 = jnp.bfloat16
    width = down_ref.shape[1]
    gate_up = dot(x_ref[...], gate_up_ref[...])
    grad_hidden = dot(g_ref[...], down_ref[...])
    gate = gate_up[:, :width]
    up = gate_up[:, width:]
    sigmoid = jax.nn.sigmoid(gate)
    silu = gate * sigmoid
    hidden_ref[...] = (silu * up).astype(bf16)
    grad_gate = (grad_hidden * up * sigmoid * (1.0 + gate * (1.0 - sigmoid))).astype(bf16)
    grad_up = (grad_hidden * silu).astype(bf16)
    grad_ref[:, :width] = grad_gate
    grad_ref[:, width:] = grad_up
    grad_x = dot(grad_gate, gate_up_ref[:, :width], NT) + dot(
        grad_up, gate_up_ref[:, width:], NT
    )
    half = pl.num_programs(0) // 2

    @pl.when(pl.program_id(0) < half)
    def _():
        kept_ref[...] = grad_x

    @pl.when(pl.program_id(0) >= half)
    def _():
        sent_ref[...] = grad_x.astype(bf16)


VMEM_LIMIT = 44 * 1024 * 1024


def project(member, normed, pieces, cosine, sine, q_gain, k_gain, q_width, k_width):
    rows, width = normed.shape
    block = rows // 4
    total = q_width + 2 * k_width

    def by_rows(columns):
        return pl.BlockSpec((block, columns), lambda i, member: (i, 0))

    def fixed(*shape):
        return pl.BlockSpec(shape, lambda i, member: (0, 0))

    return pl.pallas_call(
        project_kernel,
        grid_spec=pltpu.PrefetchScalarGridSpec(
            num_scalar_prefetch=1,
            grid=(4,),
            in_specs=[
                by_rows(width),
                by_rows(HD),
                by_rows(HD),
                fixed(1, HD),
                fixed(1, HD),
            ]
            + [fixed(*piece.shape) for piece in pieces],
            out_specs=[
                by_rows(q_width),
                by_rows(k_width),
                by_rows(k_width),
                by_rows(q_width + k_width),
                fixed(width, total),
            ],
        ),
        out_shape=[
            jax.ShapeDtypeStruct((rows, q_width), jnp.bfloat16),
            jax.ShapeDtypeStruct((rows, k_width), jnp.bfloat16),
            jax.ShapeDtypeStruct((rows, k_width), jnp.bfloat16),
            jax.ShapeDtypeStruct((rows, q_width + k_width), jnp.float32),
            jax.ShapeDtypeStruct((width, total), jnp.bfloat16),
        ],
        compiler_params=pltpu.CompilerParams(vmem_limit_bytes=VMEM_LIMIT),
        cost_estimate=pl.CostEstimate(
            flops=2 * rows * width * total,
            bytes_accessed=2 * rows * width + 2 * width * total + 6 * rows * total,
            transcendentals=0,
        ),
    )(member, normed, cosine, sine, q_gain, k_gain, *pieces)


def out_kernel(member_ref, mixed_ref, *refs):
    pieces, (kept_ref, sent_ref, weight_ref) = refs[:-3], refs[-3:]

    @pl.when(pl.program_id(0) == 0)
    def _():
        place_pieces(member_ref[0], weight_ref, pieces)

    product = dot(mixed_ref[...], weight_ref[...], NT)
    half = pl.num_programs(0) // 2

    @pl.when(pl.program_id(0) < half)
    def _():
        kept_ref[...] = product

    @pl.when(pl.program_id(0) >= half)
    def _():
        sent_ref[...] = product.astype(jnp.bfloat16)


def project_out(member, mixed, pieces):
    rows, depth = mixed.shape
    block = rows // 4
    width = pieces[0].shape[0] * len(pieces)
    return pl.pallas_call(
        out_kernel,
        grid_spec=pltpu.PrefetchScalarGridSpec(
            num_scalar_prefetch=1,
            grid=(4,),
            in_specs=[pl.BlockSpec((block, depth), lambda i, member: (i, 0))]
            + [pl.BlockSpec(piece.shape, lambda i, member: (0, 0)) for piece in pieces],
            out_specs=[
                pl.BlockSpec((block, width), lambda i, member: (jnp.minimum(i, 1), 0)),
                pl.BlockSpec((block, width), lambda i, member: (jnp.maximum(i - 2, 0), 0)),
                pl.BlockSpec((width, depth), lambda i, member: (0, 0)),
            ],
        ),
        out_shape=[
            jax.ShapeDtypeStruct((rows // 2, width), jnp.float32),
            jax.ShapeDtypeStruct((rows // 2, width), jnp.bfloat16),
            jax.ShapeDtypeStruct((width, depth), jnp.bfloat16),
        ],
        compiler_params=pltpu.CompilerParams(vmem_limit_bytes=VMEM_LIMIT),
        cost_estimate=pl.CostEstimate(
            flops=2 * rows * width * depth,
            bytes_accessed=6 * rows * width + 4 * width * depth,
            transcendentals=0,
        ),
    )(member, mixed, *pieces)


def weight_grad_kernel(member_ref, left_ref, *refs):
    rights, (kept_ref, sent_ref, product) = refs[:-3], refs[-3:]
    half = kept_ref.shape[0]
    start = 0
    for right_ref in rights:
        stop = start + right_ref.shape[1]
        product[:, start:stop] = dot(left_ref[...], right_ref[...], TN).astype(jnp.bfloat16)
        start = stop
    near = member_ref[0] % 2
    kept_ref[...] = product[pl.ds(pl.multiple_of(near * half, half), half), :]
    sent_ref[...] = product[pl.ds(pl.multiple_of((1 - near) * half, half), half), :]


def weight_grad(member, dp_size, left, rights):
    rows, width = left.shape
    pairs = dp_size // 2
    half = width // dp_size
    total = sum(right.shape[1] for right in rights)
    out_spec = pl.BlockSpec((None, half, total), lambda i, member: (i, 0, 0))
    shape = jax.ShapeDtypeStruct((pairs, half, total), jnp.bfloat16)
    return pl.pallas_call(
        weight_grad_kernel,
        grid_spec=pltpu.PrefetchScalarGridSpec(
            num_scalar_prefetch=1,
            grid=(pairs,),
            in_specs=[
                pl.BlockSpec((rows, 2 * half), lambda i, member: (0, (member[0] // 2) ^ i)),
            ]
            + [pl.BlockSpec(right.shape, lambda i, member: (0, 0)) for right in rights],
            out_specs=[out_spec, out_spec],
            scratch_shapes=[pltpu.VMEM((2 * half, total), jnp.bfloat16)],
        ),
        out_shape=[shape, shape],
        compiler_params=pltpu.CompilerParams(vmem_limit_bytes=VMEM_LIMIT),
        cost_estimate=pl.CostEstimate(
            flops=2 * rows * width * total,
            bytes_accessed=2 * rows * (width + total) + 2 * width * total,
            transcendentals=0,
        ),
    )(member, left, *rights)


def feed(rows_two, grad_rows, weight):
    rows, width = rows_two.shape
    hidden_width = weight.shape[1] // 3
    block = rows // 4

    def by_rows(columns):
        return pl.BlockSpec((block, columns), lambda i: (i, 0))

    return pl.pallas_call(
        mlp_kernel,
        grid=(4,),
        in_specs=[
            by_rows(width),
            by_rows(width),
            pl.BlockSpec((width, 2 * hidden_width), lambda i: (0, 0)),
            pl.BlockSpec((width, hidden_width), lambda i: (0, 2)),
        ],
        out_specs=[
            by_rows(hidden_width),
            by_rows(2 * hidden_width),
            pl.BlockSpec((block, width), lambda i: (jnp.minimum(i, 1), 0)),
            pl.BlockSpec((block, width), lambda i: (jnp.maximum(i - 2, 0), 0)),
        ],
        out_shape=[
            jax.ShapeDtypeStruct((rows, hidden_width), jnp.bfloat16),
            jax.ShapeDtypeStruct((rows, 2 * hidden_width), jnp.bfloat16),
            jax.ShapeDtypeStruct((rows // 2, width), jnp.float32),
            jax.ShapeDtypeStruct((rows // 2, width), jnp.bfloat16),
        ],
        compiler_params=pltpu.CompilerParams(vmem_limit_bytes=VMEM_LIMIT),
        cost_estimate=pl.CostEstimate(
            flops=10 * rows * width * hidden_width,
            bytes_accessed=6 * width * hidden_width + 10 * rows * width,
            transcendentals=rows * hidden_width,
        ),
    )(rows_two, grad_rows, weight, weight)


def head_spec(rows, width):
    return pl.BlockSpec((rows, width), lambda group, order: (0, group))


def attend(block_of, queries, keys, values, place_column, place_row):
    rows, width = keys.shape
    groups = width // HD
    pair = queries.shape[1] // groups
    fixed_column = pl.BlockSpec((rows, 1), lambda group, order: (0, 0))
    fixed_row = pl.BlockSpec((1, rows), lambda group, order: (0, 0))
    lse_spec = pl.BlockSpec((None, pair // HD, rows), lambda group, order: (group, 0, 0))
    return pl.pallas_call(
        forward_kernel,
        grid_spec=pltpu.PrefetchScalarGridSpec(
            num_scalar_prefetch=1,
            grid=(groups,),
            in_specs=[
                head_spec(rows, pair),
                head_spec(rows, HD),
                head_spec(rows, HD),
                fixed_column,
                fixed_row,
            ],
            out_specs=[head_spec(rows, pair), lse_spec],
            scratch_shapes=[
                pltpu.VMEM((rows, HD), jnp.bfloat16),
                pltpu.VMEM((rows, HD), jnp.bfloat16),
                pltpu.VMEM((rows, 1), jnp.int32),
            ],
        ),
        out_shape=[
            jax.ShapeDtypeStruct(queries.shape, jnp.bfloat16),
            jax.ShapeDtypeStruct((groups, pair // HD, rows), jnp.float32),
        ],
        compiler_params=pltpu.CompilerParams(vmem_limit_bytes=40 * 1024 * 1024),
        cost_estimate=pl.CostEstimate(
            flops=3 * rows * rows * queries.shape[1],
            bytes_accessed=8 * rows * queries.shape[1],
            transcendentals=rows * rows * queries.shape[1] // HD,
        ),
    )(block_of, queries, keys, values, place_column, place_row)


def attend_back(
    block_of, queries, keys, values, grad_mixed, lse_rows, column, row, raw, cosine, sine, q_gain, k_gain
):
    rows, width = keys.shape
    groups = width // HD
    pair = queries.shape[1] // groups
    first_key = queries.shape[1] // HD

    def fixed(*shape):
        return pl.BlockSpec(shape, lambda group, order: (0, 0))

    lse_spec = pl.BlockSpec((None, pair // HD, rows), lambda group, order: (group, 0, 0))
    part_spec = pl.BlockSpec((None, 1, HD), lambda group, order: (group, 0, 0))
    return pl.pallas_call(
        backward_kernel,
        grid_spec=pltpu.PrefetchScalarGridSpec(
            num_scalar_prefetch=1,
            grid=(groups,),
            in_specs=[
                head_spec(rows, pair),
                head_spec(rows, HD),
                head_spec(rows, HD),
                head_spec(rows, pair),
                lse_spec,
                fixed(rows, 1),
                fixed(1, rows),
                head_spec(rows, pair),
                pl.BlockSpec((rows, HD), lambda group, order: (0, first_key + group)),
                fixed(rows, HD),
                fixed(rows, HD),
                fixed(1, HD),
                fixed(1, HD),
            ],
            out_specs=[
                head_spec(rows, pair),
                head_spec(rows, HD),
                head_spec(rows, HD),
                part_spec,
                part_spec,
            ],
            scratch_shapes=[
                pltpu.VMEM((rows, HD), jnp.bfloat16),
                pltpu.VMEM((rows, HD), jnp.bfloat16),
                pltpu.VMEM((rows, 1), jnp.int32),
                pltpu.VMEM((rows, HD), jnp.float32),
                pltpu.VMEM((rows, HD), jnp.float32),
            ],
        ),
        out_shape=[
            jax.ShapeDtypeStruct(queries.shape, jnp.bfloat16),
            jax.ShapeDtypeStruct(keys.shape, jnp.bfloat16),
            jax.ShapeDtypeStruct(keys.shape, jnp.bfloat16),
            jax.ShapeDtypeStruct((groups, 1, HD), jnp.float32),
            jax.ShapeDtypeStruct((groups, 1, HD), jnp.float32),
        ],
        compiler_params=pltpu.CompilerParams(vmem_limit_bytes=VMEM_LIMIT),
        cost_estimate=pl.CostEstimate(
            flops=7 * rows * rows * queries.shape[1],
            bytes_accessed=16 * rows * queries.shape[1],
            transcendentals=rows * rows * queries.shape[1] // HD,
        ),
    )(
        block_of,
        queries,
        keys,
        values,
        grad_mixed,
        lse_rows,
        column,
        row,
        raw,
        raw,
        cosine,
        sine,
        q_gain,
        k_gain,
    )


def swap(source, axis, size, bit=1):
    return lax.ppermute(source, axis, [(i, i ^ bit) for i in range(size)])


def group_body(
    dp_size,
    tokens,
    places,
    attn_gain,
    w_query,
    w_key,
    w_value,
    q_gain,
    k_gain,
    w_out,
    mlp_gain,
    w_gate,
    w_up,
    w_down,
    cotangent,
):
    bf16, f32 = jnp.bfloat16, jnp.float32
    run, width = tokens.shape[1:]
    side = lax.axis_index("ctx")
    core = lax.axis_index("tensor")
    member = lax.axis_index("dp")

    def over_core(source):
        return swap(source, "tensor", 2)

    def over_ctx(source):
        return swap(source, "ctx", 2)

    def spread(own):
        half = jnp.concatenate([own, over_ctx(own)], axis=0)
        return jnp.concatenate([half, over_core(half)], axis=0)

    def core_sum(parts):
        half = parts.shape[0] // 2
        return parts[:half] + over_core(parts[half:].astype(bf16)).astype(f32)

    def own_sum(parts):
        summed = core_sum(parts)
        return summed[:run] + over_ctx(summed[run:].astype(bf16)).astype(f32)

    def ctx_sum(summed):
        other = over_ctx(summed.astype(bf16)).astype(f32)
        return summed + jnp.concatenate([other[run:], other[:run]], axis=0)

    def mine(source, axis):
        size = source.shape[axis] // 2
        return lax.dynamic_slice_in_dim(source, side * size, size, axis).astype(bf16)

    def gather_small(source):
        bit = 1
        while bit < dp_size:
            other = swap(source, "dp", dp_size, bit)
            first = (member // bit) % 2 == 0
            source = jnp.where(
                first,
                jnp.concatenate([source, other], axis=0),
                jnp.concatenate([other, source], axis=0),
            )
            bit *= 2
        return source

    def sum_small(source):
        source = source + over_core(source)
        source = source + over_ctx(source)
        bit = 1
        while bit < dp_size:
            source = source + swap(source, "dp", dp_size, bit)
            bit *= 2
        return source

    def halves(block):
        size = block.shape[0] // 2
        kept = lax.dynamic_slice_in_dim(block, side * size, size, 0)
        sent = lax.dynamic_slice_in_dim(block, (1 - side) * size, size, 0)
        return kept.astype(f32), over_ctx(sent).astype(f32)

    def reduced(pair):
        kept, sent = pair
        summed = kept.astype(f32) + over_dp(sent, 1).astype(f32)
        block = summed[0]
        for step in depths:
            block = block + over_dp(summed[step].astype(bf16), 2 * step).astype(f32)
        return halves(block)

    gain_block = attn_gain.shape[0]
    head_block = q_gain.shape[0]
    gains = gather_small(
        jnp.concatenate([attn_gain, mlp_gain, q_gain, k_gain]).astype(bf16)[None]
    ).astype(f32)
    gain_one = gains[:, :gain_block].reshape(-1)
    gain_two = gains[:, gain_block : 2 * gain_block].reshape(-1)
    query_gain = gains[:, 2 * gain_block : 2 * gain_block + head_block].reshape(1, -1)
    key_gain = gains[:, 2 * gain_block + head_block :].reshape(1, -1)

    def over_dp(source, bit):
        return swap(source, "dp", dp_size, bit)

    depths = range(1, dp_size // 2)
    qkv_shard = jnp.concatenate([mine(w_query, 1), mine(w_key, 1), mine(w_value, 1)], axis=1)
    near_pieces = [qkv_shard] + [over_dp(qkv_shard, 2 * step) for step in depths]
    qkv_pieces = []
    for piece in near_pieces:
        qkv_pieces += [piece, over_dp(piece, 1)]
    out_shard = mine(w_out, 0).T
    near_out = jnp.concatenate([out_shard] + [over_dp(out_shard, 2 * step) for step in depths])
    far_out = over_dp(near_out, 1)
    out_pieces = []
    for step in range(dp_size // 2):
        rows = slice(step * out_shard.shape[0], (step + 1) * out_shard.shape[0])
        out_pieces += [near_out[rows], far_out[rows]]
    mlp_shard = jnp.concatenate([mine(w_gate, 1), mine(w_up, 1), mine(w_down, 0).T], axis=1)
    mlp_weight = lax.all_gather(mlp_shard, "dp", axis=0, tiled=True)
    member_word = member[None]
    q_width = w_query.shape[1] // 2
    k_width = w_key.shape[1] // 2
    hidden_width = w_gate.shape[1] // 2
    down_weight = mlp_weight[:, 2 * hidden_width :]

    rows_all = spread(tokens[0])
    source = rows_all.astype(f32)
    grad_rows = spread(cotangent[0])
    other_places = over_ctx(places)[0].reshape(2, run)
    own_places = places[0].reshape(2, run)
    place_blocks = jnp.stack([own_places, other_places], axis=1)
    place_blocks = jnp.where(core == 0, place_blocks, place_blocks[::-1]).reshape(-1)
    place_column = place_blocks[:, None]
    place_row = place_blocks[None, :]
    home_side = jnp.array([0, 1, 1, 0], jnp.int32)
    home_core = jnp.array([0, 0, 1, 1], jnp.int32)
    block_of = (home_core ^ core) * 2 + (home_side ^ side)

    normed_one, unit_one, factor_one = norm_forward(source, gain_one)
    normed_one = normed_one.astype(bf16)
    row_count = source.shape[0]
    cosine, sine_table = (table[:, 0] for table in rope_tables(place_blocks))
    signs = jnp.where(jnp.arange(HD) < HD // 2, -1.0, 1.0).astype(f32)
    sine_table = sine_table * signs
    queries, key_rows, value_rows, raw, qkv_weight = project(
        member_word,
        normed_one,
        qkv_pieces,
        cosine,
        sine_table,
        query_gain,
        key_gain,
        q_width,
        k_width,
    )
    mixed, lse_rows = attend(block_of, queries, key_rows, value_rows, place_column, place_row)

    out_kept, out_sent, out_weight = project_out(member_word, mixed, out_pieces)
    middle = source[: 2 * run] + ctx_sum(out_kept + over_core(out_sent).astype(f32))
    normed_two, unit_two, factor_two = norm_forward(middle, gain_two)
    normed_two = normed_two.astype(bf16)
    rows_two = jnp.concatenate([normed_two, over_core(normed_two)], axis=0)
    hidden, grad_gate_up, grad_kept, grad_sent = feed(rows_two, grad_rows, mlp_weight)
    layer_out = middle[:run] + own_sum(dot(hidden, down_weight, NT))

    grad_normed_two = ctx_sum(grad_kept + over_core(grad_sent).astype(f32))
    mlp_grad = jnp.concatenate(
        [
            dot(rows_two, grad_gate_up, TN).astype(bf16),
            dot(grad_rows, hidden, TN).astype(bf16),
        ],
        axis=1,
    )
    grad_source_two, _ = norm_backward(grad_normed_two, unit_two, factor_two, gain_two)
    grad_gain_two = jnp.sum(grad_normed_two[:run] * unit_two[:run], axis=0)
    grad_middle = grad_rows[: 2 * run].astype(f32) + grad_source_two
    branch_half = grad_middle.astype(bf16)
    grad_branch = jnp.concatenate([branch_half, over_core(branch_half)], axis=0)
    grad_mixed = dot(grad_branch, out_weight).astype(bf16)
    out_pair = reduced(weight_grad(member_word, dp_size, grad_branch, [mixed]))
    grad_query, grad_key, grad_value, grad_q_part, grad_k_part = attend_back(
        block_of,
        queries,
        key_rows,
        value_rows,
        grad_mixed,
        lse_rows,
        place_column,
        place_row,
        raw,
        cosine,
        sine_table,
        query_gain,
        key_gain,
    )
    grad_q_part = jnp.sum(grad_q_part, axis=(0, 1))
    grad_k_part = jnp.sum(grad_k_part, axis=(0, 1))
    grad_qkv = jnp.concatenate([grad_query, grad_key, grad_value], axis=1)
    qkv_pair = reduced(weight_grad(member_word, dp_size, normed_one, [grad_query, grad_key, grad_value]))
    grad_normed_one = own_sum(dot(grad_qkv, qkv_weight, NT))
    grad_source_one, grad_gain_one = norm_backward(
        grad_normed_one, unit_one[:run], factor_one[:run], gain_one
    )
    grad_tokens = grad_middle[:run] + grad_source_one

    def joined(kept, other):
        return jnp.where(
            side == 0,
            jnp.concatenate([kept, other], axis=1),
            jnp.concatenate([other, kept], axis=1),
        )

    mlp_pair = halves(lax.psum_scatter(mlp_grad, "dp", scatter_dimension=0, tiled=True))

    def part(pair, start, stop):
        return joined(pair[0][:, start:stop], pair[1][:, start:stop])

    gain_grads = sum_small(
        jnp.concatenate([grad_gain_one, grad_gain_two, grad_q_part, grad_k_part])
    )
    return (
        layer_out[None],
        grad_tokens[None],
        gain_grads[:width],
        part(qkv_pair, 0, q_width),
        part(qkv_pair, q_width, q_width + k_width),
        part(qkv_pair, q_width + k_width, q_width + 2 * k_width),
        gain_grads[2 * width : 2 * width + HD],
        gain_grads[2 * width + HD :],
        joined(*out_pair).T,
        gain_grads[width : 2 * width],
        part(mlp_pair, 0, hidden_width),
        part(mlp_pair, hidden_width, 2 * hidden_width),
        part(mlp_pair, 2 * hidden_width, 3 * hidden_width).T,
    )


def plan(mesh):
    sizes = dict(mesh.shape)
    if sizes["ctx"] == 2 and sizes["tensor"] == 2 and sizes["dp"] & (sizes["dp"] - 1) == 0:
        return functools.partial(group_body, sizes["dp"])
    return split_body


def solution(mesh):
    in_specs = (
        P("dp", ("ctx", "tensor"), None),
        P("dp", "ctx"),
        P("dp"),
        P("dp", "tensor"),
        P("dp", "tensor"),
        P("dp", "tensor"),
        P("dp"),
        P("dp"),
        P("tensor", "dp"),
        P("dp"),
        P("dp", "tensor"),
        P("dp", "tensor"),
        P("tensor", "dp"),
        P("dp", ("ctx", "tensor"), None),
    )
    out_specs = (
        P("dp", ("ctx", "tensor"), None),
        P("dp", ("ctx", "tensor"), None),
        P(),
        P(("dp", "ctx"), "tensor"),
        P(("dp", "ctx"), "tensor"),
        P(("dp", "ctx"), "tensor"),
        P(),
        P(),
        P("tensor", ("dp", "ctx")),
        P(),
        P(("dp", "ctx"), "tensor"),
        P(("dp", "ctx"), "tensor"),
        P("tensor", ("dp", "ctx")),
    )
    return jax.shard_map(plan(mesh), mesh=mesh, in_specs=in_specs, out_specs=out_specs, check_vma=False)
```

```python
import functools

import jax
import jax.numpy as jnp
from jax import lax
from jax.experimental import pallas as pl
from jax.experimental.pallas import tpu as pltpu
from jax.sharding import PartitionSpec as P

HD = 128


EPSILON = 1e-06
ROPE_BASE = 1000000.0
NEGATIVE = -1e30


def gather_rows(source):
    return lax.all_gather(source, "tensor", axis=1, tiled=True)


def reduce_rows(partial_sum):
    return lax.psum_scatter(partial_sum, "tensor", scatter_dimension=1, tiled=True)


def norm_forward(source, gain):
    factor = lax.rsqrt(jnp.mean(source * source, axis=-1, keepdims=True) + EPSILON)
    unit = source * factor
    return (unit * gain, unit, factor)


def norm_backward(grad_normed, unit, factor, gain):
    grad_unit = grad_normed * gain
    grad_gain = jnp.sum((grad_normed * unit).reshape(-1, unit.shape[-1]), axis=0)
    grad_source = factor * (grad_unit - unit * jnp.mean(grad_unit * unit, axis=-1, keepdims=True))
    return (grad_source, grad_gain)


def rope_tables(positions):
    freq_index = jnp.arange(HD // 2, dtype=jnp.float32)
    inverse = ROPE_BASE ** (-2.0 * freq_index / HD)
    angles = positions.astype(jnp.float32)[..., None] * inverse
    cosine = jnp.concatenate([jnp.cos(angles), jnp.cos(angles)], axis=-1)
    sine_table = jnp.concatenate([jnp.sin(angles), jnp.sin(angles)], axis=-1)
    return (cosine[..., None, :], sine_table[..., None, :])


def rotate(source, cosine, sine_table):
    half_width = source.shape[-1] // 2
    turned = jnp.concatenate([-source[..., half_width:], source[..., :half_width]], axis=-1)
    return source * cosine + turned * sine_table


def rotate_back(grad_rotated, cosine, sine_table):
    half_width = grad_rotated.shape[-1] // 2
    sined = grad_rotated * sine_table
    turned = jnp.concatenate([sined[..., half_width:], -sined[..., :half_width]], axis=-1)
    return grad_rotated * cosine + turned


def to_blocks(heads_last, kv_heads):
    seqs, row_count, width = heads_last.shape
    group_size = width // (kv_heads * HD)
    shaped = heads_last.reshape(seqs, row_count, kv_heads, group_size, HD)
    return shaped.transpose(0, 2, 3, 1, 4).reshape(seqs * kv_heads, group_size, row_count, HD)


def from_blocks(blocked, seqs):
    count, group_size, row_count, width = blocked.shape
    kv_heads = count // seqs
    shaped = blocked.reshape(seqs, kv_heads, group_size, row_count, width)
    return shaped.transpose(0, 3, 1, 2, 4).reshape(seqs, row_count, kv_heads * group_size * width)


def masked_scores(queries, key_rows, query_places, key_places):
    scores = jnp.einsum(
        "hqd,kd->hqk", queries, key_rows, preferred_element_type=jnp.float32
    ) * HD ** (-0.5)
    visible = key_places[None, None, :] <= query_places[None, :, None]
    return jnp.where(visible, scores, NEGATIVE)


def recompute(queries, key_rows, lse_rows, query_places, key_places):
    return jnp.exp(masked_scores(queries, key_rows, query_places, key_places) - lse_rows[..., None])


def forward_block(pieces):
    queries, key_rows, value_rows, query_places, key_places = pieces
    scores = masked_scores(queries, key_rows, query_places, key_places)
    row_max = jnp.max(scores, axis=-1, keepdims=True)
    raised = jnp.exp(scores - row_max)
    row_total = jnp.sum(raised, axis=-1, keepdims=True)
    attn_probs = raised / row_total
    mixed = jnp.einsum(
        "hqk,kd->hqd",
        attn_probs.astype(jnp.bfloat16),
        value_rows,
        preferred_element_type=jnp.float32,
    )
    return (mixed, (row_max + jnp.log(row_total))[..., 0])


def full_block(pieces):
    queries, grad_mixed, lse_rows, query_places, key_rows, value_rows, key_places = pieces
    attn_probs = recompute(queries, key_rows, lse_rows, query_places, key_places)
    grad_probs = jnp.einsum(
        "hqd,kd->hqk", grad_mixed, value_rows, preferred_element_type=jnp.float32
    )
    row_delta = jnp.sum(attn_probs * grad_probs, axis=-1)
    grad_scores = (attn_probs * (grad_probs - row_delta[..., None])).astype(jnp.bfloat16)
    grad_queries = jnp.einsum(
        "hqk,kd->hqd", grad_scores, key_rows, preferred_element_type=jnp.float32
    ) * HD ** (-0.5)
    grad_keys = jnp.einsum(
        "hqk,hqd->kd", grad_scores, queries, preferred_element_type=jnp.float32
    ) * HD ** (-0.5)
    grad_values = jnp.einsum(
        "hqk,hqd->kd",
        attn_probs.astype(jnp.bfloat16),
        grad_mixed,
        preferred_element_type=jnp.float32,
    )
    return (grad_queries, grad_keys, grad_values)


def split_body(
    tokens,
    places,
    attn_gain,
    w_query,
    w_key,
    w_value,
    q_gain,
    k_gain,
    w_out,
    mlp_gain,
    w_gate,
    w_up,
    w_down,
    cotangent,
):
    seqs, local_rows, width = tokens.shape
    attn_set = (
        lax.all_gather(attn_gain.astype(jnp.bfloat16), "dp", axis=0, tiled=True),
        lax.all_gather(w_query.astype(jnp.bfloat16), "dp", axis=0, tiled=True),
        lax.all_gather(w_key.astype(jnp.bfloat16), "dp", axis=0, tiled=True),
        lax.all_gather(w_value.astype(jnp.bfloat16), "dp", axis=0, tiled=True),
        lax.all_gather(q_gain.astype(jnp.bfloat16), "dp", axis=0, tiled=True),
        lax.all_gather(k_gain.astype(jnp.bfloat16), "dp", axis=0, tiled=True),
        lax.all_gather(w_out.astype(jnp.bfloat16), "dp", axis=1, tiled=True),
    )
    gain_one, query_weight, key_weight, value_weight, query_gain, key_gain, out_weight = attn_set
    mlp_set = (
        lax.all_gather(mlp_gain.astype(jnp.bfloat16), "dp", axis=0, tiled=True),
        lax.all_gather(w_gate.astype(jnp.bfloat16), "dp", axis=0, tiled=True),
        lax.all_gather(w_up.astype(jnp.bfloat16), "dp", axis=0, tiled=True),
        lax.all_gather(w_down.astype(jnp.bfloat16), "dp", axis=1, tiled=True),
    )
    gain_two, gate_weight, up_weight, down_weight = mlp_set
    gain_one = gain_one.astype(jnp.float32)
    gain_two = gain_two.astype(jnp.float32)
    query_gain = query_gain.astype(jnp.float32)
    key_gain = key_gain.astype(jnp.float32)
    source = tokens.astype(jnp.float32)
    normed_one, unit_one, factor_one = norm_forward(source, gain_one)
    rows_one = gather_rows(normed_one.astype(jnp.bfloat16))
    group_rows = rows_one.shape[1]
    flat_one = rows_one.reshape(seqs * group_rows, width)
    query_raw = jnp.dot(flat_one, query_weight, preferred_element_type=jnp.float32).reshape(
        seqs, group_rows, -1, HD
    )
    key_raw = jnp.dot(flat_one, key_weight, preferred_element_type=jnp.float32).reshape(
        seqs, group_rows, -1, HD
    )
    value_rows = (
        jnp.dot(flat_one, value_weight, preferred_element_type=jnp.float32)
        .astype(jnp.bfloat16)
        .reshape(seqs, group_rows, -1)
    )
    kv_heads = key_raw.shape[2]
    cosine, sine_table = rope_tables(places)
    query_normed, query_unit, query_factor = norm_forward(query_raw, query_gain)
    queries = (
        rotate(query_normed, cosine, sine_table).astype(jnp.bfloat16).reshape(seqs, group_rows, -1)
    )
    key_normed, key_unit, key_factor = norm_forward(key_raw, key_gain)
    key_rows = (
        rotate(key_normed, cosine, sine_table).astype(jnp.bfloat16).reshape(seqs, group_rows, -1)
    )
    key_all, value_all, places_all = (
        lax.all_gather(key_rows, "ctx", axis=1, tiled=True),
        lax.all_gather(value_rows, "ctx", axis=1, tiled=True),
        lax.all_gather(places, "ctx", axis=1, tiled=True),
    )
    query_blocks = to_blocks(queries, kv_heads)
    key_blocks = to_blocks(key_all, kv_heads)[:, 0]
    value_blocks = to_blocks(value_all, kv_heads)[:, 0]
    query_places = jnp.repeat(places, kv_heads, axis=0)
    key_places = jnp.repeat(places_all, kv_heads, axis=0)
    mixed_blocks, lse_blocks = lax.map(
        forward_block, (query_blocks, key_blocks, value_blocks, query_places, key_places)
    )
    mixed = from_blocks(mixed_blocks, seqs).astype(jnp.bfloat16).reshape(seqs * group_rows, -1)
    attn_part = jnp.dot(mixed, out_weight, preferred_element_type=jnp.float32).reshape(
        seqs, group_rows, width
    )
    middle = source + reduce_rows(attn_part)
    normed_two, unit_two, factor_two = norm_forward(middle, gain_two)
    rows_two = gather_rows(normed_two.astype(jnp.bfloat16)).reshape(seqs * group_rows, width)
    gate_act = jnp.dot(rows_two, gate_weight, preferred_element_type=jnp.float32)
    up_act = jnp.dot(rows_two, up_weight, preferred_element_type=jnp.float32)
    sigmoid_gate = jax.nn.sigmoid(gate_act)
    silu_gate = gate_act * sigmoid_gate
    hidden = (silu_gate * up_act).astype(jnp.bfloat16)
    mlp_part = jnp.dot(hidden, down_weight, preferred_element_type=jnp.float32).reshape(
        seqs, group_rows, width
    )
    layer_out = middle + reduce_rows(mlp_part)
    grad_rows = gather_rows(cotangent).reshape(seqs * group_rows, width)
    down_grad = jnp.einsum("tf,td->fd", hidden, grad_rows, preferred_element_type=jnp.float32)
    grad_hidden = jnp.einsum(
        "td,fd->tf", grad_rows, down_weight, preferred_element_type=jnp.float32
    )
    grad_gate = (
        grad_hidden * up_act * sigmoid_gate * (1.0 + gate_act * (1.0 - sigmoid_gate))
    ).astype(jnp.bfloat16)
    grad_up = (grad_hidden * silu_gate).astype(jnp.bfloat16)
    gate_grad = jnp.einsum("td,tf->df", rows_two, grad_gate, preferred_element_type=jnp.float32)
    up_grad = jnp.einsum("td,tf->df", rows_two, grad_up, preferred_element_type=jnp.float32)
    grad_normed_two = jnp.einsum(
        "tf,df->td", grad_gate, gate_weight, preferred_element_type=jnp.float32
    ) + jnp.einsum("tf,df->td", grad_up, up_weight, preferred_element_type=jnp.float32)
    grad_normed_two = reduce_rows(grad_normed_two.reshape(seqs, group_rows, width))
    grad_source_two, grad_gain_two = norm_backward(grad_normed_two, unit_two, factor_two, gain_two)
    grad_middle = cotangent.astype(jnp.float32) + grad_source_two
    grad_branch = gather_rows(grad_middle.astype(jnp.bfloat16)).reshape(seqs * group_rows, width)
    out_grad = jnp.einsum("tc,td->cd", mixed, grad_branch, preferred_element_type=jnp.float32)
    grad_mixed = (
        jnp.einsum("td,cd->tc", grad_branch, out_weight, preferred_element_type=jnp.float32)
        .astype(jnp.bfloat16)
        .reshape(seqs, group_rows, -1)
    )
    grad_blocks = to_blocks(grad_mixed, kv_heads)
    grad_query_blocks, grad_key_blocks, grad_value_blocks = lax.map(
        full_block,
        (query_blocks, grad_blocks, lse_blocks, query_places, key_blocks, value_blocks, key_places),
    )
    key_terms = jnp.concatenate(
        [
            from_blocks(grad_key_blocks[:, None], seqs),
            from_blocks(grad_value_blocks[:, None], seqs),
        ],
        axis=-1,
    )
    key_sums = lax.psum_scatter(
        key_terms.astype(jnp.bfloat16), "ctx", scatter_dimension=1, tiled=True
    ).astype(jnp.float32)
    half_width = key_sums.shape[-1] // 2
    grad_keys = key_sums[..., :half_width]
    grad_values = key_sums[..., half_width:]
    grad_query_rot = from_blocks(grad_query_blocks, seqs).reshape(seqs, group_rows, -1, HD)
    grad_query_raw, grad_q_part = norm_backward(
        rotate_back(grad_query_rot, cosine, sine_table), query_unit, query_factor, query_gain
    )
    grad_query_raw = grad_query_raw.astype(jnp.bfloat16).reshape(seqs * group_rows, -1)
    grad_key_rot = grad_keys.reshape(seqs, group_rows, kv_heads, HD)
    grad_key_raw, grad_k_part = norm_backward(
        rotate_back(grad_key_rot, cosine, sine_table), key_unit, key_factor, key_gain
    )
    grad_key_raw = grad_key_raw.astype(jnp.bfloat16).reshape(seqs * group_rows, -1)
    grad_value_raw = grad_values.astype(jnp.bfloat16).reshape(seqs * group_rows, -1)
    query_grad = jnp.einsum(
        "td,tc->dc", flat_one, grad_query_raw, preferred_element_type=jnp.float32
    )
    key_grad = jnp.einsum("td,tc->dc", flat_one, grad_key_raw, preferred_element_type=jnp.float32)
    value_grad = jnp.einsum(
        "td,tc->dc", flat_one, grad_value_raw, preferred_element_type=jnp.float32
    )
    grad_normed_one = jnp.einsum(
        "tc,dc->td", grad_query_raw, query_weight, preferred_element_type=jnp.float32
    )
    grad_normed_one = grad_normed_one + jnp.einsum(
        "tc,dc->td", grad_key_raw, key_weight, preferred_element_type=jnp.float32
    )
    grad_normed_one = grad_normed_one + jnp.einsum(
        "tc,dc->td", grad_value_raw, value_weight, preferred_element_type=jnp.float32
    )
    grad_normed_one = reduce_rows(grad_normed_one.reshape(seqs, group_rows, width))
    grad_source_one, grad_gain_one = norm_backward(grad_normed_one, unit_one, factor_one, gain_one)
    grad_tokens = grad_middle + grad_source_one
    weight_grads = (
        lax.psum_scatter(query_grad, ("dp", "ctx"), scatter_dimension=0, tiled=True),
        lax.psum_scatter(key_grad, ("dp", "ctx"), scatter_dimension=0, tiled=True),
        lax.psum_scatter(value_grad, ("dp", "ctx"), scatter_dimension=0, tiled=True),
        lax.psum_scatter(out_grad, ("dp", "ctx"), scatter_dimension=1, tiled=True),
        lax.psum_scatter(gate_grad, ("dp", "ctx"), scatter_dimension=0, tiled=True),
        lax.psum_scatter(up_grad, ("dp", "ctx"), scatter_dimension=0, tiled=True),
        lax.psum_scatter(down_grad, ("dp", "ctx"), scatter_dimension=1, tiled=True),
    )
    gain_grads = lax.psum(
        (grad_gain_one, grad_q_part, grad_k_part, grad_gain_two), ("dp", "ctx", "tensor")
    )
    return (
        layer_out,
        grad_tokens,
        gain_grads[0],
        weight_grads[0],
        weight_grads[1],
        weight_grads[2],
        gain_grads[1],
        gain_grads[2],
        weight_grads[3],
        gain_grads[3],
        weight_grads[4],
        weight_grads[5],
        weight_grads[6],
    )


NT = (((1,), (1,)), ((), ()))
TN = (((0,), (0,)), ((), ()))
NN = (((1,), (0,)), ((), ()))
SCALE = HD ** (-0.5)
GAIN_ROWS = 16
VMEM_LIMIT = 44 * 1024 * 1024
COST = 2


def dot(left, right, dims=NN):
    return lax.dot_general(left, right, dims, preferred_element_type=jnp.float32)


def shape_of(shape, dtype):
    return jax.ShapeDtypeStruct(shape, dtype)


def call(kernel, grid, words, inputs, outputs, scratch, flops):

    def spec(block, index):
        if index is None:
            return pl.BlockSpec(block, lambda *ids: (0,) * len(block))
        return pl.BlockSpec(block, index)

    return pl.pallas_call(
        kernel,
        grid_spec=pltpu.PrefetchScalarGridSpec(
            num_scalar_prefetch=1,
            grid=(grid,),
            in_specs=[spec(block, index) for _, block, index in inputs],
            out_specs=[spec(block, index) for _, _, block, index in outputs],
            scratch_shapes=scratch,
        ),
        out_shape=[shape_of(shape, dtype) for shape, dtype, _, _ in outputs],
        compiler_params=pltpu.CompilerParams(vmem_limit_bytes=VMEM_LIMIT),
        cost_estimate=pl.CostEstimate(flops=COST * flops, bytes_accessed=0, transcendentals=0),
    )(words, *[array for array, _, _ in inputs])


def whole(array):
    return (array, array.shape, None)


def sort_runs(block_of, run, *pairs):
    for index in range(4):
        source = pl.multiple_of(block_of[index] * run, run)
        for target, origin in pairs:
            target[pl.ds(index * run, run), :] = origin[pl.ds(source, run), :]


def turn(source):
    return pltpu.roll(source, HD // 2, 1)


def unit_of(raw):
    factor = lax.rsqrt(jnp.mean(raw * raw, axis=-1, keepdims=True) + EPSILON)
    return (raw * factor, factor)


def raw_scores(keys, query, visible, run):
    scores = dot(keys, query, NT) * SCALE
    count = scores.shape[0]
    last = jnp.where(visible, scores[count - run :], NEGATIVE)
    if count == run:
        return last
    return jnp.concatenate([scores[: count - run], last], axis=0)


def place_all(member, groups, refs, target, columns=slice(None), depth=None):
    for indices, ref in zip(groups, refs):
        for place, index in enumerate(indices):
            value = ref[place] if depth is None else ref[place, :depth]
            size = value.shape[0]
            start = pl.multiple_of((member ^ index) * size, size)
            target[pl.ds(start, size), columns] = value


def pick(first_ref, second_ref):
    half = pl.num_programs(0) // 2
    return jnp.where(pl.program_id(0) < half, first_ref[...], second_ref[...])


def project_kernel(groups, member_ref, xa_ref, xb_ref, cos_ref, sin_ref, *refs):
    pieces, rest = refs[:-7], refs[-7:]
    normed_ref, q_ref, k_ref, v_ref, raw_ref, weight_ref, gains_ref = rest
    depth = pieces[0].shape[1] - GAIN_ROWS

    @pl.when(pl.program_id(0) == 0)
    def _():
        place_all(member_ref[0], groups, pieces, weight_ref, depth=depth)
        gains = jnp.zeros(gains_ref.shape, jnp.float32)
        for piece in pieces:
            for place in range(piece.shape[0]):
                gains += piece[place, depth:].astype(jnp.float32)
        gains_ref[...] = gains

    unit, _ = unit_of(pick(xa_ref, xb_ref).astype(jnp.float32))
    normed = (unit * gains_ref[0:1, :]).astype(jnp.bfloat16)
    normed_ref[...] = normed
    product = dot(normed, weight_ref[...])
    raw_width = raw_ref.shape[1]
    raw_ref[...] = product[:, :raw_width]
    v_ref[...] = product[:, raw_width:].astype(jnp.bfloat16)
    cosine = cos_ref[...]
    sine = sin_ref[...]
    q_heads = q_ref.shape[1] // HD
    for head in range(raw_width // HD):
        unit, _ = unit_of(product[:, head * HD : (head + 1) * HD])
        target, place, row = (q_ref, head, 2) if head < q_heads else (k_ref, head - q_heads, 3)
        normed = unit * gains_ref[row : row + 1, :HD]
        rotated = normed * cosine + turn(normed) * sine
        target[:, place * HD : (place + 1) * HD] = rotated.astype(jnp.bfloat16)


def project(member, x_first, x_second, groups, pieces, cosine, sine, q_width, k_width):
    rows = cosine.shape[0]
    width = x_first.shape[1]
    block = rows // 4
    total = q_width + 2 * k_width
    bf16, f32 = jnp.bfloat16, jnp.float32

    def by_rows(i, member):
        return (i, 0)

    return call(
        functools.partial(project_kernel, groups),
        4,
        member,
        [
            (x_first, (block, width), first_half),
            (x_second, (block, width), second_half),
            (cosine, (block, HD), by_rows),
            (sine, (block, HD), by_rows),
        ]
        + [whole(piece) for piece in pieces],
        [
            ((rows, width), bf16, (block, width), by_rows),
            ((rows, q_width), bf16, (block, q_width), by_rows),
            ((rows, k_width), bf16, (block, k_width), by_rows),
            ((rows, k_width), bf16, (block, k_width), by_rows),
            ((rows, q_width + k_width), f32, (block, q_width + k_width), by_rows),
            ((width, total), bf16, (width, total), None),
            ((GAIN_ROWS, width), f32, (GAIN_ROWS, width), None),
        ],
        [],
        2 * rows * width * total,
    )


def forward_kernel(
    block_of, q_ref, k_ref, v_ref, column_ref, row_ref, mixed_ref, lse_ref, keys, values, columns
):
    run = q_ref.shape[0] // 4
    sort_runs(block_of, run, (keys, k_ref), (values, v_ref), (columns, column_ref))
    for index in range(4):
        count = run * (index + 1)
        rows = pl.ds(pl.multiple_of(block_of[index] * run, run), run)
        visible = columns[pl.ds(count - run, run), :] <= row_ref[:, rows]
        for head in range(q_ref.shape[1] // HD):
            lanes = pl.ds(head * HD, HD)
            scores = raw_scores(keys[:count], q_ref[rows, lanes], visible, run)
            row_max = jnp.max(scores, axis=0, keepdims=True)
            raised = jnp.exp(scores - row_max)
            row_total = jnp.sum(raised, axis=0, keepdims=True)
            probs = (raised * (1.0 / row_total)).astype(jnp.bfloat16)
            mixed_ref[rows, lanes] = dot(probs, values[:count], TN).astype(jnp.bfloat16)
            lse_ref[pl.ds(head, 1), rows] = row_max + jnp.log(row_total)


def by_group(group, order):
    return (0, group)


def by_lead(group, order):
    return (group, 0, 0)


def attend(block_of, queries, keys, values, column, row):
    rows, width = keys.shape
    groups = width // HD
    pair = queries.shape[1] // groups
    return call(
        forward_kernel,
        groups,
        block_of,
        [
            (queries, (rows, pair), by_group),
            (keys, (rows, HD), by_group),
            (values, (rows, HD), by_group),
            whole(column),
            whole(row),
        ],
        [
            (queries.shape, jnp.bfloat16, (rows, pair), by_group),
            ((groups, pair // HD, rows), jnp.float32, (None, pair // HD, rows), by_lead),
        ],
        [
            pltpu.VMEM((rows, HD), jnp.bfloat16),
            pltpu.VMEM((rows, HD), jnp.bfloat16),
            pltpu.VMEM((rows, 1), jnp.int32),
        ],
        3 * rows * rows * queries.shape[1],
    )


def first_half(i, member):
    return (jnp.minimum(i, 1), 0)


def second_half(i, member):
    return (jnp.maximum(i - 2, 0), 0)


def store_halves(product, kept_ref, sent_ref):
    half = pl.num_programs(0) // 2

    @pl.when(pl.program_id(0) < half)
    def _():
        kept_ref[...] = product

    @pl.when(pl.program_id(0) >= half)
    def _():
        sent_ref[...] = product.astype(jnp.bfloat16)


def halves_out(rows, block, width):
    return [
        ((rows // 2, width), jnp.float32, (block, width), first_half),
        ((rows // 2, width), jnp.bfloat16, (block, width), second_half),
    ]


def out_kernel(groups, member_ref, mixed_ref, *refs):
    pieces, (kept_ref, sent_ref, weight_ref) = refs[:-3], refs[-3:]

    @pl.when(pl.program_id(0) == 0)
    def _():
        place_all(member_ref[0], groups, pieces, weight_ref)

    store_halves(dot(mixed_ref[...], weight_ref[...], NT), kept_ref, sent_ref)


def project_out(member, mixed, groups, pieces):
    rows, depth = mixed.shape
    block = rows // 4
    width = pieces[0].shape[1] * sum(piece.shape[0] for piece in pieces)
    return call(
        functools.partial(out_kernel, groups),
        4,
        member,
        [(mixed, (block, depth), lambda i, member: (i, 0))] + [whole(piece) for piece in pieces],
        halves_out(rows, block, width)
        + [((width, depth), jnp.bfloat16, (width, depth), None)],
        [],
        2 * rows * width * depth,
    )


def back_kernel(starts, member_ref, xa_ref, xb_ref, *refs):
    grad_refs, (weight_ref, kept_ref, sent_ref, gain_ref) = refs[:-4], refs[-4:]
    product = None
    for start, grad_ref in zip(starts, grad_refs):
        term = dot(grad_ref[...], weight_ref[:, start : start + grad_ref.shape[1]], NT)
        product = term if product is None else product + term
    unit, _ = unit_of(pick(xa_ref, xb_ref).astype(jnp.float32))

    @pl.when(pl.program_id(0) == 0)
    def _():
        gain_ref[...] = jnp.zeros_like(gain_ref)

    gain_ref[...] += jnp.sum(product * unit, axis=0, keepdims=True)
    store_halves(product, kept_ref, sent_ref)


def project_back(member, x_first, x_second, starts, grads, weight):
    rows = grads[0].shape[0]
    block = rows // 4
    width, total = weight.shape
    return call(
        functools.partial(back_kernel, starts),
        4,
        member,
        [
            (x_first, (block, width), first_half),
            (x_second, (block, width), second_half),
        ]
        + [(grad, (block, grad.shape[1]), lambda i, member: (i, 0)) for grad in grads]
        + [whole(weight)],
        halves_out(rows, block, width) + [((1, width), jnp.float32, (1, width), None)],
        [],
        2 * rows * width * total,
    )


def mlp_kernel(member_ref, xa_ref, xb_ref, ga_ref, gb_ref, gate_up, down_ref, *rest):
    bf16 = jnp.bfloat16
    hidden_ref, grad_ref, kept_ref, sent_ref = rest
    width = down_ref.shape[1]
    x = pick(xa_ref, xb_ref)
    product = dot(x, gate_up[...])
    grad_hidden = dot(pick(ga_ref, gb_ref), down_ref[...])
    gate = product[:, :width]
    up = product[:, width:]
    sigmoid = jax.nn.sigmoid(gate)
    silu = gate * sigmoid
    hidden_ref[...] = (silu * up).astype(bf16)
    grad_gate = (grad_hidden * up * sigmoid * (1.0 + gate * (1.0 - sigmoid))).astype(bf16)
    grad_up = (grad_hidden * silu).astype(bf16)
    grad_ref[:, :width] = grad_gate
    grad_ref[:, width:] = grad_up
    grad_x = dot(grad_gate, gate_up[:, :width], NT) + dot(grad_up, gate_up[:, width:], NT)
    store_halves(grad_x, kept_ref, sent_ref)


def third_quarter(i, member):
    return (2 + jnp.minimum(i, 1), 0)


def fourth_quarter(i, member):
    return (jnp.maximum(i, 2), 0)


def feed(member, x_first, x_second, own_half, core_half, weight):
    rows, width = own_half.shape
    hidden_width = weight.shape[1] // 3
    block = rows // 4
    bf16 = jnp.bfloat16

    def by_rows(i, member):
        return (i, 0)

    return call(
        mlp_kernel,
        4,
        member,
        [
            (x_first, (block, width), first_half),
            (x_second, (block, width), second_half),
            (own_half, (block, width), third_quarter),
            (core_half, (block, width), fourth_quarter),
            (weight, (width, 2 * hidden_width), lambda i, member: (0, 0)),
            (weight, (width, hidden_width), lambda i, member: (0, 2)),
        ],
        [
            ((rows, hidden_width), bf16, (block, hidden_width), by_rows),
            ((rows, 2 * hidden_width), bf16, (block, 2 * hidden_width), by_rows),
        ]
        + halves_out(rows, block, width),
        [],
        10 * rows * width * hidden_width,
    )


def mlp_grad_kernel(member_ref, xa_ref, xb_ref, ga_ref, gb_ref, grad_ref, hidden_ref, out_ref):
    half = xa_ref.shape[0]
    split = grad_ref.shape[1]
    product = dot(xa_ref[...], grad_ref[:half, :], TN) + dot(xb_ref[...], grad_ref[half:, :], TN)
    out_ref[:, :split] = product.astype(jnp.bfloat16)
    product = dot(ga_ref[...], hidden_ref[:half, :], TN) + dot(gb_ref[...], hidden_ref[half:, :], TN)
    out_ref[:, split:] = product.astype(jnp.bfloat16)


def mlp_grads(member, x_first, x_second, own_half, core_half, grad_gate_up, hidden):
    rows, width = own_half.shape
    block = width // 4
    total = grad_gate_up.shape[1] + hidden.shape[1]

    def by_columns(i, member):
        return (0, i)

    def low_columns(i, member):
        return (1, i)

    return call(
        mlp_grad_kernel,
        4,
        member,
        [
            (x_first, (rows // 2, block), by_columns),
            (x_second, (rows // 2, block), by_columns),
            (own_half, (rows // 2, block), low_columns),
            (core_half, (rows // 2, block), low_columns),
            whole(grad_gate_up),
            whole(hidden),
        ],
        [((width, total), jnp.bfloat16, (block, total), lambda i, member: (i, 0))],
        [],
        2 * rows * width * total,
    )[0]


def weight_grad_kernel(lefts, member_ref, *refs):
    left_refs, right_refs, rest = refs[:lefts], refs[lefts:-3], refs[-3:]
    kept_ref, sent_ref, product = rest
    half = kept_ref.shape[0]
    start = 0
    for right_ref in right_refs:
        stop = start + right_ref.shape[1]
        total = None
        row = 0
        for left_ref in left_refs:
            count = left_ref.shape[0]
            term = dot(left_ref[...], right_ref[row : row + count, :], TN)
            total = term if total is None else total + term
            row += count
        product[:, start:stop] = total.astype(jnp.bfloat16)
        start = stop
    near = member_ref[0] % 2
    kept_ref[...] = product[pl.ds(pl.multiple_of(near * half, half), half), :]
    sent_ref[...] = product[pl.ds(pl.multiple_of((1 - near) * half, half), half), :]


def weight_grad(member, dp_size, lefts, rights, quarter=0):
    width = lefts[0].shape[1]
    rows = rights[0].shape[0]
    each = rows // len(lefts)
    pairs = dp_size // 2
    half = width // dp_size
    total = sum(right.shape[1] for right in rights)

    def by_lead(i, member):
        return (i, 0, 0)

    bits = pairs.bit_length() - 1

    def by_member(i, member):
        turned = sum(((i >> bit) & 1) << (bits - 1 - bit) for bit in range(bits))
        return (quarter, (member[0] // 2) ^ turned)

    result = ((pairs, half, total), jnp.bfloat16, (None, half, total), by_lead)
    return call(
        functools.partial(weight_grad_kernel, len(lefts)),
        pairs,
        member,
        [(left, (each, 2 * half), by_member) for left in lefts]
        + [whole(right) for right in rights],
        [result, result],
        [pltpu.VMEM((2 * half, total), jnp.bfloat16)],
        2 * rows * width * total,
    )


def norm_rope_back(grad, raw, cosine, sine, gain):
    grad_normed = grad * cosine - turn(grad) * sine
    unit, factor = unit_of(raw)
    gain_part = jnp.sum(grad_normed * unit, axis=0, keepdims=True)
    grad_unit = grad_normed * gain
    projected = jnp.mean(grad_unit * unit, axis=-1, keepdims=True)
    return ((factor * (grad_unit - unit * projected)).astype(jnp.bfloat16), gain_part)


def backward_kernel(
    block_of,
    q_ref,
    k_ref,
    v_ref,
    branch_a_ref,
    branch_b_ref,
    out_weight_ref,
    lse_ref,
    column_ref,
    row_ref,
    raw_q_ref,
    raw_k_ref,
    cos_ref,
    sin_ref,
    gains_ref,
    dq_ref,
    dk_ref,
    dv_ref,
    q_part_ref,
    k_part_ref,
    keys,
    values,
    columns,
    key_sum,
    value_sum,
    grad_mixed,
):
    run = q_ref.shape[0] // 4
    sort_runs(block_of, run, (keys, k_ref), (values, v_ref), (columns, column_ref))
    key_sum[...] = jnp.zeros_like(key_sum)
    value_sum[...] = jnp.zeros_like(value_sum)
    half = branch_a_ref.shape[0]
    grad_mixed[:half, :] = dot(branch_a_ref[...], out_weight_ref[...]).astype(jnp.bfloat16)
    grad_mixed[half:, :] = dot(branch_b_ref[...], out_weight_ref[...]).astype(jnp.bfloat16)
    q_part = jnp.zeros((1, HD), jnp.float32)
    k_part = jnp.zeros((1, HD), jnp.float32)
    q_gain = gains_ref[2:3, :HD]
    k_gain = gains_ref[3:4, :HD]
    for index in range(4):
        count = run * (index + 1)
        rows = pl.ds(pl.multiple_of(block_of[index] * run, run), run)
        visible = columns[pl.ds(count - run, run), :] <= row_ref[:, rows]
        for head in range(q_ref.shape[1] // HD):
            lanes = pl.ds(head * HD, HD)
            query = q_ref[rows, lanes]
            grad = grad_mixed[rows, lanes]
            scores = raw_scores(keys[:count], query, visible, run)
            probs = jnp.exp(scores - lse_ref[pl.ds(head, 1), rows])
            grad_probs = dot(values[:count], grad, NT)
            delta = jnp.sum(probs * grad_probs, axis=0, keepdims=True)
            grad_scores = (probs * (grad_probs - delta)).astype(jnp.bfloat16)
            value_sum[:count, :] += dot(probs.astype(jnp.bfloat16), grad)
            key_sum[:count, :] += dot(grad_scores, query)
            grad_query = dot(grad_scores, keys[:count], TN) * SCALE
            dq_ref[rows, lanes], part = norm_rope_back(
                grad_query, raw_q_ref[rows, lanes], cos_ref[rows, :], sin_ref[rows, :], q_gain
            )
            q_part += part
    for index in range(4):
        rows = pl.ds(pl.multiple_of(block_of[index] * run, run), run)
        sorted_rows = pl.ds(index * run, run)
        dk_ref[rows, :], part = norm_rope_back(
            key_sum[sorted_rows, :] * SCALE,
            raw_k_ref[rows, :],
            cos_ref[rows, :],
            sin_ref[rows, :],
            k_gain,
        )
        k_part += part
        dv_ref[rows, :] = value_sum[sorted_rows, :].astype(jnp.bfloat16)
    q_part_ref[...] = q_part
    k_part_ref[...] = k_part


def attend_back(
    group, block_of, queries, keys, values, branches, out_weight, lse, column, row, raw, cosine, sine, gains
):
    rows, width = keys.shape
    groups = width // HD
    pair = queries.shape[1] // groups
    first_key = queries.shape[1] // HD
    depth = out_weight.shape[0]
    bf16, f32 = jnp.bfloat16, jnp.float32
    part = ((1, HD), f32, (1, HD), None)

    def this_group(i, order):
        return (0, group)

    return call(
        backward_kernel,
        1,
        block_of,
        [
            (queries, (rows, pair), this_group),
            (keys, (rows, HD), this_group),
            (values, (rows, HD), this_group),
            whole(branches[0]),
            whole(branches[1]),
            (out_weight, (depth, pair), this_group),
            (lse, (None, pair // HD, rows), lambda i, order: (group, 0, 0)),
            whole(column),
            whole(row),
            (raw, (rows, pair), this_group),
            (raw, (rows, HD), lambda i, order: (0, first_key + group)),
            whole(cosine),
            whole(sine),
            whole(gains),
        ],
        [
            ((rows, pair), bf16, (rows, pair), None),
            ((rows, HD), bf16, (rows, HD), None),
            ((rows, HD), bf16, (rows, HD), None),
            part,
            part,
        ],
        [
            pltpu.VMEM((rows, HD), bf16),
            pltpu.VMEM((rows, HD), bf16),
            pltpu.VMEM((rows, 1), jnp.int32),
            pltpu.VMEM((rows, HD), f32),
            pltpu.VMEM((rows, HD), f32),
            pltpu.VMEM((rows, pair), bf16),
        ],
        3 * rows * rows * queries.shape[1],
    )


def swap(source, axis, size, bit=1):
    return lax.ppermute(source, axis, [(i, i ^ bit) for i in range(size)])


def after(source, *events):
    return lax.optimization_barrier((source, events))[0]


def group_body(
    dp_size,
    tokens,
    places,
    attn_gain,
    w_query,
    w_key,
    w_value,
    q_gain,
    k_gain,
    w_out,
    mlp_gain,
    w_gate,
    w_up,
    w_down,
    cotangent,
):
    bf16, f32 = jnp.bfloat16, jnp.float32
    run, width = tokens.shape[1:]
    side = lax.axis_index("ctx")
    core = lax.axis_index("tensor")
    member = lax.axis_index("dp")
    word = member[None]
    q_width = w_query.shape[1] // 2
    k_width = w_key.shape[1] // 2
    hidden_width = w_gate.shape[1] // 2
    z_bits = [1 << bit for bit in range(1, dp_size.bit_length() - 1)]
    near_steps = list(range(2, dp_size, 2))
    groups = [[0], near_steps, [1], [step ^ 1 for step in near_steps]]

    def over_core(source):
        return swap(source, "tensor", 2)

    def over_ctx(source):
        return swap(source, "ctx", 2)

    def over_dp(source, bit):
        return swap(source, "dp", dp_size, bit)

    def over_z(shard):
        return [over_dp(shard, step) for step in near_steps]

    def mine(source, axis):
        size = source.shape[axis] // 2
        return lax.dynamic_slice_in_dim(source, side * size, size, axis).astype(bf16)

    def sum_small(source):
        source = source + over_core(source)
        source = source + over_ctx(source)
        bit = 1
        while bit < dp_size:
            source = source + over_dp(source, bit)
            bit *= 2
        return source

    gain_rows = jnp.zeros((GAIN_ROWS, width), bf16)
    for row, gain in enumerate((attn_gain, mlp_gain, q_gain, k_gain)):
        gain_rows = lax.dynamic_update_slice(
            gain_rows, gain.astype(bf16)[None], (row, member * gain.shape[0])
        )
    qkv_shard = jnp.concatenate([mine(w_query, 1), mine(w_key, 1), mine(w_value, 1)], axis=1)
    qkv_shard = jnp.concatenate([qkv_shard, gain_rows], axis=0)
    depth = qkv_shard.shape[0] - GAIN_ROWS
    out_shard = mine(w_out, 0).T
    mlp_shard = jnp.concatenate([mine(w_gate, 1), mine(w_up, 1), mine(w_down, 0).T], axis=1)

    place_count = places.shape[1]
    digits = jnp.zeros((GAIN_ROWS, width), bf16)
    for row, digit in enumerate((places // 128, places % 128)):
        digits = lax.dynamic_update_slice(digits, digit.astype(bf16), (row, 0))
    message = jnp.concatenate([tokens[0], cotangent[0], digits], axis=0)
    qkv_near, qkv_far, message = lax.optimization_barrier(
        (over_z(qkv_shard), over_dp(qkv_shard, 1), over_ctx(message))
    )
    qkv_near = jnp.stack(qkv_near)
    qkv_far_rest = over_dp(qkv_near, 1)
    mlp_weight = lax.all_gather(after(mlp_shard, qkv_near), "dp", axis=0, tiled=True)
    out_near = over_z(after(out_shard, qkv_near))
    own_half = jnp.concatenate(
        [tokens[0], message[:run], cotangent[0], message[run : 2 * run]], axis=0
    )
    core_half = over_core(own_half)
    half = 2 * run
    digits = message[2 * run : 2 * run + 2, :place_count].astype(jnp.int32)
    other_places = (digits[0] * 128 + digits[1]).reshape(2, run)
    own_places = places[0].reshape(2, run)
    place_blocks = jnp.stack([own_places, other_places], axis=1)
    place_blocks = jnp.where(core == 0, place_blocks, place_blocks[::-1]).reshape(-1)
    place_column = place_blocks[:, None]
    place_row = place_blocks[None, :]
    home_side = jnp.array([0, 1, 1, 0], jnp.int32)
    home_core = jnp.array([0, 0, 1, 1], jnp.int32)
    block_of = (home_core ^ core) * 2 + (home_side ^ side)
    cosine, sine_table = (table[:, 0] for table in rope_tables(place_blocks))
    sine_table = sine_table * jnp.where(jnp.arange(HD) < HD // 2, -1.0, 1.0).astype(f32)
    own_half, core_half, cosine, sine_table, place_column, block_of = lax.optimization_barrier(
        (own_half, core_half, cosine, sine_table, place_column, block_of)
    )
    normed_one, queries, key_rows, value_rows, raw, qkv_weight, gains = project(
        word,
        own_half,
        core_half,
        groups,
        [qkv_shard[None], qkv_near, qkv_far[None], qkv_far_rest],
        cosine,
        sine_table,
        q_width,
        k_width,
    )

    out_near = jnp.stack([out_shard] + out_near)
    out_far = over_dp(out_near, 1)
    mixed, lse_rows = attend(block_of, queries, key_rows, value_rows, place_column, place_row)
    orders = [[0] + near_steps, [1] + [step ^ 1 for step in near_steps]]
    out_kept, out_sent, out_weight = project_out(word, mixed, orders, [out_near, out_far])

    def ctx_sum(summed):
        sent = summed.astype(bf16)
        other = over_ctx(sent)
        return sent, summed, other[run:], other[:run]

    source = own_half[:half].astype(f32)
    _, summed, first, second = ctx_sum(out_kept + over_core(out_sent).astype(f32))
    middle = source + summed + jnp.concatenate([first, second], axis=0).astype(f32)
    gain_two = gains[1]
    normed_two, unit_two, factor_two = norm_forward(middle, gain_two)
    normed_two = normed_two.astype(bf16)
    normed_other = over_core(normed_two)
    hidden, grad_gate_up, grad_kept, grad_sent = feed(
        word, normed_two, normed_other, own_half, core_half, mlp_weight
    )

    def summed_x(pair, *events):
        kept, sent = pair
        return kept.astype(f32) + over_dp(after(sent, *events), 1).astype(f32)

    def summed_z(summed, bit):
        count = summed.shape[0] // 2
        return summed[:count] + over_dp(summed[count:].astype(bf16), bit).astype(f32)

    def halves(block):
        size = block.shape[0] // 2
        kept = lax.dynamic_slice_in_dim(block, side * size, size, 0)
        sent = lax.dynamic_slice_in_dim(block, (1 - side) * size, size, 0)
        return kept, sent

    def joined(kept, other):
        return jnp.where(
            side == 0,
            jnp.concatenate([kept, other], axis=1),
            jnp.concatenate([other, kept], axis=1),
        )

    def grad_of(lefts, rights, quarter=0):
        return weight_grad(word, dp_size, lefts, rights, quarter)

    sent, summed, first, second = ctx_sum(grad_kept + over_core(grad_sent).astype(f32))
    hidden, grad_gate_up = lax.optimization_barrier((hidden, grad_gate_up, sent))[:2]
    mlp_grad = mlp_grads(
        word, normed_two, normed_other, own_half, core_half, grad_gate_up, hidden
    )
    mlp_block = lax.psum_scatter(mlp_grad, "dp", scatter_dimension=0, tiled=True)
    mlp_part = dot(after(hidden, mlp_grad), mlp_weight[:, 2 * hidden_width :], NT)
    mlp_part = mlp_part[:half] + over_core(mlp_part[half:].astype(bf16)).astype(f32)
    first, second = after((first, second), mlp_part)
    grad_normed_two = summed + jnp.concatenate([first, second], axis=0).astype(f32)
    grad_source_two, _ = norm_backward(grad_normed_two, unit_two, factor_two, gain_two)
    grad_gain_two = jnp.sum(grad_normed_two[:run] * unit_two[:run], axis=0)
    grad_middle = own_half[half:].astype(f32) + grad_source_two
    branch = grad_middle.astype(bf16)
    other_part = over_ctx(after(mlp_part[run:].astype(bf16), branch)).astype(f32)
    layer_out = middle[:run] + mlp_part[:run] + other_part
    branches = [branch, over_core(branch)]
    out_pair = grad_of(branches, [mixed])

    def back(group, *events):
        return attend_back(
            group,
            block_of,
            after(queries, *events),
            key_rows,
            value_rows,
            branches,
            out_weight,
            lse_rows,
            place_column,
            place_row,
            raw,
            cosine,
            sine_table,
            gains,
        )

    first_back = back(0, out_pair)
    out_sum = summed_x(out_pair)
    first_pair = grad_of([normed_one], first_back[:3])
    second_back = back(1, first_pair, out_sum, other_part)
    first_sum = summed_x(first_pair)
    second_pair = grad_of([normed_one], second_back[:3])
    second_sum = summed_x(second_pair)
    q_half, k_half = q_width // 2, k_width // 2
    starts = [0, q_half, q_width, q_width + k_half, q_width + k_width, q_width + k_width + k_half]
    back_grads = [grads[part] for part in range(3) for grads in (first_back, second_back)]
    early_sum = jnp.concatenate([out_sum, first_sum], axis=2)
    back_grads[0] = after(back_grads[0], second_pair, early_sum)
    one_kept, one_sent, grad_gain_one = project_back(
        word, own_half, core_half, starts, back_grads, qkv_weight
    )
    one_sum = one_kept + over_core(one_sent).astype(f32)
    one_other = over_ctx(one_sum[run:].astype(bf16)).astype(f32)
    grad_normed_one = one_sum[:run] + one_other
    _, unit_one, factor_one = norm_forward(tokens[0].astype(f32), gains[0])
    grad_source_one, _ = norm_backward(grad_normed_one, unit_one, factor_one, gains[0])
    grad_tokens = grad_middle[:run] + grad_source_one
    gain_grads = sum_small(
        jnp.concatenate(
            [
                grad_gain_one[0],
                grad_gain_two,
                (first_back[3] + second_back[3])[0],
                (first_back[4] + second_back[4])[0],
            ]
        )
    )

    def finished(blocks):
        kept, sent = halves(jnp.concatenate(blocks, axis=1))
        return kept, over_ctx(sent)

    early_sum = summed_z(early_sum, z_bits[0])
    late_sum = summed_z(second_sum, z_bits[0])
    attn_sum = summed_z(jnp.concatenate([early_sum, late_sum], axis=2), z_bits[1])
    attn_pair = finished([after(attn_sum[0], grad_tokens, gain_grads)])
    mlp_pair = finished([mlp_block])

    def part(pair, *columns):
        kept, other = (
            jnp.concatenate([block[:, start : start + size] for start, size in columns], axis=1)
            for block in pair
        )
        return joined(kept.astype(f32), other.astype(f32))

    start = q_width
    other_start = start + q_half + 2 * k_half
    return (
        layer_out[None],
        grad_tokens[None],
        gain_grads[:width],
        part(attn_pair, (start, q_half), (other_start, q_half)),
        part(attn_pair, (start + q_half, k_half), (other_start + q_half, k_half)),
        part(attn_pair, (start + q_half + k_half, k_half), (other_start + q_half + k_half, k_half)),
        gain_grads[2 * width : 2 * width + HD],
        gain_grads[2 * width + HD :],
        part(attn_pair, (0, q_width)).T,
        gain_grads[width : 2 * width],
        part(mlp_pair, (0, hidden_width)),
        part(mlp_pair, (hidden_width, hidden_width)),
        part(mlp_pair, (2 * hidden_width, hidden_width)).T,
    )


def plan(mesh):
    sizes = dict(mesh.shape)
    if sizes["ctx"] == 2 and sizes["tensor"] == 2 and sizes["dp"] == 8:
        return functools.partial(group_body, sizes["dp"])
    return split_body


def solution(mesh):
    in_specs = (
        P("dp", ("ctx", "tensor"), None),
        P("dp", "ctx"),
        P("dp"),
        P("dp", "tensor"),
        P("dp", "tensor"),
        P("dp", "tensor"),
        P("dp"),
        P("dp"),
        P("tensor", "dp"),
        P("dp"),
        P("dp", "tensor"),
        P("dp", "tensor"),
        P("tensor", "dp"),
        P("dp", ("ctx", "tensor"), None),
    )
    out_specs = (
        P("dp", ("ctx", "tensor"), None),
        P("dp", ("ctx", "tensor"), None),
        P(),
        P(("dp", "ctx"), "tensor"),
        P(("dp", "ctx"), "tensor"),
        P(("dp", "ctx"), "tensor"),
        P(),
        P(),
        P("tensor", ("dp", "ctx")),
        P(),
        P(("dp", "ctx"), "tensor"),
        P(("dp", "ctx"), "tensor"),
        P("tensor", ("dp", "ctx")),
    )
    return jax.shard_map(plan(mesh), mesh=mesh, in_specs=in_specs, out_specs=out_specs, check_vma=False)
```

```python
import functools

import jax
import jax.numpy as jnp
from jax import lax
from jax.experimental import pallas as pl
from jax.experimental.pallas import tpu as pltpu
from jax.sharding import PartitionSpec as P

HD = 128


EPSILON = 1e-06
ROPE_BASE = 1000000.0
NEGATIVE = -1e30


def gather_rows(source):
    return lax.all_gather(source, "tensor", axis=1, tiled=True)


def reduce_rows(partial_sum):
    return lax.psum_scatter(partial_sum, "tensor", scatter_dimension=1, tiled=True)


def norm_forward(source, gain):
    factor = lax.rsqrt(jnp.mean(source * source, axis=-1, keepdims=True) + EPSILON)
    unit = source * factor
    return (unit * gain, unit, factor)


def norm_backward(grad_normed, unit, factor, gain):
    grad_unit = grad_normed * gain
    grad_gain = jnp.sum((grad_normed * unit).reshape(-1, unit.shape[-1]), axis=0)
    grad_source = factor * (grad_unit - unit * jnp.mean(grad_unit * unit, axis=-1, keepdims=True))
    return (grad_source, grad_gain)


def rope_tables(positions):
    freq_index = jnp.arange(HD // 2, dtype=jnp.float32)
    inverse = ROPE_BASE ** (-2.0 * freq_index / HD)
    angles = positions.astype(jnp.float32)[..., None] * inverse
    cosine = jnp.concatenate([jnp.cos(angles), jnp.cos(angles)], axis=-1)
    sine_table = jnp.concatenate([jnp.sin(angles), jnp.sin(angles)], axis=-1)
    return (cosine[..., None, :], sine_table[..., None, :])


def rotate(source, cosine, sine_table):
    half_width = source.shape[-1] // 2
    turned = jnp.concatenate([-source[..., half_width:], source[..., :half_width]], axis=-1)
    return source * cosine + turned * sine_table


def rotate_back(grad_rotated, cosine, sine_table):
    half_width = grad_rotated.shape[-1] // 2
    sined = grad_rotated * sine_table
    turned = jnp.concatenate([sined[..., half_width:], -sined[..., :half_width]], axis=-1)
    return grad_rotated * cosine + turned


def to_blocks(heads_last, kv_heads):
    seqs, row_count, width = heads_last.shape
    group_size = width // (kv_heads * HD)
    shaped = heads_last.reshape(seqs, row_count, kv_heads, group_size, HD)
    return shaped.transpose(0, 2, 3, 1, 4).reshape(seqs * kv_heads, group_size, row_count, HD)


def from_blocks(blocked, seqs):
    count, group_size, row_count, width = blocked.shape
    kv_heads = count // seqs
    shaped = blocked.reshape(seqs, kv_heads, group_size, row_count, width)
    return shaped.transpose(0, 3, 1, 2, 4).reshape(seqs, row_count, kv_heads * group_size * width)


def masked_scores(queries, key_rows, query_places, key_places):
    scores = jnp.einsum(
        "hqd,kd->hqk", queries, key_rows, preferred_element_type=jnp.float32
    ) * HD ** (-0.5)
    visible = key_places[None, None, :] <= query_places[None, :, None]
    return jnp.where(visible, scores, NEGATIVE)


def recompute(queries, key_rows, lse_rows, query_places, key_places):
    return jnp.exp(masked_scores(queries, key_rows, query_places, key_places) - lse_rows[..., None])


def forward_block(pieces):
    queries, key_rows, value_rows, query_places, key_places = pieces
    scores = masked_scores(queries, key_rows, query_places, key_places)
    row_max = jnp.max(scores, axis=-1, keepdims=True)
    raised = jnp.exp(scores - row_max)
    row_total = jnp.sum(raised, axis=-1, keepdims=True)
    attn_probs = raised / row_total
    mixed = jnp.einsum(
        "hqk,kd->hqd",
        attn_probs.astype(jnp.bfloat16),
        value_rows,
        preferred_element_type=jnp.float32,
    )
    return (mixed, (row_max + jnp.log(row_total))[..., 0])


def full_block(pieces):
    queries, grad_mixed, lse_rows, query_places, key_rows, value_rows, key_places = pieces
    attn_probs = recompute(queries, key_rows, lse_rows, query_places, key_places)
    grad_probs = jnp.einsum(
        "hqd,kd->hqk", grad_mixed, value_rows, preferred_element_type=jnp.float32
    )
    row_delta = jnp.sum(attn_probs * grad_probs, axis=-1)
    grad_scores = (attn_probs * (grad_probs - row_delta[..., None])).astype(jnp.bfloat16)
    grad_queries = jnp.einsum(
        "hqk,kd->hqd", grad_scores, key_rows, preferred_element_type=jnp.float32
    ) * HD ** (-0.5)
    grad_keys = jnp.einsum(
        "hqk,hqd->kd", grad_scores, queries, preferred_element_type=jnp.float32
    ) * HD ** (-0.5)
    grad_values = jnp.einsum(
        "hqk,hqd->kd",
        attn_probs.astype(jnp.bfloat16),
        grad_mixed,
        preferred_element_type=jnp.float32,
    )
    return (grad_queries, grad_keys, grad_values)


def split_body(
    tokens,
    places,
    attn_gain,
    w_query,
    w_key,
    w_value,
    q_gain,
    k_gain,
    w_out,
    mlp_gain,
    w_gate,
    w_up,
    w_down,
    cotangent,
):
    seqs, local_rows, width = tokens.shape
    attn_set = (
        lax.all_gather(attn_gain.astype(jnp.bfloat16), "dp", axis=0, tiled=True),
        lax.all_gather(w_query.astype(jnp.bfloat16), "dp", axis=0, tiled=True),
        lax.all_gather(w_key.astype(jnp.bfloat16), "dp", axis=0, tiled=True),
        lax.all_gather(w_value.astype(jnp.bfloat16), "dp", axis=0, tiled=True),
        lax.all_gather(q_gain.astype(jnp.bfloat16), "dp", axis=0, tiled=True),
        lax.all_gather(k_gain.astype(jnp.bfloat16), "dp", axis=0, tiled=True),
        lax.all_gather(w_out.astype(jnp.bfloat16), "dp", axis=1, tiled=True),
    )
    gain_one, query_weight, key_weight, value_weight, query_gain, key_gain, out_weight = attn_set
    mlp_set = (
        lax.all_gather(mlp_gain.astype(jnp.bfloat16), "dp", axis=0, tiled=True),
        lax.all_gather(w_gate.astype(jnp.bfloat16), "dp", axis=0, tiled=True),
        lax.all_gather(w_up.astype(jnp.bfloat16), "dp", axis=0, tiled=True),
        lax.all_gather(w_down.astype(jnp.bfloat16), "dp", axis=1, tiled=True),
    )
    gain_two, gate_weight, up_weight, down_weight = mlp_set
    gain_one = gain_one.astype(jnp.float32)
    gain_two = gain_two.astype(jnp.float32)
    query_gain = query_gain.astype(jnp.float32)
    key_gain = key_gain.astype(jnp.float32)
    source = tokens.astype(jnp.float32)
    normed_one, unit_one, factor_one = norm_forward(source, gain_one)
    rows_one = gather_rows(normed_one.astype(jnp.bfloat16))
    group_rows = rows_one.shape[1]
    flat_one = rows_one.reshape(seqs * group_rows, width)
    query_raw = jnp.dot(flat_one, query_weight, preferred_element_type=jnp.float32).reshape(
        seqs, group_rows, -1, HD
    )
    key_raw = jnp.dot(flat_one, key_weight, preferred_element_type=jnp.float32).reshape(
        seqs, group_rows, -1, HD
    )
    value_rows = (
        jnp.dot(flat_one, value_weight, preferred_element_type=jnp.float32)
        .astype(jnp.bfloat16)
        .reshape(seqs, group_rows, -1)
    )
    kv_heads = key_raw.shape[2]
    cosine, sine_table = rope_tables(places)
    query_normed, query_unit, query_factor = norm_forward(query_raw, query_gain)
    queries = (
        rotate(query_normed, cosine, sine_table).astype(jnp.bfloat16).reshape(seqs, group_rows, -1)
    )
    key_normed, key_unit, key_factor = norm_forward(key_raw, key_gain)
    key_rows = (
        rotate(key_normed, cosine, sine_table).astype(jnp.bfloat16).reshape(seqs, group_rows, -1)
    )
    key_all, value_all, places_all = (
        lax.all_gather(key_rows, "ctx", axis=1, tiled=True),
        lax.all_gather(value_rows, "ctx", axis=1, tiled=True),
        lax.all_gather(places, "ctx", axis=1, tiled=True),
    )
    query_blocks = to_blocks(queries, kv_heads)
    key_blocks = to_blocks(key_all, kv_heads)[:, 0]
    value_blocks = to_blocks(value_all, kv_heads)[:, 0]
    query_places = jnp.repeat(places, kv_heads, axis=0)
    key_places = jnp.repeat(places_all, kv_heads, axis=0)
    mixed_blocks, lse_blocks = lax.map(
        forward_block, (query_blocks, key_blocks, value_blocks, query_places, key_places)
    )
    mixed = from_blocks(mixed_blocks, seqs).astype(jnp.bfloat16).reshape(seqs * group_rows, -1)
    attn_part = jnp.dot(mixed, out_weight, preferred_element_type=jnp.float32).reshape(
        seqs, group_rows, width
    )
    middle = source + reduce_rows(attn_part)
    normed_two, unit_two, factor_two = norm_forward(middle, gain_two)
    rows_two = gather_rows(normed_two.astype(jnp.bfloat16)).reshape(seqs * group_rows, width)
    gate_act = jnp.dot(rows_two, gate_weight, preferred_element_type=jnp.float32)
    up_act = jnp.dot(rows_two, up_weight, preferred_element_type=jnp.float32)
    sigmoid_gate = jax.nn.sigmoid(gate_act)
    silu_gate = gate_act * sigmoid_gate
    hidden = (silu_gate * up_act).astype(jnp.bfloat16)
    mlp_part = jnp.dot(hidden, down_weight, preferred_element_type=jnp.float32).reshape(
        seqs, group_rows, width
    )
    layer_out = middle + reduce_rows(mlp_part)
    grad_rows = gather_rows(cotangent).reshape(seqs * group_rows, width)
    down_grad = jnp.einsum("tf,td->fd", hidden, grad_rows, preferred_element_type=jnp.float32)
    grad_hidden = jnp.einsum(
        "td,fd->tf", grad_rows, down_weight, preferred_element_type=jnp.float32
    )
    grad_gate = (
        grad_hidden * up_act * sigmoid_gate * (1.0 + gate_act * (1.0 - sigmoid_gate))
    ).astype(jnp.bfloat16)
    grad_up = (grad_hidden * silu_gate).astype(jnp.bfloat16)
    gate_grad = jnp.einsum("td,tf->df", rows_two, grad_gate, preferred_element_type=jnp.float32)
    up_grad = jnp.einsum("td,tf->df", rows_two, grad_up, preferred_element_type=jnp.float32)
    grad_normed_two = jnp.einsum(
        "tf,df->td", grad_gate, gate_weight, preferred_element_type=jnp.float32
    ) + jnp.einsum("tf,df->td", grad_up, up_weight, preferred_element_type=jnp.float32)
    grad_normed_two = reduce_rows(grad_normed_two.reshape(seqs, group_rows, width))
    grad_source_two, grad_gain_two = norm_backward(grad_normed_two, unit_two, factor_two, gain_two)
    grad_middle = cotangent.astype(jnp.float32) + grad_source_two
    grad_branch = gather_rows(grad_middle.astype(jnp.bfloat16)).reshape(seqs * group_rows, width)
    out_grad = jnp.einsum("tc,td->cd", mixed, grad_branch, preferred_element_type=jnp.float32)
    grad_mixed = (
        jnp.einsum("td,cd->tc", grad_branch, out_weight, preferred_element_type=jnp.float32)
        .astype(jnp.bfloat16)
        .reshape(seqs, group_rows, -1)
    )
    grad_blocks = to_blocks(grad_mixed, kv_heads)
    grad_query_blocks, grad_key_blocks, grad_value_blocks = lax.map(
        full_block,
        (query_blocks, grad_blocks, lse_blocks, query_places, key_blocks, value_blocks, key_places),
    )
    key_terms = jnp.concatenate(
        [
            from_blocks(grad_key_blocks[:, None], seqs),
            from_blocks(grad_value_blocks[:, None], seqs),
        ],
        axis=-1,
    )
    key_sums = lax.psum_scatter(
        key_terms.astype(jnp.bfloat16), "ctx", scatter_dimension=1, tiled=True
    ).astype(jnp.float32)
    half_width = key_sums.shape[-1] // 2
    grad_keys = key_sums[..., :half_width]
    grad_values = key_sums[..., half_width:]
    grad_query_rot = from_blocks(grad_query_blocks, seqs).reshape(seqs, group_rows, -1, HD)
    grad_query_raw, grad_q_part = norm_backward(
        rotate_back(grad_query_rot, cosine, sine_table), query_unit, query_factor, query_gain
    )
    grad_query_raw = grad_query_raw.astype(jnp.bfloat16).reshape(seqs * group_rows, -1)
    grad_key_rot = grad_keys.reshape(seqs, group_rows, kv_heads, HD)
    grad_key_raw, grad_k_part = norm_backward(
        rotate_back(grad_key_rot, cosine, sine_table), key_unit, key_factor, key_gain
    )
    grad_key_raw = grad_key_raw.astype(jnp.bfloat16).reshape(seqs * group_rows, -1)
    grad_value_raw = grad_values.astype(jnp.bfloat16).reshape(seqs * group_rows, -1)
    query_grad = jnp.einsum(
        "td,tc->dc", flat_one, grad_query_raw, preferred_element_type=jnp.float32
    )
    key_grad = jnp.einsum("td,tc->dc", flat_one, grad_key_raw, preferred_element_type=jnp.float32)
    value_grad = jnp.einsum(
        "td,tc->dc", flat_one, grad_value_raw, preferred_element_type=jnp.float32
    )
    grad_normed_one = jnp.einsum(
        "tc,dc->td", grad_query_raw, query_weight, preferred_element_type=jnp.float32
    )
    grad_normed_one = grad_normed_one + jnp.einsum(
        "tc,dc->td", grad_key_raw, key_weight, preferred_element_type=jnp.float32
    )
    grad_normed_one = grad_normed_one + jnp.einsum(
        "tc,dc->td", grad_value_raw, value_weight, preferred_element_type=jnp.float32
    )
    grad_normed_one = reduce_rows(grad_normed_one.reshape(seqs, group_rows, width))
    grad_source_one, grad_gain_one = norm_backward(grad_normed_one, unit_one, factor_one, gain_one)
    grad_tokens = grad_middle + grad_source_one
    weight_grads = (
        lax.psum_scatter(query_grad, ("dp", "ctx"), scatter_dimension=0, tiled=True),
        lax.psum_scatter(key_grad, ("dp", "ctx"), scatter_dimension=0, tiled=True),
        lax.psum_scatter(value_grad, ("dp", "ctx"), scatter_dimension=0, tiled=True),
        lax.psum_scatter(out_grad, ("dp", "ctx"), scatter_dimension=1, tiled=True),
        lax.psum_scatter(gate_grad, ("dp", "ctx"), scatter_dimension=0, tiled=True),
        lax.psum_scatter(up_grad, ("dp", "ctx"), scatter_dimension=0, tiled=True),
        lax.psum_scatter(down_grad, ("dp", "ctx"), scatter_dimension=1, tiled=True),
    )
    gain_grads = lax.psum(
        (grad_gain_one, grad_q_part, grad_k_part, grad_gain_two), ("dp", "ctx", "tensor")
    )
    return (
        layer_out,
        grad_tokens,
        gain_grads[0],
        weight_grads[0],
        weight_grads[1],
        weight_grads[2],
        gain_grads[1],
        gain_grads[2],
        weight_grads[3],
        gain_grads[3],
        weight_grads[4],
        weight_grads[5],
        weight_grads[6],
    )


NT = (((1,), (1,)), ((), ()))
TN = (((0,), (0,)), ((), ()))
NN = (((1,), (0,)), ((), ()))
SCALE = HD ** (-0.5)
GAIN_ROWS = 16
VMEM_LIMIT = 44 * 1024 * 1024
COSTS = {}
TIES = {'mo': ['m_w'], 'branch': ['mo'], 'oth': ['pb'], 'pb': ['a_w'], 'one_core': ['m_x'], 'gain_core': ['m_x'], 'gain_x': ['a_x2'], 'm_z1': ['a_w'], 'one_y': ['m_z1'], 'a_z2': ['one_y'], 'f_y': ['m_y']}


def dot(left, right, dims=NN):
    return lax.dot_general(left, right, dims, preferred_element_type=jnp.float32)


def shape_of(shape, dtype):
    return jax.ShapeDtypeStruct(shape, dtype)


def call(name, kernel, grid, words, inputs, outputs, scratch, flops):

    def spec(block, index):
        if index is None:
            return pl.BlockSpec(block, lambda *ids: (0,) * len(block))
        return pl.BlockSpec(block, index)

    return pl.pallas_call(
        kernel,
        grid_spec=pltpu.PrefetchScalarGridSpec(
            num_scalar_prefetch=1,
            grid=(grid,),
            in_specs=[spec(block, index) for _, block, index in inputs],
            out_specs=[spec(block, index) for _, _, block, index in outputs],
            scratch_shapes=scratch,
        ),
        out_shape=[shape_of(shape, dtype) for shape, dtype, _, _ in outputs],
        compiler_params=pltpu.CompilerParams(vmem_limit_bytes=VMEM_LIMIT),
        cost_estimate=pl.CostEstimate(flops=COSTS.get(name, 0) * flops, bytes_accessed=0, transcendentals=0),
    )(words, *[array for array, _, _ in inputs])


def whole(array):
    return (array, array.shape, None)


def sort_runs(block_of, run, *pairs):
    for index in range(4):
        source = pl.multiple_of(block_of[index] * run, run)
        for target, origin in pairs:
            target[pl.ds(index * run, run), :] = origin[pl.ds(source, run), :]


def turn(source):
    return pltpu.roll(source, HD // 2, 1)


def unit_of(raw):
    factor = lax.rsqrt(jnp.mean(raw * raw, axis=-1, keepdims=True) + EPSILON)
    return (raw * factor, factor)


def raw_scores(keys, query, visible, run):
    scores = dot(keys, query, NT) * SCALE
    count = scores.shape[0]
    last = jnp.where(visible, scores[count - run :], NEGATIVE)
    if count == run:
        return last
    return jnp.concatenate([scores[: count - run], last], axis=0)


def place_all(member, groups, refs, target, columns=slice(None), depth=None):
    for indices, ref in zip(groups, refs):
        for place, index in enumerate(indices):
            value = ref[place] if depth is None else ref[place, :depth]
            size = value.shape[0]
            start = pl.multiple_of((member ^ index) * size, size)
            target[pl.ds(start, size), columns] = value


def pick(first_ref, second_ref):
    half = pl.num_programs(0) // 2
    return jnp.where(pl.program_id(0) < half, first_ref[...], second_ref[...])


def project_kernel(groups, member_ref, xa_ref, xb_ref, cos_ref, sin_ref, *refs):
    pieces, rest = refs[:-7], refs[-7:]
    normed_ref, q_ref, k_ref, v_ref, raw_ref, weight_ref, gains_ref = rest
    depth = pieces[0].shape[1] - GAIN_ROWS

    @pl.when(pl.program_id(0) == 0)
    def _():
        place_all(member_ref[0], groups, pieces, weight_ref, depth=depth)
        gains = jnp.zeros(gains_ref.shape, jnp.float32)
        for piece in pieces:
            for place in range(piece.shape[0]):
                gains += piece[place, depth:].astype(jnp.float32)
        gains_ref[...] = gains

    unit, _ = unit_of(pick(xa_ref, xb_ref).astype(jnp.float32))
    normed = (unit * gains_ref[0:1, :]).astype(jnp.bfloat16)
    normed_ref[...] = normed
    product = dot(normed, weight_ref[...])
    raw_width = raw_ref.shape[1]
    raw_ref[...] = product[:, :raw_width]
    v_ref[...] = product[:, raw_width:].astype(jnp.bfloat16)
    cosine = cos_ref[...]
    sine = sin_ref[...]
    q_heads = q_ref.shape[1] // HD
    for head in range(raw_width // HD):
        unit, _ = unit_of(product[:, head * HD : (head + 1) * HD])
        target, place, row = (q_ref, head, 2) if head < q_heads else (k_ref, head - q_heads, 3)
        normed = unit * gains_ref[row : row + 1, :HD]
        rotated = normed * cosine + turn(normed) * sine
        target[:, place * HD : (place + 1) * HD] = rotated.astype(jnp.bfloat16)


def project(member, x_first, x_second, groups, pieces, cosine, sine, q_width, k_width):
    rows = cosine.shape[0]
    width = x_first.shape[1]
    block = rows // 4
    total = q_width + 2 * k_width
    bf16, f32 = jnp.bfloat16, jnp.float32

    def by_rows(i, member):
        return (i, 0)

    return call(
        "P",
        functools.partial(project_kernel, groups),
        4,
        member,
        [
            (x_first, (block, width), first_half),
            (x_second, (block, width), second_half),
            (cosine, (block, HD), by_rows),
            (sine, (block, HD), by_rows),
        ]
        + [whole(piece) for piece in pieces],
        [
            ((rows, width), bf16, (block, width), by_rows),
            ((rows, q_width), bf16, (block, q_width), by_rows),
            ((rows, k_width), bf16, (block, k_width), by_rows),
            ((rows, k_width), bf16, (block, k_width), by_rows),
            ((rows, q_width + k_width), f32, (block, q_width + k_width), by_rows),
            ((width, total), bf16, (width, total), None),
            ((GAIN_ROWS, width), f32, (GAIN_ROWS, width), None),
        ],
        [],
        2 * rows * width * total,
    )


def forward_kernel(
    block_of, q_ref, k_ref, v_ref, column_ref, row_ref, mixed_ref, lse_ref, keys, values, columns
):
    run = q_ref.shape[0] // 4
    sort_runs(block_of, run, (keys, k_ref), (values, v_ref), (columns, column_ref))
    for index in range(4):
        count = run * (index + 1)
        rows = pl.ds(pl.multiple_of(block_of[index] * run, run), run)
        visible = columns[pl.ds(count - run, run), :] <= row_ref[:, rows]
        for head in range(q_ref.shape[1] // HD):
            lanes = pl.ds(head * HD, HD)
            scores = raw_scores(keys[:count], q_ref[rows, lanes], visible, run)
            row_max = jnp.max(scores, axis=0, keepdims=True)
            raised = jnp.exp(scores - row_max)
            row_total = jnp.sum(raised, axis=0, keepdims=True)
            probs = (raised * (1.0 / row_total)).astype(jnp.bfloat16)
            mixed_ref[rows, lanes] = dot(probs, values[:count], TN).astype(jnp.bfloat16)
            lse_ref[pl.ds(head, 1), rows] = row_max + jnp.log(row_total)


def by_group(group, order):
    return (0, group)


def by_lead(group, order):
    return (group, 0, 0)


def attend(block_of, queries, keys, values, column, row):
    rows, width = keys.shape
    groups = width // HD
    pair = queries.shape[1] // groups
    return call(
        "attn",
        forward_kernel,
        groups,
        block_of,
        [
            (queries, (rows, pair), by_group),
            (keys, (rows, HD), by_group),
            (values, (rows, HD), by_group),
            whole(column),
            whole(row),
        ],
        [
            (queries.shape, jnp.bfloat16, (rows, pair), by_group),
            ((groups, pair // HD, rows), jnp.float32, (None, pair // HD, rows), by_lead),
        ],
        [
            pltpu.VMEM((rows, HD), jnp.bfloat16),
            pltpu.VMEM((rows, HD), jnp.bfloat16),
            pltpu.VMEM((rows, 1), jnp.int32),
        ],
        3 * rows * rows * queries.shape[1],
    )


def first_half(i, member):
    return (jnp.minimum(i, 1), 0)


def second_half(i, member):
    return (jnp.maximum(i - 2, 0), 0)


def store_halves(product, kept_ref, sent_ref):
    half = pl.num_programs(0) // 2

    @pl.when(pl.program_id(0) < half)
    def _():
        kept_ref[...] = product

    @pl.when(pl.program_id(0) >= half)
    def _():
        sent_ref[...] = product.astype(jnp.bfloat16)


def halves_out(rows, block, width):
    return [
        ((rows // 2, width), jnp.float32, (block, width), first_half),
        ((rows // 2, width), jnp.bfloat16, (block, width), second_half),
    ]


def out_kernel(groups, member_ref, mixed_ref, *refs):
    pieces, (kept_ref, sent_ref, weight_ref) = refs[:-3], refs[-3:]

    @pl.when(pl.program_id(0) == 0)
    def _():
        place_all(member_ref[0], groups, pieces, weight_ref)

    store_halves(dot(mixed_ref[...], weight_ref[...], NT), kept_ref, sent_ref)


def project_out(member, mixed, groups, pieces):
    rows, depth = mixed.shape
    block = rows // 4
    width = pieces[0].shape[1] * sum(piece.shape[0] for piece in pieces)
    return call(
        "out",
        functools.partial(out_kernel, groups),
        4,
        member,
        [(mixed, (block, depth), lambda i, member: (i, 0))] + [whole(piece) for piece in pieces],
        halves_out(rows, block, width)
        + [((width, depth), jnp.bfloat16, (width, depth), None)],
        [],
        2 * rows * width * depth,
    )


def back_kernel(starts, member_ref, xa_ref, xb_ref, *refs):
    grad_refs, (weight_ref, kept_ref, sent_ref, gain_ref) = refs[:-4], refs[-4:]
    product = None
    for start, grad_ref in zip(starts, grad_refs):
        term = dot(grad_ref[...], weight_ref[:, start : start + grad_ref.shape[1]], NT)
        product = term if product is None else product + term
    unit, _ = unit_of(pick(xa_ref, xb_ref).astype(jnp.float32))

    @pl.when(pl.program_id(0) == 0)
    def _():
        gain_ref[...] = jnp.zeros_like(gain_ref)

    gain_ref[...] += jnp.sum(product * unit, axis=0, keepdims=True)
    store_halves(product, kept_ref, sent_ref)


def project_back(member, x_first, x_second, starts, grads, weight):
    rows = grads[0].shape[0]
    block = rows // 4
    width, total = weight.shape
    return call(
        "pb",
        functools.partial(back_kernel, starts),
        4,
        member,
        [
            (x_first, (block, width), first_half),
            (x_second, (block, width), second_half),
        ]
        + [(grad, (block, grad.shape[1]), lambda i, member: (i, 0)) for grad in grads]
        + [whole(weight)],
        halves_out(rows, block, width) + [((1, width), jnp.float32, (1, width), None)],
        [],
        2 * rows * width * total,
    )


def mlp_kernel(member_ref, xa_ref, xb_ref, ga_ref, gb_ref, gate_up, down_ref, *rest):
    bf16 = jnp.bfloat16
    hidden_ref, grad_ref, kept_ref, sent_ref = rest
    width = down_ref.shape[1]
    x = pick(xa_ref, xb_ref)
    product = dot(x, gate_up[...])
    grad_hidden = dot(pick(ga_ref, gb_ref), down_ref[...])
    gate = product[:, :width]
    up = product[:, width:]
    sigmoid = jax.nn.sigmoid(gate)
    silu = gate * sigmoid
    hidden_ref[...] = (silu * up).astype(bf16)
    grad_gate = (grad_hidden * up * sigmoid * (1.0 + gate * (1.0 - sigmoid))).astype(bf16)
    grad_up = (grad_hidden * silu).astype(bf16)
    grad_ref[:, :width] = grad_gate
    grad_ref[:, width:] = grad_up
    grad_x = dot(grad_gate, gate_up[:, :width], NT) + dot(grad_up, gate_up[:, width:], NT)
    store_halves(grad_x, kept_ref, sent_ref)


def third_quarter(i, member):
    return (2 + jnp.minimum(i, 1), 0)


def fourth_quarter(i, member):
    return (jnp.maximum(i, 2), 0)


def feed(member, x_first, x_second, own_half, core_half, weight):
    rows, width = own_half.shape
    hidden_width = weight.shape[1] // 3
    block = rows // 4
    bf16 = jnp.bfloat16

    def by_rows(i, member):
        return (i, 0)

    return call(
        "mlp",
        mlp_kernel,
        4,
        member,
        [
            (x_first, (block, width), first_half),
            (x_second, (block, width), second_half),
            (own_half, (block, width), third_quarter),
            (core_half, (block, width), fourth_quarter),
            (weight, (width, 2 * hidden_width), lambda i, member: (0, 0)),
            (weight, (width, hidden_width), lambda i, member: (0, 2)),
        ],
        [
            ((rows, hidden_width), bf16, (block, hidden_width), by_rows),
            ((rows, 2 * hidden_width), bf16, (block, 2 * hidden_width), by_rows),
        ]
        + halves_out(rows, block, width),
        [],
        10 * rows * width * hidden_width,
    )


def mlp_out_kernel(member_ref, hidden_ref, weight_ref, kept_ref, sent_ref):
    store_halves(dot(hidden_ref[...], weight_ref[...], NT), kept_ref, sent_ref)


def feed_out(member, hidden, weight):
    rows, depth = hidden.shape
    width = weight.shape[0]
    block = rows // 4
    return call(
        "mo",
        mlp_out_kernel,
        4,
        member,
        [
            (hidden, (block, depth), lambda i, member: (i, 0)),
            (weight, (width, depth), lambda i, member: (0, 2)),
        ],
        halves_out(rows, block, width),
        [],
        2 * rows * width * depth,
    )


def weight_grad_kernel(layout, member_ref, *refs):
    inputs, (kept_ref, sent_ref, product) = refs[:-3], refs[-3:]
    half = product.shape[0] // 2
    start = place = 0
    for lefts, rights in layout:
        left_refs = inputs[place : place + lefts]
        right_refs = inputs[place + lefts : place + lefts + rights]
        place += lefts + rights
        for right_ref in right_refs:
            stop = start + right_ref.shape[1]
            total = None
            row = 0
            for left_ref in left_refs:
                count = left_ref.shape[0]
                term = dot(left_ref[...], right_ref[row : row + count, :], TN)
                total = term if total is None else total + term
                row += count
            product[:, start:stop] = total.astype(jnp.bfloat16)
            start = stop
    near = member_ref[0] % 2
    kept_ref[...] = product[pl.ds(pl.multiple_of(near * half, half), half), :]
    sent_ref[...] = product[pl.ds(pl.multiple_of((1 - near) * half, half), half), :]


def weight_grad(member, dp_size, parts):
    width = parts[0][0][0].shape[1]
    pairs = dp_size // 2
    half = width // dp_size
    bits = pairs.bit_length() - 1
    inputs = []
    layout = []
    total = flops = 0

    def by_member(quarter, i, member):
        turned = sum(((i >> bit) & 1) << (bits - 1 - bit) for bit in range(bits))
        return (quarter, (member[0] // 2) ^ turned)

    for lefts, quarter, rights in parts:
        rows = rights[0].shape[0]
        for left in lefts:
            index = functools.partial(by_member, quarter)
            inputs.append((left, (rows // len(lefts), 2 * half), index))
        inputs += [whole(right) for right in rights]
        layout.append((len(lefts), len(rights)))
        columns = sum(right.shape[1] for right in rights)
        total += columns
        flops += 2 * rows * width * columns
    result = ((pairs, half, total), jnp.bfloat16, (None, half, total), lambda i, member: (i, 0, 0))
    return call(
        "wg",
        functools.partial(weight_grad_kernel, layout),
        pairs,
        member,
        inputs,
        [result, result],
        [pltpu.VMEM((2 * half, total), jnp.bfloat16)],
        flops,
    )


def norm_rope_back(grad, raw, cosine, sine, gain):
    grad_normed = grad * cosine - turn(grad) * sine
    unit, factor = unit_of(raw)
    gain_part = jnp.sum(grad_normed * unit, axis=0, keepdims=True)
    grad_unit = grad_normed * gain
    projected = jnp.mean(grad_unit * unit, axis=-1, keepdims=True)
    return ((factor * (grad_unit - unit * projected)).astype(jnp.bfloat16), gain_part)


def backward_kernel(
    block_of,
    q_ref,
    k_ref,
    v_ref,
    branch_a_ref,
    branch_b_ref,
    out_weight_ref,
    lse_ref,
    column_ref,
    row_ref,
    raw_q_ref,
    raw_k_ref,
    cos_ref,
    sin_ref,
    gains_ref,
    dq_ref,
    dk_ref,
    dv_ref,
    q_part_ref,
    k_part_ref,
    keys,
    values,
    columns,
    key_sum,
    value_sum,
    grad_mixed,
):
    run = q_ref.shape[0] // 4
    sort_runs(block_of, run, (keys, k_ref), (values, v_ref), (columns, column_ref))
    key_sum[...] = jnp.zeros_like(key_sum)
    value_sum[...] = jnp.zeros_like(value_sum)
    half = branch_a_ref.shape[0]
    grad_mixed[:half, :] = dot(branch_a_ref[...], out_weight_ref[...]).astype(jnp.bfloat16)
    grad_mixed[half:, :] = dot(branch_b_ref[...], out_weight_ref[...]).astype(jnp.bfloat16)
    q_part = jnp.zeros((1, HD), jnp.float32)
    k_part = jnp.zeros((1, HD), jnp.float32)
    q_gain = gains_ref[2:3, :HD]
    k_gain = gains_ref[3:4, :HD]
    for index in range(4):
        count = run * (index + 1)
        rows = pl.ds(pl.multiple_of(block_of[index] * run, run), run)
        visible = columns[pl.ds(count - run, run), :] <= row_ref[:, rows]
        for head in range(q_ref.shape[1] // HD):
            lanes = pl.ds(head * HD, HD)
            query = q_ref[rows, lanes]
            grad = grad_mixed[rows, lanes]
            scores = raw_scores(keys[:count], query, visible, run)
            probs = jnp.exp(scores - lse_ref[pl.ds(head, 1), rows])
            grad_probs = dot(values[:count], grad, NT)
            delta = jnp.sum(probs * grad_probs, axis=0, keepdims=True)
            grad_scores = (probs * (grad_probs - delta)).astype(jnp.bfloat16)
            value_sum[:count, :] += dot(probs.astype(jnp.bfloat16), grad)
            key_sum[:count, :] += dot(grad_scores, query)
            grad_query = dot(grad_scores, keys[:count], TN) * SCALE
            dq_ref[rows, lanes], part = norm_rope_back(
                grad_query, raw_q_ref[rows, lanes], cos_ref[rows, :], sin_ref[rows, :], q_gain
            )
            q_part += part
    for index in range(4):
        rows = pl.ds(pl.multiple_of(block_of[index] * run, run), run)
        sorted_rows = pl.ds(index * run, run)
        dk_ref[rows, :], part = norm_rope_back(
            key_sum[sorted_rows, :] * SCALE,
            raw_k_ref[rows, :],
            cos_ref[rows, :],
            sin_ref[rows, :],
            k_gain,
        )
        k_part += part
        dv_ref[rows, :] = value_sum[sorted_rows, :].astype(jnp.bfloat16)
    q_part_ref[...] = q_part
    k_part_ref[...] = k_part


def attend_back(
    group, block_of, queries, keys, values, branches, out_weight, lse, column, row, raw, cosine, sine, gains
):
    rows, width = keys.shape
    groups = width // HD
    pair = queries.shape[1] // groups
    first_key = queries.shape[1] // HD
    depth = out_weight.shape[0]
    bf16, f32 = jnp.bfloat16, jnp.float32
    part = ((1, HD), f32, (1, HD), None)

    def this_group(i, order):
        return (0, group)

    return call(
        "ab",
        backward_kernel,
        1,
        block_of,
        [
            (queries, (rows, pair), this_group),
            (keys, (rows, HD), this_group),
            (values, (rows, HD), this_group),
            whole(branches[0]),
            whole(branches[1]),
            (out_weight, (depth, pair), this_group),
            (lse, (None, pair // HD, rows), lambda i, order: (group, 0, 0)),
            whole(column),
            whole(row),
            (raw, (rows, pair), this_group),
            (raw, (rows, HD), lambda i, order: (0, first_key + group)),
            whole(cosine),
            whole(sine),
            whole(gains),
        ],
        [
            ((rows, pair), bf16, (rows, pair), None),
            ((rows, HD), bf16, (rows, HD), None),
            ((rows, HD), bf16, (rows, HD), None),
            part,
            part,
        ],
        [
            pltpu.VMEM((rows, HD), bf16),
            pltpu.VMEM((rows, HD), bf16),
            pltpu.VMEM((rows, 1), jnp.int32),
            pltpu.VMEM((rows, HD), f32),
            pltpu.VMEM((rows, HD), f32),
            pltpu.VMEM((rows, pair), bf16),
        ],
        3 * rows * rows * queries.shape[1],
    )


def swap(source, axis, size, bit=1):
    return lax.ppermute(source, axis, [(i, i ^ bit) for i in range(size)])


def after(source, *events):
    return lax.optimization_barrier((source, events))[0]


def group_body(
    dp_size,
    tokens,
    places,
    attn_gain,
    w_query,
    w_key,
    w_value,
    q_gain,
    k_gain,
    w_out,
    mlp_gain,
    w_gate,
    w_up,
    w_down,
    cotangent,
):
    bf16, f32 = jnp.bfloat16, jnp.float32
    run, width = tokens.shape[1:]
    side = lax.axis_index("ctx")
    core = lax.axis_index("tensor")
    member = lax.axis_index("dp")
    word = member[None]
    q_width = w_query.shape[1] // 2
    k_width = w_key.shape[1] // 2
    hidden_width = w_gate.shape[1] // 2
    z_bits = [1 << bit for bit in range(1, dp_size.bit_length() - 1)]
    near_steps = list(range(2, dp_size, 2))
    groups = [[0], near_steps, [1], [step ^ 1 for step in near_steps]]

    def over_core(source):
        return swap(source, "tensor", 2)

    def over_ctx(source):
        return swap(source, "ctx", 2)

    def over_dp(source, bit):
        return swap(source, "dp", dp_size, bit)

    def over_z(shard):
        return [over_dp(shard, step) for step in near_steps]

    def mine(source, axis):
        size = source.shape[axis] // 2
        return lax.dynamic_slice_in_dim(source, side * size, size, axis).astype(bf16)

    def as_rows(values, columns):
        high = values.astype(bf16)
        low = (values - high.astype(f32)).astype(bf16)
        digits = jnp.concatenate([high, low])
        return jnp.pad(digits, (0, GAIN_ROWS * columns - digits.shape[0])).reshape(GAIN_ROWS, columns)

    def from_rows(rows, count):
        digits = rows.reshape(-1).astype(f32)
        return digits[:count] + digits[count : 2 * count]

    gain_rows = jnp.zeros((GAIN_ROWS, width), bf16)
    for row, gain in enumerate((attn_gain, mlp_gain, q_gain, k_gain)):
        gain_rows = lax.dynamic_update_slice(
            gain_rows, gain.astype(bf16)[None], (row, member * gain.shape[0])
        )
    qkv_shard = jnp.concatenate([mine(w_query, 1), mine(w_key, 1), mine(w_value, 1)], axis=1)
    qkv_shard = jnp.concatenate([qkv_shard, gain_rows], axis=0)
    out_shard = mine(w_out, 0).T
    mlp_shard = jnp.concatenate([mine(w_gate, 1), mine(w_up, 1), mine(w_down, 0).T], axis=1)

    place_count = places.shape[1]
    digits = jnp.zeros((GAIN_ROWS, width), bf16)
    for row, digit in enumerate((places // 128, places % 128)):
        digits = lax.dynamic_update_slice(digits, digit.astype(bf16), (row, 0))
    message = jnp.concatenate([tokens[0], cotangent[0], digits], axis=0)
    events = {}

    def tied(name, source):
        names = [other for other in TIES.get(name, ()) if other in events]
        return after(source, *[events[other] for other in names]) if names else source

    def told(name, raw):
        events[name] = raw
        return raw

    qkv_near, qkv_far, message = lax.optimization_barrier(
        (over_z(qkv_shard), over_dp(qkv_shard, 1), over_ctx(message))
    )
    told("s0", message)
    qkv_near = jnp.stack(qkv_near)
    own_half = jnp.concatenate(
        [tokens[0], message[:run], cotangent[0], message[run : 2 * run]], axis=0
    )
    core_half = told("tok", over_core(tied("tok", own_half)))
    qkv_far_rest = told("a_x", over_dp(tied("a_x", qkv_near), 1))
    mlp_weight = lax.all_gather(
        after(tied("ag", mlp_shard), qkv_near), "dp", axis=0, tiled=True
    )
    out_near = told("o_z", over_z(after(tied("o_z", out_shard), qkv_near)))
    half = 2 * run
    digits = message[2 * run : 2 * run + 2, :place_count].astype(jnp.int32)
    other_places = (digits[0] * 128 + digits[1]).reshape(2, run)
    own_places = places[0].reshape(2, run)
    place_blocks = jnp.stack([own_places, other_places], axis=1)
    place_blocks = jnp.where(core == 0, place_blocks, place_blocks[::-1]).reshape(-1)
    place_column = place_blocks[:, None]
    place_row = place_blocks[None, :]
    home_side = jnp.array([0, 1, 1, 0], jnp.int32)
    home_core = jnp.array([0, 0, 1, 1], jnp.int32)
    block_of = (home_core ^ core) * 2 + (home_side ^ side)
    cosine, sine_table = (table[:, 0] for table in rope_tables(place_blocks))
    sine_table = sine_table * jnp.where(jnp.arange(HD) < HD // 2, -1.0, 1.0).astype(f32)
    own_half, core_half, cosine, sine_table, place_column, block_of = lax.optimization_barrier(
        (own_half, core_half, cosine, sine_table, place_column, block_of)
    )
    normed_one, queries, key_rows, value_rows, raw, qkv_weight, gains = project(
        word,
        tied("P", own_half),
        core_half,
        groups,
        [qkv_shard[None], qkv_near, qkv_far[None], qkv_far_rest],
        cosine,
        sine_table,
        q_width,
        k_width,
    )
    told("P", queries)
    out_near = jnp.stack([out_shard] + out_near)
    out_far = told("o_ax", over_dp(tied("o_ax", out_near), 1))
    mixed, lse_rows = attend(
        block_of, tied("attn", queries), key_rows, value_rows, place_column, place_row
    )
    told("attn", mixed)
    orders = [[0] + near_steps, [1] + [step ^ 1 for step in near_steps]]
    out_kept, out_sent, out_weight = project_out(
        word, tied("out", mixed), orders, [out_near, out_far]
    )

    def ctx_sum(name, summed):
        other = told(name, over_ctx(tied(name, summed.astype(bf16))))
        return summed + jnp.concatenate([other[run:], other[:run]], axis=0).astype(f32)

    source = own_half[:half].astype(f32)
    middle = source + ctx_sum("ar1", out_kept + over_core(out_sent).astype(f32))
    gain_two = gains[1]
    normed_two, unit_two, factor_two = norm_forward(middle, gain_two)
    normed_two = normed_two.astype(bf16)
    normed_other = over_core(normed_two)
    hidden, grad_gate_up, grad_kept, grad_sent = feed(
        word, tied("mlp", normed_two), normed_other, own_half, core_half, mlp_weight
    )

    def halves(block):
        size = block.shape[0] // 2
        kept = lax.dynamic_slice_in_dim(block, side * size, size, 0)
        sent = lax.dynamic_slice_in_dim(block, (1 - side) * size, size, 0)
        return kept, sent

    def joined(kept, other):
        return jnp.where(
            side == 0,
            jnp.concatenate([kept, other], axis=1),
            jnp.concatenate([other, kept], axis=1),
        )

    def summed(name, kept, sent, bit):
        received = told(name, over_dp(tied(name, sent.astype(bf16)), bit))
        return kept.astype(f32) + received.astype(f32)

    def summed_half(name, total, bit):
        count = total.shape[0] // 2
        return summed(name, total[:count], total[count:], bit)

    grad_other = told("mid_core", over_core(grad_sent))
    hidden, grad_gate_up, grad_other = lax.optimization_barrier((hidden, grad_gate_up, grad_other))
    grad_normed_two = grad_kept + grad_other.astype(f32)
    m_pair = weight_grad(
        word,
        dp_size,
        [
            ([normed_two, normed_other], 0, [tied("m_w", grad_gate_up)]),
            ([own_half, core_half], 1, [hidden]),
        ],
    )
    told("m_w", m_pair[1])
    m_sum = summed("m_x", *m_pair, 1)
    mlp_kept, mlp_sent = feed_out(word, tied("mo", hidden), mlp_weight)
    told("mo", mlp_sent)
    mlp_event = told("mo_core", over_core(tied("mo_core", mlp_sent)))
    grad_normed_two = ctx_sum("ar2", grad_normed_two)
    grad_source_two, _ = norm_backward(grad_normed_two, unit_two, factor_two, gain_two)
    grad_gain_two = jnp.sum(grad_normed_two[:run] * unit_two[:run], axis=0)
    grad_middle = own_half[half:].astype(f32) + grad_source_two
    branch = grad_middle.astype(bf16)
    branches = [branch, told("branch", over_core(tied("branch", branch)))]
    def back(name, group):
        result = attend_back(
            group,
            block_of,
            tied(name, queries),
            key_rows,
            value_rows,
            branches,
            out_weight,
            lse_rows,
            place_column,
            place_row,
            raw,
            cosine,
            sine_table,
            gains,
        )
        told(name, result[0])
        return result

    first_back = back("g0", 0)
    second_back = back("g1", 1)
    mlp_part = tied("oth", mlp_kept) + mlp_event.astype(f32)
    other_part = told("oth", over_ctx(mlp_part[run:].astype(bf16)))
    layer_out = middle[:run] + mlp_part[:run] + other_part.astype(f32)
    back_grads = [grads[part] for part in range(3) for grads in (first_back, second_back)]
    a_pair = weight_grad(
        word,
        dp_size,
        [(branches, 0, [tied("a_w", mixed)]), ([normed_one], 0, back_grads)],
    )
    told("a_w", a_pair[1])
    a_sum = summed("a_x2", *a_pair, 1)
    m_sum = summed_half("m_z1", m_sum, z_bits[0])
    m_sum = summed("m_z2", m_sum[0], m_sum[1], z_bits[1])
    q_half, k_half = q_width // 2, k_width // 2
    starts = [0, q_half, q_width, q_width + k_half, q_width + k_width, q_width + k_width + k_half]
    back_grads[0] = tied("pb", back_grads[0])
    one_kept, one_sent, grad_gain_one = project_back(
        word, own_half, core_half, starts, back_grads, qkv_weight
    )
    told("pb", one_sent)
    one_event = told("one_core", over_core(tied("one_core", one_sent)))
    gain_grads = jnp.concatenate(
        [
            grad_gain_one[0],
            grad_gain_two,
            (first_back[3] + second_back[3])[0],
            (first_back[4] + second_back[4])[0],
        ]
    )
    gain_count = gain_grads.shape[0]
    gain_grads = gain_grads + told("gain_core", over_core(tied("gain_core", gain_grads)))
    gain_grads = gain_grads + told("gain_x", over_dp(tied("gain_x", gain_grads), 1))
    gain_grads = gain_grads + told("gain_z", over_dp(tied("gain_z", gain_grads), z_bits[0]))
    a_sum = summed_half("a_z1", a_sum, z_bits[0])
    one_sum = one_kept + one_event.astype(f32)
    one_other = told("one_y", over_ctx(tied("one_y", one_sum[run:].astype(bf16))))
    grad_normed_one = one_sum[:run] + one_other.astype(f32)
    _, unit_one, factor_one = norm_forward(tokens[0].astype(f32), gains[0])
    grad_source_one, _ = norm_backward(grad_normed_one, unit_one, factor_one, gains[0])
    grad_tokens = grad_middle[:run] + grad_source_one

    def with_gains(blocks, gains):
        columns = blocks.shape[-1]
        return jnp.concatenate(
            [blocks.astype(bf16).reshape(-1, columns), as_rows(gains, columns)], axis=0
        )

    rows = a_sum.shape[1]
    mlp_kept, mlp_sent = halves(m_sum)
    mlp_other = told("m_y", over_ctx(tied("m_y", mlp_sent.astype(bf16))))
    received = told("a_z2", over_dp(tied("a_z2", with_gains(a_sum[1], gain_grads)), z_bits[1]))
    a_sum = a_sum[0] + received[:rows].astype(f32)
    gain_grads = gain_grads + from_rows(received[rows:], gain_count)
    attn_kept, attn_sent = halves(a_sum)
    received = over_ctx(tied("f_y", with_gains(attn_sent, gain_grads)))
    gain_grads = gain_grads + from_rows(received[rows // 2 :], gain_count)
    attn_pair = (attn_kept, received[: rows // 2])
    mlp_pair = (mlp_kept, mlp_other)

    def part(pair, *columns):
        kept, other = (
            jnp.concatenate([block[:, start : start + size] for start, size in columns], axis=1)
            for block in pair
        )
        return joined(kept.astype(f32), other.astype(f32))

    v_start = 2 * q_width + k_width
    return (
        layer_out[None],
        grad_tokens[None],
        gain_grads[:width],
        part(attn_pair, (q_width, q_width)),
        part(attn_pair, (2 * q_width, k_width)),
        part(attn_pair, (v_start, k_width)),
        gain_grads[2 * width : 2 * width + HD],
        gain_grads[2 * width + HD :],
        part(attn_pair, (0, q_width)).T,
        gain_grads[width : 2 * width],
        part(mlp_pair, (0, hidden_width)),
        part(mlp_pair, (hidden_width, hidden_width)),
        part(mlp_pair, (2 * hidden_width, hidden_width)).T,
    )


def plan(mesh):
    sizes = dict(mesh.shape)
    if sizes["ctx"] == 2 and sizes["tensor"] == 2 and sizes["dp"] == 8:
        return functools.partial(group_body, sizes["dp"])
    return split_body


def solution(mesh):
    in_specs = (
        P("dp", ("ctx", "tensor"), None),
        P("dp", "ctx"),
        P("dp"),
        P("dp", "tensor"),
        P("dp", "tensor"),
        P("dp", "tensor"),
        P("dp"),
        P("dp"),
        P("tensor", "dp"),
        P("dp"),
        P("dp", "tensor"),
        P("dp", "tensor"),
        P("tensor", "dp"),
        P("dp", ("ctx", "tensor"), None),
    )
    out_specs = (
        P("dp", ("ctx", "tensor"), None),
        P("dp", ("ctx", "tensor"), None),
        P(),
        P(("dp", "ctx"), "tensor"),
        P(("dp", "ctx"), "tensor"),
        P(("dp", "ctx"), "tensor"),
        P(),
        P(),
        P("tensor", ("dp", "ctx")),
        P(),
        P(("dp", "ctx"), "tensor"),
        P(("dp", "ctx"), "tensor"),
        P("tensor", ("dp", "ctx")),
    )
    return jax.shard_map(plan(mesh), mesh=mesh, in_specs=in_specs, out_specs=out_specs, check_vma=False)
```

```python
import functools

import jax
import jax.numpy as jnp
from jax import lax
from jax.experimental import pallas as pl
from jax.experimental.pallas import tpu as pltpu
from jax.sharding import PartitionSpec as P

HD = 128


EPSILON = 1e-06
ROPE_BASE = 1000000.0
NEGATIVE = -1e30


def gather_rows(source):
    return lax.all_gather(source, "tensor", axis=1, tiled=True)


def reduce_rows(partial_sum):
    return lax.psum_scatter(partial_sum, "tensor", scatter_dimension=1, tiled=True)


def norm_forward(source, gain):
    factor = lax.rsqrt(jnp.mean(source * source, axis=-1, keepdims=True) + EPSILON)
    unit = source * factor
    return (unit * gain, unit, factor)


def norm_backward(grad_normed, unit, factor, gain):
    grad_unit = grad_normed * gain
    grad_gain = jnp.sum((grad_normed * unit).reshape(-1, unit.shape[-1]), axis=0)
    grad_source = factor * (grad_unit - unit * jnp.mean(grad_unit * unit, axis=-1, keepdims=True))
    return (grad_source, grad_gain)


def rope_tables(positions):
    freq_index = jnp.arange(HD // 2, dtype=jnp.float32)
    inverse = ROPE_BASE ** (-2.0 * freq_index / HD)
    angles = positions.astype(jnp.float32)[..., None] * inverse
    cosine = jnp.concatenate([jnp.cos(angles), jnp.cos(angles)], axis=-1)
    sine_table = jnp.concatenate([jnp.sin(angles), jnp.sin(angles)], axis=-1)
    return (cosine[..., None, :], sine_table[..., None, :])


def rotate(source, cosine, sine_table):
    half_width = source.shape[-1] // 2
    turned = jnp.concatenate([-source[..., half_width:], source[..., :half_width]], axis=-1)
    return source * cosine + turned * sine_table


def rotate_back(grad_rotated, cosine, sine_table):
    half_width = grad_rotated.shape[-1] // 2
    sined = grad_rotated * sine_table
    turned = jnp.concatenate([sined[..., half_width:], -sined[..., :half_width]], axis=-1)
    return grad_rotated * cosine + turned


def to_blocks(heads_last, kv_heads):
    seqs, row_count, width = heads_last.shape
    group_size = width // (kv_heads * HD)
    shaped = heads_last.reshape(seqs, row_count, kv_heads, group_size, HD)
    return shaped.transpose(0, 2, 3, 1, 4).reshape(seqs * kv_heads, group_size, row_count, HD)


def from_blocks(blocked, seqs):
    count, group_size, row_count, width = blocked.shape
    kv_heads = count // seqs
    shaped = blocked.reshape(seqs, kv_heads, group_size, row_count, width)
    return shaped.transpose(0, 3, 1, 2, 4).reshape(seqs, row_count, kv_heads * group_size * width)


def masked_scores(queries, key_rows, query_places, key_places):
    scores = jnp.einsum(
        "hqd,kd->hqk", queries, key_rows, preferred_element_type=jnp.float32
    ) * HD ** (-0.5)
    visible = key_places[None, None, :] <= query_places[None, :, None]
    return jnp.where(visible, scores, NEGATIVE)


def recompute(queries, key_rows, lse_rows, query_places, key_places):
    return jnp.exp(masked_scores(queries, key_rows, query_places, key_places) - lse_rows[..., None])


def forward_block(pieces):
    queries, key_rows, value_rows, query_places, key_places = pieces
    scores = masked_scores(queries, key_rows, query_places, key_places)
    row_max = jnp.max(scores, axis=-1, keepdims=True)
    raised = jnp.exp(scores - row_max)
    row_total = jnp.sum(raised, axis=-1, keepdims=True)
    attn_probs = raised / row_total
    mixed = jnp.einsum(
        "hqk,kd->hqd",
        attn_probs.astype(jnp.bfloat16),
        value_rows,
        preferred_element_type=jnp.float32,
    )
    return (mixed, (row_max + jnp.log(row_total))[..., 0])


def full_block(pieces):
    queries, grad_mixed, lse_rows, query_places, key_rows, value_rows, key_places = pieces
    attn_probs = recompute(queries, key_rows, lse_rows, query_places, key_places)
    grad_probs = jnp.einsum(
        "hqd,kd->hqk", grad_mixed, value_rows, preferred_element_type=jnp.float32
    )
    row_delta = jnp.sum(attn_probs * grad_probs, axis=-1)
    grad_scores = (attn_probs * (grad_probs - row_delta[..., None])).astype(jnp.bfloat16)
    grad_queries = jnp.einsum(
        "hqk,kd->hqd", grad_scores, key_rows, preferred_element_type=jnp.float32
    ) * HD ** (-0.5)
    grad_keys = jnp.einsum(
        "hqk,hqd->kd", grad_scores, queries, preferred_element_type=jnp.float32
    ) * HD ** (-0.5)
    grad_values = jnp.einsum(
        "hqk,hqd->kd",
        attn_probs.astype(jnp.bfloat16),
        grad_mixed,
        preferred_element_type=jnp.float32,
    )
    return (grad_queries, grad_keys, grad_values)


def split_body(
    tokens,
    places,
    attn_gain,
    w_query,
    w_key,
    w_value,
    q_gain,
    k_gain,
    w_out,
    mlp_gain,
    w_gate,
    w_up,
    w_down,
    cotangent,
):
    seqs, local_rows, width = tokens.shape
    attn_set = (
        lax.all_gather(attn_gain.astype(jnp.bfloat16), "dp", axis=0, tiled=True),
        lax.all_gather(w_query.astype(jnp.bfloat16), "dp", axis=0, tiled=True),
        lax.all_gather(w_key.astype(jnp.bfloat16), "dp", axis=0, tiled=True),
        lax.all_gather(w_value.astype(jnp.bfloat16), "dp", axis=0, tiled=True),
        lax.all_gather(q_gain.astype(jnp.bfloat16), "dp", axis=0, tiled=True),
        lax.all_gather(k_gain.astype(jnp.bfloat16), "dp", axis=0, tiled=True),
        lax.all_gather(w_out.astype(jnp.bfloat16), "dp", axis=1, tiled=True),
    )
    gain_one, query_weight, key_weight, value_weight, query_gain, key_gain, out_weight = attn_set
    mlp_set = (
        lax.all_gather(mlp_gain.astype(jnp.bfloat16), "dp", axis=0, tiled=True),
        lax.all_gather(w_gate.astype(jnp.bfloat16), "dp", axis=0, tiled=True),
        lax.all_gather(w_up.astype(jnp.bfloat16), "dp", axis=0, tiled=True),
        lax.all_gather(w_down.astype(jnp.bfloat16), "dp", axis=1, tiled=True),
    )
    gain_two, gate_weight, up_weight, down_weight = mlp_set
    gain_one = gain_one.astype(jnp.float32)
    gain_two = gain_two.astype(jnp.float32)
    query_gain = query_gain.astype(jnp.float32)
    key_gain = key_gain.astype(jnp.float32)
    source = tokens.astype(jnp.float32)
    normed_one, unit_one, factor_one = norm_forward(source, gain_one)
    rows_one = gather_rows(normed_one.astype(jnp.bfloat16))
    group_rows = rows_one.shape[1]
    flat_one = rows_one.reshape(seqs * group_rows, width)
    query_raw = jnp.dot(flat_one, query_weight, preferred_element_type=jnp.float32).reshape(
        seqs, group_rows, -1, HD
    )
    key_raw = jnp.dot(flat_one, key_weight, preferred_element_type=jnp.float32).reshape(
        seqs, group_rows, -1, HD
    )
    value_rows = (
        jnp.dot(flat_one, value_weight, preferred_element_type=jnp.float32)
        .astype(jnp.bfloat16)
        .reshape(seqs, group_rows, -1)
    )
    kv_heads = key_raw.shape[2]
    cosine, sine_table = rope_tables(places)
    query_normed, query_unit, query_factor = norm_forward(query_raw, query_gain)
    queries = (
        rotate(query_normed, cosine, sine_table).astype(jnp.bfloat16).reshape(seqs, group_rows, -1)
    )
    key_normed, key_unit, key_factor = norm_forward(key_raw, key_gain)
    key_rows = (
        rotate(key_normed, cosine, sine_table).astype(jnp.bfloat16).reshape(seqs, group_rows, -1)
    )
    key_all, value_all, places_all = (
        lax.all_gather(key_rows, "ctx", axis=1, tiled=True),
        lax.all_gather(value_rows, "ctx", axis=1, tiled=True),
        lax.all_gather(places, "ctx", axis=1, tiled=True),
    )
    query_blocks = to_blocks(queries, kv_heads)
    key_blocks = to_blocks(key_all, kv_heads)[:, 0]
    value_blocks = to_blocks(value_all, kv_heads)[:, 0]
    query_places = jnp.repeat(places, kv_heads, axis=0)
    key_places = jnp.repeat(places_all, kv_heads, axis=0)
    mixed_blocks, lse_blocks = lax.map(
        forward_block, (query_blocks, key_blocks, value_blocks, query_places, key_places)
    )
    mixed = from_blocks(mixed_blocks, seqs).astype(jnp.bfloat16).reshape(seqs * group_rows, -1)
    attn_part = jnp.dot(mixed, out_weight, preferred_element_type=jnp.float32).reshape(
        seqs, group_rows, width
    )
    middle = source + reduce_rows(attn_part)
    normed_two, unit_two, factor_two = norm_forward(middle, gain_two)
    rows_two = gather_rows(normed_two.astype(jnp.bfloat16)).reshape(seqs * group_rows, width)
    gate_act = jnp.dot(rows_two, gate_weight, preferred_element_type=jnp.float32)
    up_act = jnp.dot(rows_two, up_weight, preferred_element_type=jnp.float32)
    sigmoid_gate = jax.nn.sigmoid(gate_act)
    silu_gate = gate_act * sigmoid_gate
    hidden = (silu_gate * up_act).astype(jnp.bfloat16)
    mlp_part = jnp.dot(hidden, down_weight, preferred_element_type=jnp.float32).reshape(
        seqs, group_rows, width
    )
    layer_out = middle + reduce_rows(mlp_part)
    grad_rows = gather_rows(cotangent).reshape(seqs * group_rows, width)
    down_grad = jnp.einsum("tf,td->fd", hidden, grad_rows, preferred_element_type=jnp.float32)
    grad_hidden = jnp.einsum(
        "td,fd->tf", grad_rows, down_weight, preferred_element_type=jnp.float32
    )
    grad_gate = (
        grad_hidden * up_act * sigmoid_gate * (1.0 + gate_act * (1.0 - sigmoid_gate))
    ).astype(jnp.bfloat16)
    grad_up = (grad_hidden * silu_gate).astype(jnp.bfloat16)
    gate_grad = jnp.einsum("td,tf->df", rows_two, grad_gate, preferred_element_type=jnp.float32)
    up_grad = jnp.einsum("td,tf->df", rows_two, grad_up, preferred_element_type=jnp.float32)
    grad_normed_two = jnp.einsum(
        "tf,df->td", grad_gate, gate_weight, preferred_element_type=jnp.float32
    ) + jnp.einsum("tf,df->td", grad_up, up_weight, preferred_element_type=jnp.float32)
    grad_normed_two = reduce_rows(grad_normed_two.reshape(seqs, group_rows, width))
    grad_source_two, grad_gain_two = norm_backward(grad_normed_two, unit_two, factor_two, gain_two)
    grad_middle = cotangent.astype(jnp.float32) + grad_source_two
    grad_branch = gather_rows(grad_middle.astype(jnp.bfloat16)).reshape(seqs * group_rows, width)
    out_grad = jnp.einsum("tc,td->cd", mixed, grad_branch, preferred_element_type=jnp.float32)
    grad_mixed = (
        jnp.einsum("td,cd->tc", grad_branch, out_weight, preferred_element_type=jnp.float32)
        .astype(jnp.bfloat16)
        .reshape(seqs, group_rows, -1)
    )
    grad_blocks = to_blocks(grad_mixed, kv_heads)
    grad_query_blocks, grad_key_blocks, grad_value_blocks = lax.map(
        full_block,
        (query_blocks, grad_blocks, lse_blocks, query_places, key_blocks, value_blocks, key_places),
    )
    key_terms = jnp.concatenate(
        [
            from_blocks(grad_key_blocks[:, None], seqs),
            from_blocks(grad_value_blocks[:, None], seqs),
        ],
        axis=-1,
    )
    key_sums = lax.psum_scatter(
        key_terms.astype(jnp.bfloat16), "ctx", scatter_dimension=1, tiled=True
    ).astype(jnp.float32)
    half_width = key_sums.shape[-1] // 2
    grad_keys = key_sums[..., :half_width]
    grad_values = key_sums[..., half_width:]
    grad_query_rot = from_blocks(grad_query_blocks, seqs).reshape(seqs, group_rows, -1, HD)
    grad_query_raw, grad_q_part = norm_backward(
        rotate_back(grad_query_rot, cosine, sine_table), query_unit, query_factor, query_gain
    )
    grad_query_raw = grad_query_raw.astype(jnp.bfloat16).reshape(seqs * group_rows, -1)
    grad_key_rot = grad_keys.reshape(seqs, group_rows, kv_heads, HD)
    grad_key_raw, grad_k_part = norm_backward(
        rotate_back(grad_key_rot, cosine, sine_table), key_unit, key_factor, key_gain
    )
    grad_key_raw = grad_key_raw.astype(jnp.bfloat16).reshape(seqs * group_rows, -1)
    grad_value_raw = grad_values.astype(jnp.bfloat16).reshape(seqs * group_rows, -1)
    query_grad = jnp.einsum(
        "td,tc->dc", flat_one, grad_query_raw, preferred_element_type=jnp.float32
    )
    key_grad = jnp.einsum("td,tc->dc", flat_one, grad_key_raw, preferred_element_type=jnp.float32)
    value_grad = jnp.einsum(
        "td,tc->dc", flat_one, grad_value_raw, preferred_element_type=jnp.float32
    )
    grad_normed_one = jnp.einsum(
        "tc,dc->td", grad_query_raw, query_weight, preferred_element_type=jnp.float32
    )
    grad_normed_one = grad_normed_one + jnp.einsum(
        "tc,dc->td", grad_key_raw, key_weight, preferred_element_type=jnp.float32
    )
    grad_normed_one = grad_normed_one + jnp.einsum(
        "tc,dc->td", grad_value_raw, value_weight, preferred_element_type=jnp.float32
    )
    grad_normed_one = reduce_rows(grad_normed_one.reshape(seqs, group_rows, width))
    grad_source_one, grad_gain_one = norm_backward(grad_normed_one, unit_one, factor_one, gain_one)
    grad_tokens = grad_middle + grad_source_one
    weight_grads = (
        lax.psum_scatter(query_grad, ("dp", "ctx"), scatter_dimension=0, tiled=True),
        lax.psum_scatter(key_grad, ("dp", "ctx"), scatter_dimension=0, tiled=True),
        lax.psum_scatter(value_grad, ("dp", "ctx"), scatter_dimension=0, tiled=True),
        lax.psum_scatter(out_grad, ("dp", "ctx"), scatter_dimension=1, tiled=True),
        lax.psum_scatter(gate_grad, ("dp", "ctx"), scatter_dimension=0, tiled=True),
        lax.psum_scatter(up_grad, ("dp", "ctx"), scatter_dimension=0, tiled=True),
        lax.psum_scatter(down_grad, ("dp", "ctx"), scatter_dimension=1, tiled=True),
    )
    gain_grads = lax.psum(
        (grad_gain_one, grad_q_part, grad_k_part, grad_gain_two), ("dp", "ctx", "tensor")
    )
    return (
        layer_out,
        grad_tokens,
        gain_grads[0],
        weight_grads[0],
        weight_grads[1],
        weight_grads[2],
        gain_grads[1],
        gain_grads[2],
        weight_grads[3],
        gain_grads[3],
        weight_grads[4],
        weight_grads[5],
        weight_grads[6],
    )


NT = (((1,), (1,)), ((), ()))
TN = (((0,), (0,)), ((), ()))
NN = (((1,), (0,)), ((), ()))
SCALE = HD ** (-0.5)
GAIN_ROWS = 16
VMEM_LIMIT = 44 * 1024 * 1024
COSTS = {}
TIES = {'m_w': ['m_w1'], 'a_w': ['a_w1'], 'pb': ['a_w', 'm_z1'], 'm_x': ['branch'], 'm_z1': ['branch'], 'f_y': ['m_y', 'one_y'], 'a_x2': ['pb', 'gain_x'], 'a_z1': ['gain_x']}


def dot(left, right, dims=NN):
    return lax.dot_general(left, right, dims, preferred_element_type=jnp.float32)


def shape_of(shape, dtype):
    return jax.ShapeDtypeStruct(shape, dtype)


def call(name, kernel, grid, words, inputs, outputs, scratch, flops):

    def spec(block, index):
        if index is None:
            return pl.BlockSpec(block, lambda *ids: (0,) * len(block))
        return pl.BlockSpec(block, index)

    return pl.pallas_call(
        kernel,
        grid_spec=pltpu.PrefetchScalarGridSpec(
            num_scalar_prefetch=1,
            grid=(grid,),
            in_specs=[spec(block, index) for _, block, index in inputs],
            out_specs=[spec(block, index) for _, _, block, index in outputs],
            scratch_shapes=scratch,
        ),
        out_shape=[shape_of(shape, dtype) for shape, dtype, _, _ in outputs],
        compiler_params=pltpu.CompilerParams(vmem_limit_bytes=VMEM_LIMIT),
        cost_estimate=pl.CostEstimate(flops=int(COSTS.get(name, 0) * flops), bytes_accessed=0, transcendentals=0),
    )(words, *[array for array, _, _ in inputs])


def whole(array):
    return (array, array.shape, None)


def sort_runs(block_of, run, *pairs):
    for index in range(4):
        source = pl.multiple_of(block_of[index] * run, run)
        for target, origin in pairs:
            target[pl.ds(index * run, run), :] = origin[pl.ds(source, run), :]


def turn(source):
    return pltpu.roll(source, HD // 2, 1)


def unit_of(raw):
    factor = lax.rsqrt(jnp.mean(raw * raw, axis=-1, keepdims=True) + EPSILON)
    return (raw * factor, factor)


def raw_scores(keys, query, visible, run):
    scores = dot(keys, query, NT) * SCALE
    count = scores.shape[0]
    last = jnp.where(visible, scores[count - run :], NEGATIVE)
    if count == run:
        return last
    return jnp.concatenate([scores[: count - run], last], axis=0)


def place_all(member, groups, refs, target, columns=slice(None), depth=None):
    for indices, ref in zip(groups, refs):
        for place, index in enumerate(indices):
            value = ref[place] if depth is None else ref[place, :depth]
            size = value.shape[0]
            start = pl.multiple_of((member ^ index) * size, size)
            target[pl.ds(start, size), columns] = value


def pick(first_ref, second_ref):
    half = pl.num_programs(0) // 2
    return jnp.where(pl.program_id(0) < half, first_ref[...], second_ref[...])


def project_kernel(groups, member_ref, xa_ref, xb_ref, cos_ref, sin_ref, *refs):
    pieces, rest = refs[:-7], refs[-7:]
    normed_ref, q_ref, k_ref, v_ref, raw_ref, weight_ref, gains_ref = rest
    depth = pieces[0].shape[1] - GAIN_ROWS

    @pl.when(pl.program_id(0) == 0)
    def _():
        place_all(member_ref[0], groups, pieces, weight_ref, depth=depth)
        gains = jnp.zeros(gains_ref.shape, jnp.float32)
        for piece in pieces:
            for place in range(piece.shape[0]):
                gains += piece[place, depth:].astype(jnp.float32)
        gains_ref[...] = gains

    unit, _ = unit_of(pick(xa_ref, xb_ref).astype(jnp.float32))
    normed = (unit * gains_ref[0:1, :]).astype(jnp.bfloat16)
    normed_ref[...] = normed
    product = dot(normed, weight_ref[...])
    raw_width = raw_ref.shape[1]
    raw_ref[...] = product[:, :raw_width]
    v_ref[...] = product[:, raw_width:].astype(jnp.bfloat16)
    cosine = cos_ref[...]
    sine = sin_ref[...]
    q_heads = q_ref.shape[1] // HD
    for head in range(raw_width // HD):
        unit, _ = unit_of(product[:, head * HD : (head + 1) * HD])
        target, place, row = (q_ref, head, 2) if head < q_heads else (k_ref, head - q_heads, 3)
        normed = unit * gains_ref[row : row + 1, :HD]
        rotated = normed * cosine + turn(normed) * sine
        target[:, place * HD : (place + 1) * HD] = rotated.astype(jnp.bfloat16)


def project(member, x_first, x_second, groups, pieces, cosine, sine, q_width, k_width):
    rows = cosine.shape[0]
    width = x_first.shape[1]
    block = rows // 4
    total = q_width + 2 * k_width
    bf16, f32 = jnp.bfloat16, jnp.float32

    def by_rows(i, member):
        return (i, 0)

    return call(
        "P",
        functools.partial(project_kernel, groups),
        4,
        member,
        [
            (x_first, (block, width), first_half),
            (x_second, (block, width), second_half),
            (cosine, (block, HD), by_rows),
            (sine, (block, HD), by_rows),
        ]
        + [whole(piece) for piece in pieces],
        [
            ((rows, width), bf16, (block, width), by_rows),
            ((rows, q_width), bf16, (block, q_width), by_rows),
            ((rows, k_width), bf16, (block, k_width), by_rows),
            ((rows, k_width), bf16, (block, k_width), by_rows),
            ((rows, q_width + k_width), f32, (block, q_width + k_width), by_rows),
            ((width, total), bf16, (width, total), None),
            ((GAIN_ROWS, width), f32, (GAIN_ROWS, width), None),
        ],
        [],
        2 * rows * width * total,
    )


def forward_kernel(
    block_of, q_ref, k_ref, v_ref, column_ref, row_ref, mixed_ref, lse_ref, keys, values, columns
):
    run = q_ref.shape[0] // 4
    sort_runs(block_of, run, (keys, k_ref), (values, v_ref), (columns, column_ref))
    for index in range(4):
        count = run * (index + 1)
        rows = pl.ds(pl.multiple_of(block_of[index] * run, run), run)
        visible = columns[pl.ds(count - run, run), :] <= row_ref[:, rows]
        for head in range(q_ref.shape[1] // HD):
            lanes = pl.ds(head * HD, HD)
            scores = raw_scores(keys[:count], q_ref[rows, lanes], visible, run)
            row_max = jnp.max(scores, axis=0, keepdims=True)
            raised = jnp.exp(scores - row_max)
            row_total = jnp.sum(raised, axis=0, keepdims=True)
            probs = (raised * (1.0 / row_total)).astype(jnp.bfloat16)
            mixed_ref[rows, lanes] = dot(probs, values[:count], TN).astype(jnp.bfloat16)
            lse_ref[pl.ds(head, 1), rows] = row_max + jnp.log(row_total)


def by_group(group, order):
    return (0, group)


def by_lead(group, order):
    return (group, 0, 0)


def attend(block_of, queries, keys, values, column, row):
    rows, width = keys.shape
    groups = width // HD
    pair = queries.shape[1] // groups
    return call(
        "attn",
        forward_kernel,
        groups,
        block_of,
        [
            (queries, (rows, pair), by_group),
            (keys, (rows, HD), by_group),
            (values, (rows, HD), by_group),
            whole(column),
            whole(row),
        ],
        [
            (queries.shape, jnp.bfloat16, (rows, pair), by_group),
            ((groups, pair // HD, rows), jnp.float32, (None, pair // HD, rows), by_lead),
        ],
        [
            pltpu.VMEM((rows, HD), jnp.bfloat16),
            pltpu.VMEM((rows, HD), jnp.bfloat16),
            pltpu.VMEM((rows, 1), jnp.int32),
        ],
        3 * rows * rows * queries.shape[1],
    )


def first_half(i, member):
    return (jnp.minimum(i, 1), 0)


def second_half(i, member):
    return (jnp.maximum(i - 2, 0), 0)


def store_halves(product, kept_ref, sent_ref):
    half = pl.num_programs(0) // 2

    @pl.when(pl.program_id(0) < half)
    def _():
        kept_ref[...] = product

    @pl.when(pl.program_id(0) >= half)
    def _():
        sent_ref[...] = product.astype(jnp.bfloat16)


def halves_out(rows, block, width):
    return [
        ((rows // 2, width), jnp.float32, (block, width), first_half),
        ((rows // 2, width), jnp.bfloat16, (block, width), second_half),
    ]


def out_kernel(groups, member_ref, mixed_ref, *refs):
    pieces, (kept_ref, sent_ref, weight_ref) = refs[:-3], refs[-3:]

    @pl.when(pl.program_id(0) == 0)
    def _():
        place_all(member_ref[0], groups, pieces, weight_ref)

    store_halves(dot(mixed_ref[...], weight_ref[...], NT), kept_ref, sent_ref)


def project_out(member, mixed, groups, pieces):
    rows, depth = mixed.shape
    block = rows // 4
    width = pieces[0].shape[1] * sum(piece.shape[0] for piece in pieces)
    return call(
        "out",
        functools.partial(out_kernel, groups),
        4,
        member,
        [(mixed, (block, depth), lambda i, member: (i, 0))] + [whole(piece) for piece in pieces],
        halves_out(rows, block, width)
        + [((width, depth), jnp.bfloat16, (width, depth), None)],
        [],
        2 * rows * width * depth,
    )


def back_kernel(starts, member_ref, xa_ref, xb_ref, *refs):
    grad_refs, (weight_ref, kept_ref, sent_ref, gain_ref) = refs[:-4], refs[-4:]
    product = None
    for start, grad_ref in zip(starts, grad_refs):
        term = dot(grad_ref[...], weight_ref[:, start : start + grad_ref.shape[1]], NT)
        product = term if product is None else product + term
    unit, _ = unit_of(pick(xa_ref, xb_ref).astype(jnp.float32))

    @pl.when(pl.program_id(0) == 0)
    def _():
        gain_ref[...] = jnp.zeros_like(gain_ref)

    gain_ref[...] += jnp.sum(product * unit, axis=0, keepdims=True)
    store_halves(product, kept_ref, sent_ref)


def project_back(member, x_first, x_second, starts, grads, weight):
    rows = grads[0].shape[0]
    block = rows // 4
    width, total = weight.shape
    return call(
        "pb",
        functools.partial(back_kernel, starts),
        4,
        member,
        [
            (x_first, (block, width), first_half),
            (x_second, (block, width), second_half),
        ]
        + [(grad, (block, grad.shape[1]), lambda i, member: (i, 0)) for grad in grads]
        + [whole(weight)],
        halves_out(rows, block, width) + [((1, width), jnp.float32, (1, width), None)],
        [],
        2 * rows * width * total,
    )


def mlp_kernel(member_ref, xa_ref, xb_ref, ga_ref, gb_ref, gate_up, down_ref, *rest):
    bf16 = jnp.bfloat16
    hidden_ref, grad_ref, kept_ref, sent_ref = rest
    width = down_ref.shape[1]
    x = pick(xa_ref, xb_ref)
    product = dot(x, gate_up[...])
    grad_hidden = dot(pick(ga_ref, gb_ref), down_ref[...])
    gate = product[:, :width]
    up = product[:, width:]
    sigmoid = jax.nn.sigmoid(gate)
    silu = gate * sigmoid
    hidden_ref[...] = (silu * up).astype(bf16)
    grad_gate = (grad_hidden * up * sigmoid * (1.0 + gate * (1.0 - sigmoid))).astype(bf16)
    grad_up = (grad_hidden * silu).astype(bf16)
    grad_ref[:, :width] = grad_gate
    grad_ref[:, width:] = grad_up
    grad_x = dot(grad_gate, gate_up[:, :width], NT) + dot(grad_up, gate_up[:, width:], NT)
    store_halves(grad_x, kept_ref, sent_ref)


def third_quarter(i, member):
    return (2 + jnp.minimum(i, 1), 0)


def fourth_quarter(i, member):
    return (jnp.maximum(i, 2), 0)


def feed(member, x_first, x_second, own_half, core_half, weight):
    rows, width = own_half.shape
    hidden_width = weight.shape[1] // 3
    block = rows // 4
    bf16 = jnp.bfloat16

    def by_rows(i, member):
        return (i, 0)

    return call(
        "mlp",
        mlp_kernel,
        4,
        member,
        [
            (x_first, (block, width), first_half),
            (x_second, (block, width), second_half),
            (own_half, (block, width), third_quarter),
            (core_half, (block, width), fourth_quarter),
            (weight, (width, 2 * hidden_width), lambda i, member: (0, 0)),
            (weight, (width, hidden_width), lambda i, member: (0, 2)),
        ],
        [
            ((rows, hidden_width), bf16, (block, hidden_width), by_rows),
            ((rows, 2 * hidden_width), bf16, (block, 2 * hidden_width), by_rows),
        ]
        + halves_out(rows, block, width),
        [],
        10 * rows * width * hidden_width,
    )


def mlp_out_kernel(member_ref, hidden_ref, weight_ref, kept_ref, sent_ref):
    store_halves(dot(hidden_ref[...], weight_ref[...], NT), kept_ref, sent_ref)


def feed_out(member, hidden, weight):
    rows, depth = hidden.shape
    width = weight.shape[0]
    block = rows // 4
    return call(
        "mo",
        mlp_out_kernel,
        4,
        member,
        [
            (hidden, (block, depth), lambda i, member: (i, 0)),
            (weight, (width, depth), lambda i, member: (0, 2)),
        ],
        halves_out(rows, block, width),
        [],
        2 * rows * width * depth,
    )


def weight_grad_kernel(layout, member_ref, *refs):
    inputs, (kept_ref, sent_ref, product) = refs[:-3], refs[-3:]
    half = product.shape[0] // 2
    start = place = 0
    for lefts, rights in layout:
        left_refs = inputs[place : place + lefts]
        right_refs = inputs[place + lefts : place + lefts + rights]
        place += lefts + rights
        for right_ref in right_refs:
            stop = start + right_ref.shape[1]
            total = None
            row = 0
            for left_ref in left_refs:
                count = left_ref.shape[0]
                term = dot(left_ref[...], right_ref[row : row + count, :], TN)
                total = term if total is None else total + term
                row += count
            product[:, start:stop] = total.astype(jnp.bfloat16)
            start = stop
    near = member_ref[0] % 2
    kept_ref[...] = product[pl.ds(pl.multiple_of(near * half, half), half), :]
    sent_ref[...] = product[pl.ds(pl.multiple_of((1 - near) * half, half), half), :]


def weight_grad(member, dp_size, parts, upper):
    width = parts[0][0][0].shape[1]
    pairs = dp_size // 2
    half = width // dp_size
    bits = pairs.bit_length() - 1
    inputs = []
    layout = []
    total = flops = 0

    def by_member(quarter, i, member):
        i = i + upper * (pairs // 2)
        turned = sum(((i >> bit) & 1) << (bits - 1 - bit) for bit in range(bits))
        return (quarter, (member[0] // 2) ^ turned)

    for lefts, quarter, rights in parts:
        rows = rights[0].shape[0]
        for left in lefts:
            index = functools.partial(by_member, quarter)
            inputs.append((left, (rows // len(lefts), 2 * half), index))
        inputs += [whole(right) for right in rights]
        layout.append((len(lefts), len(rights)))
        columns = sum(right.shape[1] for right in rights)
        total += columns
        flops += 2 * rows * width * columns
    result = (
        (pairs // 2, half, total),
        jnp.bfloat16,
        (None, half, total),
        lambda i, member: (i, 0, 0),
    )
    return call(
        "wg",
        functools.partial(weight_grad_kernel, layout),
        pairs // 2,
        member,
        inputs,
        [result, result],
        [pltpu.VMEM((2 * half, total), jnp.bfloat16)],
        flops,
    )


def norm_rope_back(grad, raw, cosine, sine, gain):
    grad_normed = grad * cosine - turn(grad) * sine
    unit, factor = unit_of(raw)
    gain_part = jnp.sum(grad_normed * unit, axis=0, keepdims=True)
    grad_unit = grad_normed * gain
    projected = jnp.mean(grad_unit * unit, axis=-1, keepdims=True)
    return ((factor * (grad_unit - unit * projected)).astype(jnp.bfloat16), gain_part)


def backward_kernel(
    block_of,
    q_ref,
    k_ref,
    v_ref,
    branch_a_ref,
    branch_b_ref,
    out_weight_ref,
    lse_ref,
    column_ref,
    row_ref,
    raw_q_ref,
    raw_k_ref,
    cos_ref,
    sin_ref,
    gains_ref,
    dq_ref,
    dk_ref,
    dv_ref,
    q_part_ref,
    k_part_ref,
    keys,
    values,
    columns,
    key_sum,
    value_sum,
    grad_mixed,
):
    run = q_ref.shape[0] // 4
    sort_runs(block_of, run, (keys, k_ref), (values, v_ref), (columns, column_ref))
    key_sum[...] = jnp.zeros_like(key_sum)
    value_sum[...] = jnp.zeros_like(value_sum)
    half = branch_a_ref.shape[0]
    grad_mixed[:half, :] = dot(branch_a_ref[...], out_weight_ref[...]).astype(jnp.bfloat16)
    grad_mixed[half:, :] = dot(branch_b_ref[...], out_weight_ref[...]).astype(jnp.bfloat16)
    q_part = jnp.zeros((1, HD), jnp.float32)
    k_part = jnp.zeros((1, HD), jnp.float32)
    q_gain = gains_ref[2:3, :HD]
    k_gain = gains_ref[3:4, :HD]
    for index in range(4):
        count = run * (index + 1)
        rows = pl.ds(pl.multiple_of(block_of[index] * run, run), run)
        visible = columns[pl.ds(count - run, run), :] <= row_ref[:, rows]
        for head in range(q_ref.shape[1] // HD):
            lanes = pl.ds(head * HD, HD)
            query = q_ref[rows, lanes]
            grad = grad_mixed[rows, lanes]
            scores = raw_scores(keys[:count], query, visible, run)
            probs = jnp.exp(scores - lse_ref[pl.ds(head, 1), rows])
            grad_probs = dot(values[:count], grad, NT)
            delta = jnp.sum(probs * grad_probs, axis=0, keepdims=True)
            grad_scores = (probs * (grad_probs - delta)).astype(jnp.bfloat16)
            value_sum[:count, :] += dot(probs.astype(jnp.bfloat16), grad)
            key_sum[:count, :] += dot(grad_scores, query)
            grad_query = dot(grad_scores, keys[:count], TN) * SCALE
            dq_ref[rows, lanes], part = norm_rope_back(
                grad_query, raw_q_ref[rows, lanes], cos_ref[rows, :], sin_ref[rows, :], q_gain
            )
            q_part += part
    for index in range(4):
        rows = pl.ds(pl.multiple_of(block_of[index] * run, run), run)
        sorted_rows = pl.ds(index * run, run)
        dk_ref[rows, :], part = norm_rope_back(
            key_sum[sorted_rows, :] * SCALE,
            raw_k_ref[rows, :],
            cos_ref[rows, :],
            sin_ref[rows, :],
            k_gain,
        )
        k_part += part
        dv_ref[rows, :] = value_sum[sorted_rows, :].astype(jnp.bfloat16)
    q_part_ref[...] = q_part
    k_part_ref[...] = k_part


def attend_back(
    group, block_of, queries, keys, values, branches, out_weight, lse, column, row, raw, cosine, sine, gains
):
    rows, width = keys.shape
    groups = width // HD
    pair = queries.shape[1] // groups
    first_key = queries.shape[1] // HD
    depth = out_weight.shape[0]
    bf16, f32 = jnp.bfloat16, jnp.float32
    part = ((1, HD), f32, (1, HD), None)

    def this_group(i, order):
        return (0, group)

    return call(
        "ab",
        backward_kernel,
        1,
        block_of,
        [
            (queries, (rows, pair), this_group),
            (keys, (rows, HD), this_group),
            (values, (rows, HD), this_group),
            whole(branches[0]),
            whole(branches[1]),
            (out_weight, (depth, pair), this_group),
            (lse, (None, pair // HD, rows), lambda i, order: (group, 0, 0)),
            whole(column),
            whole(row),
            (raw, (rows, pair), this_group),
            (raw, (rows, HD), lambda i, order: (0, first_key + group)),
            whole(cosine),
            whole(sine),
            whole(gains),
        ],
        [
            ((rows, pair), bf16, (rows, pair), None),
            ((rows, HD), bf16, (rows, HD), None),
            ((rows, HD), bf16, (rows, HD), None),
            part,
            part,
        ],
        [
            pltpu.VMEM((rows, HD), bf16),
            pltpu.VMEM((rows, HD), bf16),
            pltpu.VMEM((rows, 1), jnp.int32),
            pltpu.VMEM((rows, HD), f32),
            pltpu.VMEM((rows, HD), f32),
            pltpu.VMEM((rows, pair), bf16),
        ],
        3 * rows * rows * queries.shape[1],
    )


def finish_kernel(starts, side_ref, kept_ref, other_ref, *outputs):
    first = side_ref[0] == 0
    for start, target in zip(starts, outputs):
        width = target.shape[1] // 2
        kept = kept_ref[:, start : start + width]
        other = other_ref[: kept_ref.shape[0], start : start + width].astype(jnp.float32)
        target[:, :width] = jnp.where(first, kept, other)
        target[:, width:] = jnp.where(first, other, kept)


def finish(side, kept, other, columns):
    rows = kept.shape[0]
    return call(
        "fin",
        functools.partial(finish_kernel, [start for start, _ in columns]),
        1,
        side,
        [whole(kept), whole(other)],
        [
            ((rows, 2 * width), jnp.float32, (rows, 2 * width), None)
            for _, width in columns
        ],
        [],
        0,
    )


def swap(source, axis, size, bit=1):
    return lax.ppermute(source, axis, [(i, i ^ bit) for i in range(size)])


def after(source, *events):
    return lax.optimization_barrier((source, events))[0]


def group_body(
    dp_size,
    tokens,
    places,
    attn_gain,
    w_query,
    w_key,
    w_value,
    q_gain,
    k_gain,
    w_out,
    mlp_gain,
    w_gate,
    w_up,
    w_down,
    cotangent,
):
    bf16, f32 = jnp.bfloat16, jnp.float32
    run, width = tokens.shape[1:]
    side = lax.axis_index("ctx")
    core = lax.axis_index("tensor")
    member = lax.axis_index("dp")
    word = member[None]
    q_width = w_query.shape[1] // 2
    k_width = w_key.shape[1] // 2
    hidden_width = w_gate.shape[1] // 2
    z_bits = [1 << bit for bit in range(1, dp_size.bit_length() - 1)]
    near_steps = list(range(2, dp_size, 2))
    groups = [[0], near_steps, [1], [step ^ 1 for step in near_steps]]

    def over_core(source):
        return swap(source, "tensor", 2)

    def over_ctx(source):
        return swap(source, "ctx", 2)

    def over_dp(source, bit):
        return swap(source, "dp", dp_size, bit)

    def over_z(shard):
        return [over_dp(shard, step) for step in near_steps]

    def mine(source, axis):
        size = source.shape[axis] // 2
        return lax.dynamic_slice_in_dim(source, side * size, size, axis).astype(bf16)

    def as_rows(values, columns):
        high = values.astype(bf16)
        low = (values - high.astype(f32)).astype(bf16)
        digits = jnp.concatenate([high, low])
        return jnp.pad(digits, (0, GAIN_ROWS * columns - digits.shape[0])).reshape(GAIN_ROWS, columns)

    def from_rows(rows, count):
        digits = rows.reshape(-1).astype(f32)
        return digits[:count] + digits[count : 2 * count]

    gain_rows = jnp.zeros((GAIN_ROWS, width), bf16)
    for row, gain in enumerate((attn_gain, mlp_gain, q_gain, k_gain)):
        gain_rows = lax.dynamic_update_slice(
            gain_rows, gain.astype(bf16)[None], (row, member * gain.shape[0])
        )
    qkv_shard = jnp.concatenate([mine(w_query, 1), mine(w_key, 1), mine(w_value, 1)], axis=1)
    qkv_shard = jnp.concatenate([qkv_shard, gain_rows], axis=0)
    out_shard = mine(w_out, 0).T
    mlp_shard = jnp.concatenate([mine(w_gate, 1), mine(w_up, 1), mine(w_down, 0).T], axis=1)

    place_count = places.shape[1]
    digits = jnp.zeros((GAIN_ROWS, width), bf16)
    for row, digit in enumerate((places // 128, places % 128)):
        digits = lax.dynamic_update_slice(digits, digit.astype(bf16), (row, 0))
    message = jnp.concatenate([tokens[0], cotangent[0], digits], axis=0)
    events = {}

    def tied(name, source):
        names = [other for other in TIES.get(name, ()) if other in events]
        return after(source, *[events[other] for other in names]) if names else source

    def told(name, raw):
        events[name] = raw
        return raw

    qkv_near, qkv_far, message = lax.optimization_barrier(
        (over_z(qkv_shard), over_dp(qkv_shard, 1), over_ctx(message))
    )
    told("s0", message)
    qkv_near = jnp.stack(qkv_near)
    own_half = jnp.concatenate(
        [tokens[0], message[:run], cotangent[0], message[run : 2 * run]], axis=0
    )
    core_half = told("tok", over_core(tied("tok", own_half)))
    qkv_far_rest = told("a_x", over_dp(tied("a_x", qkv_near), 1))
    mlp_weight = lax.all_gather(
        after(tied("ag", mlp_shard), qkv_near), "dp", axis=0, tiled=True
    )
    out_near = told("o_z", over_z(after(tied("o_z", out_shard), qkv_near)))
    half = 2 * run
    digits = message[2 * run : 2 * run + 2, :place_count].astype(jnp.int32)
    other_places = (digits[0] * 128 + digits[1]).reshape(2, run)
    own_places = places[0].reshape(2, run)
    place_blocks = jnp.stack([own_places, other_places], axis=1)
    place_blocks = jnp.where(core == 0, place_blocks, place_blocks[::-1]).reshape(-1)
    place_column = place_blocks[:, None]
    place_row = place_blocks[None, :]
    home_side = jnp.array([0, 1, 1, 0], jnp.int32)
    home_core = jnp.array([0, 0, 1, 1], jnp.int32)
    block_of = (home_core ^ core) * 2 + (home_side ^ side)
    cosine, sine_table = (table[:, 0] for table in rope_tables(place_blocks))
    sine_table = sine_table * jnp.where(jnp.arange(HD) < HD // 2, -1.0, 1.0).astype(f32)
    own_half, core_half, cosine, sine_table, place_column, block_of = lax.optimization_barrier(
        (own_half, core_half, cosine, sine_table, place_column, block_of)
    )
    normed_one, queries, key_rows, value_rows, raw, qkv_weight, gains = project(
        word,
        tied("P", own_half),
        core_half,
        groups,
        [qkv_shard[None], qkv_near, qkv_far[None], qkv_far_rest],
        cosine,
        sine_table,
        q_width,
        k_width,
    )
    told("P", queries)
    out_near = jnp.stack([out_shard] + out_near)
    out_far = told("o_ax", over_dp(tied("o_ax", out_near), 1))
    mixed, lse_rows = attend(
        block_of, tied("attn", queries), key_rows, value_rows, place_column, place_row
    )
    told("attn", mixed)
    orders = [[0] + near_steps, [1] + [step ^ 1 for step in near_steps]]
    out_kept, out_sent, out_weight = project_out(
        word, tied("out", mixed), orders, [out_near, out_far]
    )

    def ctx_sum(name, summed):
        other = told(name, over_ctx(tied(name, summed.astype(bf16))))
        return summed + jnp.concatenate([other[run:], other[:run]], axis=0).astype(f32)

    source = own_half[:half].astype(f32)
    middle = source + ctx_sum("ar1", out_kept + over_core(out_sent).astype(f32))
    gain_two = gains[1]
    normed_two, unit_two, factor_two = norm_forward(middle, gain_two)
    normed_two = normed_two.astype(bf16)
    normed_other = over_core(normed_two)
    hidden, grad_gate_up, grad_kept, grad_sent = feed(
        word, tied("mlp", normed_two), normed_other, own_half, core_half, mlp_weight
    )

    def halves(block):
        size = block.shape[0] // 2
        kept = lax.dynamic_slice_in_dim(block, side * size, size, 0)
        sent = lax.dynamic_slice_in_dim(block, (1 - side) * size, size, 0)
        return kept, sent

    def summed(name, kept, sent, bit):
        received = told(name, over_dp(tied(name, sent.astype(bf16)), bit))
        return kept.astype(f32) + received.astype(f32)

    def summed_half(name, total, bit):
        count = total.shape[0] // 2
        return summed(name, total[:count], total[count:], bit)

    grad_other = told("mid_core", over_core(grad_sent))
    hidden, grad_gate_up, grad_other = lax.optimization_barrier((hidden, grad_gate_up, grad_other))
    grad_normed_two = grad_kept + grad_other.astype(f32)
    def m_grads(name, upper):
        pair = weight_grad(
            word,
            dp_size,
            [
                ([normed_two, normed_other], 0, [tied(name, grad_gate_up)]),
                ([own_half, core_half], 1, [hidden]),
            ],
            upper,
        )
        told(name, pair[1])
        return pair

    m_high = summed("m_x1", *m_grads("m_w1", 1), 1)
    m_pair = m_grads("m_w", 0)
    mlp_kept, mlp_sent = feed_out(word, tied("mo", hidden), mlp_weight)
    told("mo", mlp_sent)
    mlp_event = told("mo_core", over_core(tied("mo_core", mlp_sent)))
    grad_normed_two = ctx_sum("ar2", grad_normed_two)
    grad_source_two, _ = norm_backward(grad_normed_two, unit_two, factor_two, gain_two)
    grad_gain_two = jnp.sum(grad_normed_two[:run] * unit_two[:run], axis=0)
    grad_middle = own_half[half:].astype(f32) + grad_source_two
    branch = grad_middle.astype(bf16)
    branches = [branch, told("branch", over_core(tied("branch", branch)))]
    def back(name, group):
        result = attend_back(
            group,
            block_of,
            tied(name, queries),
            key_rows,
            value_rows,
            branches,
            out_weight,
            lse_rows,
            place_column,
            place_row,
            raw,
            cosine,
            sine_table,
            gains,
        )
        told(name, result[0])
        return result

    first_back = back("g0", 0)
    m_low = summed("m_x", *m_pair, 1)
    m_sum = summed("m_z1", m_low, m_high, z_bits[0])
    second_back = back("g1", 1)
    back_grads = [grads[part] for part in range(3) for grads in (first_back, second_back)]

    def a_grads(name, upper):
        pair = weight_grad(
            word,
            dp_size,
            [(branches, 0, [tied(name, mixed)]), ([normed_one], 0, back_grads)],
            upper,
        )
        told(name, pair[1])
        return pair

    a_high = summed("a_x1", *a_grads("a_w1", 1), 1)
    a_pair = a_grads("a_w", 0)
    m_sum = summed("m_z2", m_sum[0], m_sum[1], z_bits[1])
    q_half, k_half = q_width // 2, k_width // 2
    starts = [0, q_half, q_width, q_width + k_half, q_width + k_width, q_width + k_width + k_half]
    back_grads[0] = tied("pb", back_grads[0])
    one_kept, one_sent, grad_gain_one = project_back(
        word, own_half, core_half, starts, back_grads, qkv_weight
    )
    told("pb", one_sent)
    a_low = summed("a_x2", *a_pair, 1)
    one_event = told("one_core", over_core(tied("one_core", one_sent)))
    gain_grads = jnp.concatenate(
        [
            grad_gain_one[0],
            grad_gain_two,
            (first_back[3] + second_back[3])[0],
            (first_back[4] + second_back[4])[0],
        ]
    )
    gain_count = gain_grads.shape[0]
    gain_grads = gain_grads + told("gain_core", over_core(tied("gain_core", gain_grads)))
    gain_grads = gain_grads + told("gain_x", over_dp(tied("gain_x", gain_grads), 1))
    gain_grads = gain_grads + told("gain_z", over_dp(tied("gain_z", gain_grads), z_bits[0]))
    a_sum = summed("a_z1", a_low, a_high, z_bits[0])
    one_sum = one_kept + one_event.astype(f32)
    one_other = told("one_y", over_ctx(tied("one_y", one_sum[run:].astype(bf16))))
    grad_normed_one = one_sum[:run] + one_other.astype(f32)
    _, unit_one, factor_one = norm_forward(tokens[0].astype(f32), gains[0])
    grad_source_one, _ = norm_backward(grad_normed_one, unit_one, factor_one, gains[0])
    grad_tokens = grad_middle[:run] + grad_source_one

    mlp_part = tied("oth", mlp_kept) + mlp_event.astype(f32)
    other_part = told("oth", over_ctx(mlp_part[run:].astype(bf16)))
    layer_out = middle[:run] + mlp_part[:run] + other_part.astype(f32)

    def with_gains(blocks, gains):
        columns = blocks.shape[-1]
        return jnp.concatenate(
            [blocks.astype(bf16).reshape(-1, columns), as_rows(gains, columns)], axis=0
        )

    rows = a_sum.shape[1]
    mlp_kept, mlp_sent = halves(m_sum)
    mlp_other = told("m_y", over_ctx(tied("m_y", mlp_sent.astype(bf16))))
    received = told("a_z2", over_dp(tied("a_z2", with_gains(a_sum[1], gain_grads)), z_bits[1]))
    a_sum = a_sum[0] + received[:rows].astype(f32)
    gain_grads = gain_grads + from_rows(received[rows:], gain_count)
    attn_kept, attn_sent = halves(a_sum)
    received = over_ctx(tied("f_y", with_gains(attn_sent, gain_grads)))
    gain_grads = gain_grads + from_rows(received[rows // 2 :], gain_count)
    gate_grad, up_grad, down_grad = finish(
        side[None],
        mlp_kept,
        mlp_other,
        [(place * hidden_width, hidden_width) for place in range(3)],
    )
    out_grad, query_grad, key_grad, value_grad = finish(
        side[None],
        attn_kept,
        received,
        [
            (0, q_width),
            (q_width, q_width),
            (2 * q_width, k_width),
            (2 * q_width + k_width, k_width),
        ],
    )
    return (
        layer_out[None],
        grad_tokens[None],
        gain_grads[:width],
        query_grad,
        key_grad,
        value_grad,
        gain_grads[2 * width : 2 * width + HD],
        gain_grads[2 * width + HD :],
        out_grad.T,
        gain_grads[width : 2 * width],
        gate_grad,
        up_grad,
        down_grad.T,
    )


def plan(mesh):
    sizes = dict(mesh.shape)
    if sizes["ctx"] == 2 and sizes["tensor"] == 2 and sizes["dp"] == 8:
        return functools.partial(group_body, sizes["dp"])
    return split_body


def solution(mesh):
    in_specs = (
        P("dp", ("ctx", "tensor"), None),
        P("dp", "ctx"),
        P("dp"),
        P("dp", "tensor"),
        P("dp", "tensor"),
        P("dp", "tensor"),
        P("dp"),
        P("dp"),
        P("tensor", "dp"),
        P("dp"),
        P("dp", "tensor"),
        P("dp", "tensor"),
        P("tensor", "dp"),
        P("dp", ("ctx", "tensor"), None),
    )
    out_specs = (
        P("dp", ("ctx", "tensor"), None),
        P("dp", ("ctx", "tensor"), None),
        P(),
        P(("dp", "ctx"), "tensor"),
        P(("dp", "ctx"), "tensor"),
        P(("dp", "ctx"), "tensor"),
        P(),
        P(),
        P("tensor", ("dp", "ctx")),
        P(),
        P(("dp", "ctx"), "tensor"),
        P(("dp", "ctx"), "tensor"),
        P("tensor", ("dp", "ctx")),
    )
    return jax.shard_map(plan(mesh), mesh=mesh, in_specs=in_specs, out_specs=out_specs, check_vma=False)
```

```python
import functools

import jax
import jax.numpy as jnp
from jax import lax
from jax.experimental import pallas as pl
from jax.experimental.pallas import tpu as pltpu
from jax.sharding import PartitionSpec as P

HD = 128


EPSILON = 1e-06
ROPE_BASE = 1000000.0
NEGATIVE = -1e30


def gather_rows(source):
    return lax.all_gather(source, "tensor", axis=1, tiled=True)


def reduce_rows(partial_sum):
    return lax.psum_scatter(partial_sum, "tensor", scatter_dimension=1, tiled=True)


def norm_forward(source, gain):
    factor = lax.rsqrt(jnp.mean(source * source, axis=-1, keepdims=True) + EPSILON)
    unit = source * factor
    return (unit * gain, unit, factor)


def norm_backward(grad_normed, unit, factor, gain):
    grad_unit = grad_normed * gain
    grad_gain = jnp.sum((grad_normed * unit).reshape(-1, unit.shape[-1]), axis=0)
    grad_source = factor * (grad_unit - unit * jnp.mean(grad_unit * unit, axis=-1, keepdims=True))
    return (grad_source, grad_gain)


def rope_tables(positions):
    freq_index = jnp.arange(HD // 2, dtype=jnp.float32)
    inverse = ROPE_BASE ** (-2.0 * freq_index / HD)
    angles = positions.astype(jnp.float32)[..., None] * inverse
    cosine = jnp.concatenate([jnp.cos(angles), jnp.cos(angles)], axis=-1)
    sine_table = jnp.concatenate([jnp.sin(angles), jnp.sin(angles)], axis=-1)
    return (cosine[..., None, :], sine_table[..., None, :])


def rotate(source, cosine, sine_table):
    half_width = source.shape[-1] // 2
    turned = jnp.concatenate([-source[..., half_width:], source[..., :half_width]], axis=-1)
    return source * cosine + turned * sine_table


def rotate_back(grad_rotated, cosine, sine_table):
    half_width = grad_rotated.shape[-1] // 2
    sined = grad_rotated * sine_table
    turned = jnp.concatenate([sined[..., half_width:], -sined[..., :half_width]], axis=-1)
    return grad_rotated * cosine + turned


def to_blocks(heads_last, kv_heads):
    seqs, row_count, width = heads_last.shape
    group_size = width // (kv_heads * HD)
    shaped = heads_last.reshape(seqs, row_count, kv_heads, group_size, HD)
    return shaped.transpose(0, 2, 3, 1, 4).reshape(seqs * kv_heads, group_size, row_count, HD)


def from_blocks(blocked, seqs):
    count, group_size, row_count, width = blocked.shape
    kv_heads = count // seqs
    shaped = blocked.reshape(seqs, kv_heads, group_size, row_count, width)
    return shaped.transpose(0, 3, 1, 2, 4).reshape(seqs, row_count, kv_heads * group_size * width)


def masked_scores(queries, key_rows, query_places, key_places):
    scores = jnp.einsum(
        "hqd,kd->hqk", queries, key_rows, preferred_element_type=jnp.float32
    ) * HD ** (-0.5)
    visible = key_places[None, None, :] <= query_places[None, :, None]
    return jnp.where(visible, scores, NEGATIVE)


def recompute(queries, key_rows, lse_rows, query_places, key_places):
    return jnp.exp(masked_scores(queries, key_rows, query_places, key_places) - lse_rows[..., None])


def forward_block(pieces):
    queries, key_rows, value_rows, query_places, key_places = pieces
    scores = masked_scores(queries, key_rows, query_places, key_places)
    row_max = jnp.max(scores, axis=-1, keepdims=True)
    raised = jnp.exp(scores - row_max)
    row_total = jnp.sum(raised, axis=-1, keepdims=True)
    attn_probs = raised / row_total
    mixed = jnp.einsum(
        "hqk,kd->hqd",
        attn_probs.astype(jnp.bfloat16),
        value_rows,
        preferred_element_type=jnp.float32,
    )
    return (mixed, (row_max + jnp.log(row_total))[..., 0])


def full_block(pieces):
    queries, grad_mixed, lse_rows, query_places, key_rows, value_rows, key_places = pieces
    attn_probs = recompute(queries, key_rows, lse_rows, query_places, key_places)
    grad_probs = jnp.einsum(
        "hqd,kd->hqk", grad_mixed, value_rows, preferred_element_type=jnp.float32
    )
    row_delta = jnp.sum(attn_probs * grad_probs, axis=-1)
    grad_scores = (attn_probs * (grad_probs - row_delta[..., None])).astype(jnp.bfloat16)
    grad_queries = jnp.einsum(
        "hqk,kd->hqd", grad_scores, key_rows, preferred_element_type=jnp.float32
    ) * HD ** (-0.5)
    grad_keys = jnp.einsum(
        "hqk,hqd->kd", grad_scores, queries, preferred_element_type=jnp.float32
    ) * HD ** (-0.5)
    grad_values = jnp.einsum(
        "hqk,hqd->kd",
        attn_probs.astype(jnp.bfloat16),
        grad_mixed,
        preferred_element_type=jnp.float32,
    )
    return (grad_queries, grad_keys, grad_values)


def split_body(
    tokens,
    places,
    attn_gain,
    w_query,
    w_key,
    w_value,
    q_gain,
    k_gain,
    w_out,
    mlp_gain,
    w_gate,
    w_up,
    w_down,
    cotangent,
):
    seqs, local_rows, width = tokens.shape
    attn_set = (
        lax.all_gather(attn_gain.astype(jnp.bfloat16), "dp", axis=0, tiled=True),
        lax.all_gather(w_query.astype(jnp.bfloat16), "dp", axis=0, tiled=True),
        lax.all_gather(w_key.astype(jnp.bfloat16), "dp", axis=0, tiled=True),
        lax.all_gather(w_value.astype(jnp.bfloat16), "dp", axis=0, tiled=True),
        lax.all_gather(q_gain.astype(jnp.bfloat16), "dp", axis=0, tiled=True),
        lax.all_gather(k_gain.astype(jnp.bfloat16), "dp", axis=0, tiled=True),
        lax.all_gather(w_out.astype(jnp.bfloat16), "dp", axis=1, tiled=True),
    )
    gain_one, query_weight, key_weight, value_weight, query_gain, key_gain, out_weight = attn_set
    mlp_set = (
        lax.all_gather(mlp_gain.astype(jnp.bfloat16), "dp", axis=0, tiled=True),
        lax.all_gather(w_gate.astype(jnp.bfloat16), "dp", axis=0, tiled=True),
        lax.all_gather(w_up.astype(jnp.bfloat16), "dp", axis=0, tiled=True),
        lax.all_gather(w_down.astype(jnp.bfloat16), "dp", axis=1, tiled=True),
    )
    gain_two, gate_weight, up_weight, down_weight = mlp_set
    gain_one = gain_one.astype(jnp.float32)
    gain_two = gain_two.astype(jnp.float32)
    query_gain = query_gain.astype(jnp.float32)
    key_gain = key_gain.astype(jnp.float32)
    source = tokens.astype(jnp.float32)
    normed_one, unit_one, factor_one = norm_forward(source, gain_one)
    rows_one = gather_rows(normed_one.astype(jnp.bfloat16))
    group_rows = rows_one.shape[1]
    flat_one = rows_one.reshape(seqs * group_rows, width)
    query_raw = jnp.dot(flat_one, query_weight, preferred_element_type=jnp.float32).reshape(
        seqs, group_rows, -1, HD
    )
    key_raw = jnp.dot(flat_one, key_weight, preferred_element_type=jnp.float32).reshape(
        seqs, group_rows, -1, HD
    )
    value_rows = (
        jnp.dot(flat_one, value_weight, preferred_element_type=jnp.float32)
        .astype(jnp.bfloat16)
        .reshape(seqs, group_rows, -1)
    )
    kv_heads = key_raw.shape[2]
    cosine, sine_table = rope_tables(places)
    query_normed, query_unit, query_factor = norm_forward(query_raw, query_gain)
    queries = (
        rotate(query_normed, cosine, sine_table).astype(jnp.bfloat16).reshape(seqs, group_rows, -1)
    )
    key_normed, key_unit, key_factor = norm_forward(key_raw, key_gain)
    key_rows = (
        rotate(key_normed, cosine, sine_table).astype(jnp.bfloat16).reshape(seqs, group_rows, -1)
    )
    key_all, value_all, places_all = (
        lax.all_gather(key_rows, "ctx", axis=1, tiled=True),
        lax.all_gather(value_rows, "ctx", axis=1, tiled=True),
        lax.all_gather(places, "ctx", axis=1, tiled=True),
    )
    query_blocks = to_blocks(queries, kv_heads)
    key_blocks = to_blocks(key_all, kv_heads)[:, 0]
    value_blocks = to_blocks(value_all, kv_heads)[:, 0]
    query_places = jnp.repeat(places, kv_heads, axis=0)
    key_places = jnp.repeat(places_all, kv_heads, axis=0)
    mixed_blocks, lse_blocks = lax.map(
        forward_block, (query_blocks, key_blocks, value_blocks, query_places, key_places)
    )
    mixed = from_blocks(mixed_blocks, seqs).astype(jnp.bfloat16).reshape(seqs * group_rows, -1)
    attn_part = jnp.dot(mixed, out_weight, preferred_element_type=jnp.float32).reshape(
        seqs, group_rows, width
    )
    middle = source + reduce_rows(attn_part)
    normed_two, unit_two, factor_two = norm_forward(middle, gain_two)
    rows_two = gather_rows(normed_two.astype(jnp.bfloat16)).reshape(seqs * group_rows, width)
    gate_act = jnp.dot(rows_two, gate_weight, preferred_element_type=jnp.float32)
    up_act = jnp.dot(rows_two, up_weight, preferred_element_type=jnp.float32)
    sigmoid_gate = jax.nn.sigmoid(gate_act)
    silu_gate = gate_act * sigmoid_gate
    hidden = (silu_gate * up_act).astype(jnp.bfloat16)
    mlp_part = jnp.dot(hidden, down_weight, preferred_element_type=jnp.float32).reshape(
        seqs, group_rows, width
    )
    layer_out = middle + reduce_rows(mlp_part)
    grad_rows = gather_rows(cotangent).reshape(seqs * group_rows, width)
    down_grad = jnp.einsum("tf,td->fd", hidden, grad_rows, preferred_element_type=jnp.float32)
    grad_hidden = jnp.einsum(
        "td,fd->tf", grad_rows, down_weight, preferred_element_type=jnp.float32
    )
    grad_gate = (
        grad_hidden * up_act * sigmoid_gate * (1.0 + gate_act * (1.0 - sigmoid_gate))
    ).astype(jnp.bfloat16)
    grad_up = (grad_hidden * silu_gate).astype(jnp.bfloat16)
    gate_grad = jnp.einsum("td,tf->df", rows_two, grad_gate, preferred_element_type=jnp.float32)
    up_grad = jnp.einsum("td,tf->df", rows_two, grad_up, preferred_element_type=jnp.float32)
    grad_normed_two = jnp.einsum(
        "tf,df->td", grad_gate, gate_weight, preferred_element_type=jnp.float32
    ) + jnp.einsum("tf,df->td", grad_up, up_weight, preferred_element_type=jnp.float32)
    grad_normed_two = reduce_rows(grad_normed_two.reshape(seqs, group_rows, width))
    grad_source_two, grad_gain_two = norm_backward(grad_normed_two, unit_two, factor_two, gain_two)
    grad_middle = cotangent.astype(jnp.float32) + grad_source_two
    grad_branch = gather_rows(grad_middle.astype(jnp.bfloat16)).reshape(seqs * group_rows, width)
    out_grad = jnp.einsum("tc,td->cd", mixed, grad_branch, preferred_element_type=jnp.float32)
    grad_mixed = (
        jnp.einsum("td,cd->tc", grad_branch, out_weight, preferred_element_type=jnp.float32)
        .astype(jnp.bfloat16)
        .reshape(seqs, group_rows, -1)
    )
    grad_blocks = to_blocks(grad_mixed, kv_heads)
    grad_query_blocks, grad_key_blocks, grad_value_blocks = lax.map(
        full_block,
        (query_blocks, grad_blocks, lse_blocks, query_places, key_blocks, value_blocks, key_places),
    )
    key_terms = jnp.concatenate(
        [
            from_blocks(grad_key_blocks[:, None], seqs),
            from_blocks(grad_value_blocks[:, None], seqs),
        ],
        axis=-1,
    )
    key_sums = lax.psum_scatter(
        key_terms.astype(jnp.bfloat16), "ctx", scatter_dimension=1, tiled=True
    ).astype(jnp.float32)
    half_width = key_sums.shape[-1] // 2
    grad_keys = key_sums[..., :half_width]
    grad_values = key_sums[..., half_width:]
    grad_query_rot = from_blocks(grad_query_blocks, seqs).reshape(seqs, group_rows, -1, HD)
    grad_query_raw, grad_q_part = norm_backward(
        rotate_back(grad_query_rot, cosine, sine_table), query_unit, query_factor, query_gain
    )
    grad_query_raw = grad_query_raw.astype(jnp.bfloat16).reshape(seqs * group_rows, -1)
    grad_key_rot = grad_keys.reshape(seqs, group_rows, kv_heads, HD)
    grad_key_raw, grad_k_part = norm_backward(
        rotate_back(grad_key_rot, cosine, sine_table), key_unit, key_factor, key_gain
    )
    grad_key_raw = grad_key_raw.astype(jnp.bfloat16).reshape(seqs * group_rows, -1)
    grad_value_raw = grad_values.astype(jnp.bfloat16).reshape(seqs * group_rows, -1)
    query_grad = jnp.einsum(
        "td,tc->dc", flat_one, grad_query_raw, preferred_element_type=jnp.float32
    )
    key_grad = jnp.einsum("td,tc->dc", flat_one, grad_key_raw, preferred_element_type=jnp.float32)
    value_grad = jnp.einsum(
        "td,tc->dc", flat_one, grad_value_raw, preferred_element_type=jnp.float32
    )
    grad_normed_one = jnp.einsum(
        "tc,dc->td", grad_query_raw, query_weight, preferred_element_type=jnp.float32
    )
    grad_normed_one = grad_normed_one + jnp.einsum(
        "tc,dc->td", grad_key_raw, key_weight, preferred_element_type=jnp.float32
    )
    grad_normed_one = grad_normed_one + jnp.einsum(
        "tc,dc->td", grad_value_raw, value_weight, preferred_element_type=jnp.float32
    )
    grad_normed_one = reduce_rows(grad_normed_one.reshape(seqs, group_rows, width))
    grad_source_one, grad_gain_one = norm_backward(grad_normed_one, unit_one, factor_one, gain_one)
    grad_tokens = grad_middle + grad_source_one
    weight_grads = (
        lax.psum_scatter(query_grad, ("dp", "ctx"), scatter_dimension=0, tiled=True),
        lax.psum_scatter(key_grad, ("dp", "ctx"), scatter_dimension=0, tiled=True),
        lax.psum_scatter(value_grad, ("dp", "ctx"), scatter_dimension=0, tiled=True),
        lax.psum_scatter(out_grad, ("dp", "ctx"), scatter_dimension=1, tiled=True),
        lax.psum_scatter(gate_grad, ("dp", "ctx"), scatter_dimension=0, tiled=True),
        lax.psum_scatter(up_grad, ("dp", "ctx"), scatter_dimension=0, tiled=True),
        lax.psum_scatter(down_grad, ("dp", "ctx"), scatter_dimension=1, tiled=True),
    )
    gain_grads = lax.psum(
        (grad_gain_one, grad_q_part, grad_k_part, grad_gain_two), ("dp", "ctx", "tensor")
    )
    return (
        layer_out,
        grad_tokens,
        gain_grads[0],
        weight_grads[0],
        weight_grads[1],
        weight_grads[2],
        gain_grads[1],
        gain_grads[2],
        weight_grads[3],
        gain_grads[3],
        weight_grads[4],
        weight_grads[5],
        weight_grads[6],
    )


NT = (((1,), (1,)), ((), ()))
TN = (((0,), (0,)), ((), ()))
NN = (((1,), (0,)), ((), ()))
SCALE = HD ** (-0.5)
GAIN_ROWS = 16
GRANTS = {'ab': 24, 'mlp': 30, 'wg': 24, 'P': 24, 'attn': 24, 'out': 24, 'pb': 24, 'mo': 24, 'fin': 16}
COSTS = {}
TIES = {'m_w': ['m_w1'], 'a_w': ['a_w1'], 'pb': ['a_w', 'm_z1'], 'm_x': ['branch'], 'm_z1': ['branch'], 'f_y': ['m_y', 'one_y'], 'a_x2': ['pb', 'gain_x'], 'a_z1': ['gain_x'], 'lo': ['a_w']}


def dot(left, right, dims=NN):
    return lax.dot_general(left, right, dims, preferred_element_type=jnp.float32)


def shape_of(shape, dtype):
    return jax.ShapeDtypeStruct(shape, dtype)


def call(name, kernel, grid, words, inputs, outputs, scratch, flops):

    def spec(block, index):
        if index is None:
            return pl.BlockSpec(block, lambda *ids: (0,) * len(block))
        return pl.BlockSpec(block, index)

    return pl.pallas_call(
        kernel,
        grid_spec=pltpu.PrefetchScalarGridSpec(
            num_scalar_prefetch=1,
            grid=(grid,),
            in_specs=[spec(block, index) for _, block, index in inputs],
            out_specs=[spec(block, index) for _, _, block, index in outputs],
            scratch_shapes=scratch,
        ),
        out_shape=[shape_of(shape, dtype) for shape, dtype, _, _ in outputs],
        compiler_params=pltpu.CompilerParams(vmem_limit_bytes=GRANTS.get(name, 44) * 1024 * 1024),
        cost_estimate=pl.CostEstimate(flops=int(COSTS.get(name, 0) * flops), bytes_accessed=0, transcendentals=0),
    )(words, *[array for array, _, _ in inputs])


def whole(array):
    return (array, array.shape, None)


def sort_runs(block_of, run, *pairs):
    for index in range(4):
        source = pl.multiple_of(block_of[index] * run, run)
        for target, origin in pairs:
            target[pl.ds(index * run, run), :] = origin[pl.ds(source, run), :]


def turn(source):
    return pltpu.roll(source, HD // 2, 1)


def unit_of(raw):
    factor = lax.rsqrt(jnp.mean(raw * raw, axis=-1, keepdims=True) + EPSILON)
    return (raw * factor, factor)


def raw_scores(keys, query, visible, run):
    scores = dot(keys, query, NT) * SCALE
    count = scores.shape[0]
    last = jnp.where(visible, scores[count - run :], NEGATIVE)
    if count == run:
        return last
    return jnp.concatenate([scores[: count - run], last], axis=0)


def place_all(member, groups, refs, target, columns=slice(None), depth=None):
    for indices, ref in zip(groups, refs):
        for place, index in enumerate(indices):
            value = ref[place] if depth is None else ref[place, :depth]
            size = value.shape[0]
            start = pl.multiple_of((member ^ index) * size, size)
            target[pl.ds(start, size), columns] = value


def pick(first_ref, second_ref):
    half = pl.num_programs(0) // 2
    return jnp.where(pl.program_id(0) < half, first_ref[...], second_ref[...])


def project_kernel(groups, member_ref, xa_ref, xb_ref, cos_ref, sin_ref, *refs):
    pieces, rest = refs[:-7], refs[-7:]
    normed_ref, q_ref, k_ref, v_ref, raw_ref, weight_ref, gains_ref = rest
    depth = pieces[0].shape[1] - GAIN_ROWS

    @pl.when(pl.program_id(0) == 0)
    def _():
        place_all(member_ref[0], groups, pieces, weight_ref, depth=depth)
        gains = jnp.zeros(gains_ref.shape, jnp.float32)
        for piece in pieces:
            for place in range(piece.shape[0]):
                gains += piece[place, depth:].astype(jnp.float32)
        gains_ref[...] = gains

    unit, _ = unit_of(pick(xa_ref, xb_ref).astype(jnp.float32))
    normed = (unit * gains_ref[0:1, :]).astype(jnp.bfloat16)
    normed_ref[...] = normed
    product = dot(normed, weight_ref[...])
    raw_width = raw_ref.shape[1]
    raw_ref[...] = product[:, :raw_width]
    v_ref[...] = product[:, raw_width:].astype(jnp.bfloat16)
    cosine = cos_ref[...]
    sine = sin_ref[...]
    q_heads = q_ref.shape[1] // HD
    for head in range(raw_width // HD):
        unit, _ = unit_of(product[:, head * HD : (head + 1) * HD])
        target, place, row = (q_ref, head, 2) if head < q_heads else (k_ref, head - q_heads, 3)
        normed = unit * gains_ref[row : row + 1, :HD]
        rotated = normed * cosine + turn(normed) * sine
        target[:, place * HD : (place + 1) * HD] = rotated.astype(jnp.bfloat16)


def project(member, x_first, x_second, groups, pieces, cosine, sine, q_width, k_width):
    rows = cosine.shape[0]
    width = x_first.shape[1]
    block = rows // 4
    total = q_width + 2 * k_width
    bf16, f32 = jnp.bfloat16, jnp.float32

    def by_rows(i, member):
        return (i, 0)

    return call(
        "P",
        functools.partial(project_kernel, groups),
        4,
        member,
        [
            (x_first, (block, width), first_half),
            (x_second, (block, width), second_half),
            (cosine, (block, HD), by_rows),
            (sine, (block, HD), by_rows),
        ]
        + [whole(piece) for piece in pieces],
        [
            ((rows, width), bf16, (block, width), by_rows),
            ((rows, q_width), bf16, (block, q_width), by_rows),
            ((rows, k_width), bf16, (block, k_width), by_rows),
            ((rows, k_width), bf16, (block, k_width), by_rows),
            ((rows, q_width + k_width), f32, (block, q_width + k_width), by_rows),
            ((width, total), bf16, (width, total), None),
            ((GAIN_ROWS, width), f32, (GAIN_ROWS, width), None),
        ],
        [],
        2 * rows * width * total,
    )


def forward_kernel(
    block_of, q_ref, k_ref, v_ref, column_ref, row_ref, mixed_ref, lse_ref, keys, values, columns
):
    run = q_ref.shape[0] // 4
    sort_runs(block_of, run, (keys, k_ref), (values, v_ref), (columns, column_ref))
    for index in range(4):
        count = run * (index + 1)
        rows = pl.ds(pl.multiple_of(block_of[index] * run, run), run)
        visible = columns[pl.ds(count - run, run), :] <= row_ref[:, rows]
        for head in range(q_ref.shape[1] // HD):
            lanes = pl.ds(head * HD, HD)
            scores = raw_scores(keys[:count], q_ref[rows, lanes], visible, run)
            row_max = jnp.max(scores, axis=0, keepdims=True)
            raised = jnp.exp(scores - row_max)
            row_total = jnp.sum(raised, axis=0, keepdims=True)
            probs = (raised * (1.0 / row_total)).astype(jnp.bfloat16)
            mixed_ref[rows, lanes] = dot(probs, values[:count], TN).astype(jnp.bfloat16)
            lse_ref[pl.ds(head, 1), rows] = row_max + jnp.log(row_total)


def by_group(group, order):
    return (0, group)


def by_lead(group, order):
    return (group, 0, 0)


def attend(block_of, queries, keys, values, column, row):
    rows, width = keys.shape
    groups = width // HD
    pair = queries.shape[1] // groups
    return call(
        "attn",
        forward_kernel,
        groups,
        block_of,
        [
            (queries, (rows, pair), by_group),
            (keys, (rows, HD), by_group),
            (values, (rows, HD), by_group),
            whole(column),
            whole(row),
        ],
        [
            (queries.shape, jnp.bfloat16, (rows, pair), by_group),
            ((groups, pair // HD, rows), jnp.float32, (None, pair // HD, rows), by_lead),
        ],
        [
            pltpu.VMEM((rows, HD), jnp.bfloat16),
            pltpu.VMEM((rows, HD), jnp.bfloat16),
            pltpu.VMEM((rows, 1), jnp.int32),
        ],
        3 * rows * rows * queries.shape[1],
    )


def first_half(i, member):
    return (jnp.minimum(i, 1), 0)


def second_half(i, member):
    return (jnp.maximum(i - 2, 0), 0)


def store_halves(product, kept_ref, sent_ref):
    half = pl.num_programs(0) // 2

    @pl.when(pl.program_id(0) < half)
    def _():
        kept_ref[...] = product

    @pl.when(pl.program_id(0) >= half)
    def _():
        sent_ref[...] = product.astype(jnp.bfloat16)


def halves_out(rows, block, width):
    return [
        ((rows // 2, width), jnp.float32, (block, width), first_half),
        ((rows // 2, width), jnp.bfloat16, (block, width), second_half),
    ]


def out_kernel(groups, member_ref, mixed_ref, *refs):
    pieces, (kept_ref, sent_ref, weight_ref) = refs[:-3], refs[-3:]

    @pl.when(pl.program_id(0) == 0)
    def _():
        place_all(member_ref[0], groups, pieces, weight_ref)

    store_halves(dot(mixed_ref[...], weight_ref[...], NT), kept_ref, sent_ref)


def project_out(member, mixed, groups, pieces):
    rows, depth = mixed.shape
    block = rows // 4
    width = pieces[0].shape[1] * sum(piece.shape[0] for piece in pieces)
    return call(
        "out",
        functools.partial(out_kernel, groups),
        4,
        member,
        [(mixed, (block, depth), lambda i, member: (i, 0))] + [whole(piece) for piece in pieces],
        halves_out(rows, block, width)
        + [((width, depth), jnp.bfloat16, (width, depth), None)],
        [],
        2 * rows * width * depth,
    )


def back_kernel(starts, member_ref, xa_ref, xb_ref, *refs):
    grad_refs, (weight_ref, kept_ref, sent_ref, gain_ref) = refs[:-4], refs[-4:]
    product = None
    for start, grad_ref in zip(starts, grad_refs):
        term = dot(grad_ref[...], weight_ref[:, start : start + grad_ref.shape[1]], NT)
        product = term if product is None else product + term
    unit, _ = unit_of(pick(xa_ref, xb_ref).astype(jnp.float32))

    @pl.when(pl.program_id(0) == 0)
    def _():
        gain_ref[...] = jnp.zeros_like(gain_ref)

    gain_ref[...] += jnp.sum(product * unit, axis=0, keepdims=True)
    store_halves(product, kept_ref, sent_ref)


def project_back(member, x_first, x_second, starts, grads, weight):
    rows = grads[0].shape[0]
    block = rows // 4
    width, total = weight.shape
    return call(
        "pb",
        functools.partial(back_kernel, starts),
        4,
        member,
        [
            (x_first, (block, width), first_half),
            (x_second, (block, width), second_half),
        ]
        + [(grad, (block, grad.shape[1]), lambda i, member: (i, 0)) for grad in grads]
        + [whole(weight)],
        halves_out(rows, block, width) + [((1, width), jnp.float32, (1, width), None)],
        [],
        2 * rows * width * total,
    )


def mlp_kernel(member_ref, xa_ref, xb_ref, ga_ref, gb_ref, gate_up, down_ref, *rest):
    bf16 = jnp.bfloat16
    hidden_ref, grad_ref, kept_ref, sent_ref = rest
    width = down_ref.shape[1]
    x = pick(xa_ref, xb_ref)
    product = dot(x, gate_up[...])
    grad_hidden = dot(pick(ga_ref, gb_ref), down_ref[...])
    gate = product[:, :width]
    up = product[:, width:]
    sigmoid = jax.nn.sigmoid(gate)
    silu = gate * sigmoid
    hidden_ref[...] = (silu * up).astype(bf16)
    grad_gate = (grad_hidden * up * sigmoid * (1.0 + gate * (1.0 - sigmoid))).astype(bf16)
    grad_up = (grad_hidden * silu).astype(bf16)
    grad_ref[:, :width] = grad_gate
    grad_ref[:, width:] = grad_up
    grad_x = dot(grad_gate, gate_up[:, :width], NT) + dot(grad_up, gate_up[:, width:], NT)
    store_halves(grad_x, kept_ref, sent_ref)


def third_quarter(i, member):
    return (2 + jnp.minimum(i, 1), 0)


def fourth_quarter(i, member):
    return (jnp.maximum(i, 2), 0)


def feed(member, x_first, x_second, own_half, core_half, weight):
    rows, width = own_half.shape
    hidden_width = weight.shape[1] // 3
    block = rows // 4
    bf16 = jnp.bfloat16

    def by_rows(i, member):
        return (i, 0)

    return call(
        "mlp",
        mlp_kernel,
        4,
        member,
        [
            (x_first, (block, width), first_half),
            (x_second, (block, width), second_half),
            (own_half, (block, width), third_quarter),
            (core_half, (block, width), fourth_quarter),
            (weight, (width, 2 * hidden_width), lambda i, member: (0, 0)),
            (weight, (width, hidden_width), lambda i, member: (0, 2)),
        ],
        [
            ((rows, hidden_width), bf16, (block, hidden_width), by_rows),
            ((rows, 2 * hidden_width), bf16, (block, 2 * hidden_width), by_rows),
        ]
        + halves_out(rows, block, width),
        [],
        10 * rows * width * hidden_width,
    )


def mlp_out_kernel(member_ref, hidden_ref, weight_ref, kept_ref, sent_ref):
    store_halves(dot(hidden_ref[...], weight_ref[...], NT), kept_ref, sent_ref)


def feed_out(member, hidden, weight):
    rows, depth = hidden.shape
    width = weight.shape[0]
    block = rows // 4
    return call(
        "mo",
        mlp_out_kernel,
        4,
        member,
        [
            (hidden, (block, depth), lambda i, member: (i, 0)),
            (weight, (width, depth), lambda i, member: (0, 2)),
        ],
        halves_out(rows, block, width),
        [],
        2 * rows * width * depth,
    )


def weight_grad_kernel(layout, member_ref, *refs):
    inputs, (kept_ref, sent_ref, product) = refs[:-3], refs[-3:]
    half = product.shape[0] // 2
    start = place = 0
    for lefts, rights in layout:
        left_refs = inputs[place : place + lefts]
        right_refs = inputs[place + lefts : place + lefts + rights]
        place += lefts + rights
        for right_ref in right_refs:
            stop = start + right_ref.shape[1]
            total = None
            row = 0
            for left_ref in left_refs:
                count = left_ref.shape[0]
                term = dot(left_ref[...], right_ref[row : row + count, :], TN)
                total = term if total is None else total + term
                row += count
            product[:, start:stop] = total.astype(jnp.bfloat16)
            start = stop
    near = member_ref[0] % 2
    kept_ref[...] = product[pl.ds(pl.multiple_of(near * half, half), half), :]
    sent_ref[...] = product[pl.ds(pl.multiple_of((1 - near) * half, half), half), :]


def weight_grad(member, dp_size, parts, upper):
    width = parts[0][0][0].shape[1]
    pairs = dp_size // 2
    half = width // dp_size
    bits = pairs.bit_length() - 1
    inputs = []
    layout = []
    total = flops = 0

    def by_member(quarter, i, member):
        i = i + upper * (pairs // 2)
        turned = sum(((i >> bit) & 1) << (bits - 1 - bit) for bit in range(bits))
        return (quarter, (member[0] // 2) ^ turned)

    for lefts, quarter, rights in parts:
        rows = rights[0].shape[0]
        for left in lefts:
            index = functools.partial(by_member, quarter)
            inputs.append((left, (rows // len(lefts), 2 * half), index))
        inputs += [whole(right) for right in rights]
        layout.append((len(lefts), len(rights)))
        columns = sum(right.shape[1] for right in rights)
        total += columns
        flops += 2 * rows * width * columns
    result = (
        (pairs // 2, half, total),
        jnp.bfloat16,
        (None, half, total),
        lambda i, member: (i, 0, 0),
    )
    return call(
        "wg",
        functools.partial(weight_grad_kernel, layout),
        pairs // 2,
        member,
        inputs,
        [result, result],
        [pltpu.VMEM((2 * half, total), jnp.bfloat16)],
        flops,
    )


def norm_rope_back(grad, raw, cosine, sine, gain):
    grad_normed = grad * cosine - turn(grad) * sine
    unit, factor = unit_of(raw)
    gain_part = jnp.sum(grad_normed * unit, axis=0, keepdims=True)
    grad_unit = grad_normed * gain
    projected = jnp.mean(grad_unit * unit, axis=-1, keepdims=True)
    return ((factor * (grad_unit - unit * projected)).astype(jnp.bfloat16), gain_part)


def backward_kernel(
    block_of,
    q_ref,
    k_ref,
    v_ref,
    branch_a_ref,
    branch_b_ref,
    out_weight_ref,
    lse_ref,
    column_ref,
    row_ref,
    raw_q_ref,
    raw_k_ref,
    cos_ref,
    sin_ref,
    gains_ref,
    dq_ref,
    dk_ref,
    dv_ref,
    q_part_ref,
    k_part_ref,
    keys,
    values,
    columns,
    key_sum,
    value_sum,
    grad_mixed,
):
    run = q_ref.shape[0] // 4
    sort_runs(block_of, run, (keys, k_ref), (values, v_ref), (columns, column_ref))
    key_sum[...] = jnp.zeros_like(key_sum)
    value_sum[...] = jnp.zeros_like(value_sum)
    half = branch_a_ref.shape[0]
    grad_mixed[:half, :] = dot(branch_a_ref[...], out_weight_ref[...]).astype(jnp.bfloat16)
    grad_mixed[half:, :] = dot(branch_b_ref[...], out_weight_ref[...]).astype(jnp.bfloat16)
    q_part = jnp.zeros((1, HD), jnp.float32)
    k_part = jnp.zeros((1, HD), jnp.float32)
    q_gain = gains_ref[2:3, :HD]
    k_gain = gains_ref[3:4, :HD]
    for index in range(4):
        count = run * (index + 1)
        rows = pl.ds(pl.multiple_of(block_of[index] * run, run), run)
        visible = columns[pl.ds(count - run, run), :] <= row_ref[:, rows]
        for head in range(q_ref.shape[1] // HD):
            lanes = pl.ds(head * HD, HD)
            query = q_ref[rows, lanes]
            grad = grad_mixed[rows, lanes]
            scores = raw_scores(keys[:count], query, visible, run)
            probs = jnp.exp(scores - lse_ref[pl.ds(head, 1), rows])
            grad_probs = dot(values[:count], grad, NT)
            delta = jnp.sum(probs * grad_probs, axis=0, keepdims=True)
            grad_scores = (probs * (grad_probs - delta)).astype(jnp.bfloat16)
            value_sum[:count, :] += dot(probs.astype(jnp.bfloat16), grad)
            key_sum[:count, :] += dot(grad_scores, query)
            grad_query = dot(grad_scores, keys[:count], TN) * SCALE
            dq_ref[rows, lanes], part = norm_rope_back(
                grad_query, raw_q_ref[rows, lanes], cos_ref[rows, :], sin_ref[rows, :], q_gain
            )
            q_part += part
    for index in range(4):
        rows = pl.ds(pl.multiple_of(block_of[index] * run, run), run)
        sorted_rows = pl.ds(index * run, run)
        dk_ref[rows, :], part = norm_rope_back(
            key_sum[sorted_rows, :] * SCALE,
            raw_k_ref[rows, :],
            cos_ref[rows, :],
            sin_ref[rows, :],
            k_gain,
        )
        k_part += part
        dv_ref[rows, :] = value_sum[sorted_rows, :].astype(jnp.bfloat16)
    q_part_ref[...] = q_part
    k_part_ref[...] = k_part


def attend_back(
    group, block_of, queries, keys, values, branches, out_weight, lse, column, row, raw, cosine, sine, gains
):
    rows, width = keys.shape
    groups = width // HD
    pair = queries.shape[1] // groups
    first_key = queries.shape[1] // HD
    depth = out_weight.shape[0]
    bf16, f32 = jnp.bfloat16, jnp.float32
    part = ((1, HD), f32, (1, HD), None)

    def this_group(i, order):
        return (0, group)

    return call(
        "ab",
        backward_kernel,
        1,
        block_of,
        [
            (queries, (rows, pair), this_group),
            (keys, (rows, HD), this_group),
            (values, (rows, HD), this_group),
            whole(branches[0]),
            whole(branches[1]),
            (out_weight, (depth, pair), this_group),
            (lse, (None, pair // HD, rows), lambda i, order: (group, 0, 0)),
            whole(column),
            whole(row),
            (raw, (rows, pair), this_group),
            (raw, (rows, HD), lambda i, order: (0, first_key + group)),
            whole(cosine),
            whole(sine),
            whole(gains),
        ],
        [
            ((rows, pair), bf16, (rows, pair), None),
            ((rows, HD), bf16, (rows, HD), None),
            ((rows, HD), bf16, (rows, HD), None),
            part,
            part,
        ],
        [
            pltpu.VMEM((rows, HD), bf16),
            pltpu.VMEM((rows, HD), bf16),
            pltpu.VMEM((rows, 1), jnp.int32),
            pltpu.VMEM((rows, HD), f32),
            pltpu.VMEM((rows, HD), f32),
            pltpu.VMEM((rows, pair), bf16),
        ],
        3 * rows * rows * queries.shape[1],
    )


def finish_kernel(starts, side_ref, kept_ref, other_ref, *outputs):
    first = side_ref[0] == 0
    for start, target in zip(starts, outputs):
        width = target.shape[1] // 2
        kept = kept_ref[:, start : start + width]
        other = other_ref[: kept_ref.shape[0], start : start + width].astype(jnp.float32)
        target[:, :width] = jnp.where(first, kept, other)
        target[:, width:] = jnp.where(first, other, kept)


def finish(side, kept, other, columns):
    rows = kept.shape[0]
    return call(
        "fin",
        functools.partial(finish_kernel, [start for start, _ in columns]),
        1,
        side,
        [whole(kept), whole(other)],
        [
            ((rows, 2 * width), jnp.float32, (rows, 2 * width), None)
            for _, width in columns
        ],
        [],
        0,
    )


def swap(source, axis, size, bit=1):
    return lax.ppermute(source, axis, [(i, i ^ bit) for i in range(size)])


def after(source, *events):
    return lax.optimization_barrier((source, events))[0]


def group_body(
    dp_size,
    tokens,
    places,
    attn_gain,
    w_query,
    w_key,
    w_value,
    q_gain,
    k_gain,
    w_out,
    mlp_gain,
    w_gate,
    w_up,
    w_down,
    cotangent,
):
    bf16, f32 = jnp.bfloat16, jnp.float32
    run, width = tokens.shape[1:]
    side = lax.axis_index("ctx")
    core = lax.axis_index("tensor")
    member = lax.axis_index("dp")
    word = member[None]
    q_width = w_query.shape[1] // 2
    k_width = w_key.shape[1] // 2
    hidden_width = w_gate.shape[1] // 2
    z_bits = [1 << bit for bit in range(1, dp_size.bit_length() - 1)]
    near_steps = list(range(2, dp_size, 2))
    groups = [[0], near_steps, [1], [step ^ 1 for step in near_steps]]

    def over_core(source):
        return swap(source, "tensor", 2)

    def over_ctx(source):
        return swap(source, "ctx", 2)

    def over_dp(source, bit):
        return swap(source, "dp", dp_size, bit)

    def over_z(shard):
        return [over_dp(shard, step) for step in near_steps]

    def mine(source, axis):
        size = source.shape[axis] // 2
        return lax.dynamic_slice_in_dim(source, side * size, size, axis).astype(bf16)

    def as_rows(values, columns):
        high = values.astype(bf16)
        low = (values - high.astype(f32)).astype(bf16)
        digits = jnp.concatenate([high, low])
        return jnp.pad(digits, (0, GAIN_ROWS * columns - digits.shape[0])).reshape(GAIN_ROWS, columns)

    def from_rows(rows, count):
        digits = rows.reshape(-1).astype(f32)
        return digits[:count] + digits[count : 2 * count]

    gain_rows = jnp.zeros((GAIN_ROWS, width), bf16)
    for row, gain in enumerate((attn_gain, mlp_gain, q_gain, k_gain)):
        gain_rows = lax.dynamic_update_slice(
            gain_rows, gain.astype(bf16)[None], (row, member * gain.shape[0])
        )
    qkv_shard = jnp.concatenate([mine(w_query, 1), mine(w_key, 1), mine(w_value, 1)], axis=1)
    qkv_shard = jnp.concatenate([qkv_shard, gain_rows], axis=0)
    out_shard = mine(w_out, 0).T
    mlp_shard = jnp.concatenate([mine(w_gate, 1), mine(w_up, 1), mine(w_down, 0).T], axis=1)

    place_count = places.shape[1]
    digits = jnp.zeros((GAIN_ROWS, width), bf16)
    for row, digit in enumerate((places // 128, places % 128)):
        digits = lax.dynamic_update_slice(digits, digit.astype(bf16), (row, 0))
    message = jnp.concatenate([tokens[0], cotangent[0], digits], axis=0)
    events = {}

    def tied(name, source):
        names = [other for other in TIES.get(name, ()) if other in events]
        return after(source, *[events[other] for other in names]) if names else source

    def told(name, raw):
        events[name] = raw
        return raw

    qkv_near, qkv_far, message = lax.optimization_barrier(
        (over_z(qkv_shard), over_dp(qkv_shard, 1), over_ctx(message))
    )
    told("s0", message)
    qkv_near = jnp.stack(qkv_near)
    own_half = jnp.concatenate(
        [tokens[0], message[:run], cotangent[0], message[run : 2 * run]], axis=0
    )
    core_half = told("tok", over_core(tied("tok", own_half)))
    qkv_far_rest = told("a_x", over_dp(tied("a_x", qkv_near), 1))
    mlp_weight = lax.all_gather(
        after(tied("ag", mlp_shard), qkv_near), "dp", axis=0, tiled=True
    )
    out_near = told("o_z", over_z(after(tied("o_z", out_shard), qkv_near)))
    half = 2 * run
    digits = message[2 * run : 2 * run + 2, :place_count].astype(jnp.int32)
    other_places = (digits[0] * 128 + digits[1]).reshape(2, run)
    own_places = places[0].reshape(2, run)
    place_blocks = jnp.stack([own_places, other_places], axis=1)
    place_blocks = jnp.where(core == 0, place_blocks, place_blocks[::-1]).reshape(-1)
    place_column = place_blocks[:, None]
    place_row = place_blocks[None, :]
    home_side = jnp.array([0, 1, 1, 0], jnp.int32)
    home_core = jnp.array([0, 0, 1, 1], jnp.int32)
    block_of = (home_core ^ core) * 2 + (home_side ^ side)
    cosine, sine_table = (table[:, 0] for table in rope_tables(place_blocks))
    sine_table = sine_table * jnp.where(jnp.arange(HD) < HD // 2, -1.0, 1.0).astype(f32)
    own_half, core_half, cosine, sine_table, place_column, block_of = lax.optimization_barrier(
        (own_half, core_half, cosine, sine_table, place_column, block_of)
    )
    normed_one, queries, key_rows, value_rows, raw, qkv_weight, gains = project(
        word,
        tied("P", own_half),
        core_half,
        groups,
        [qkv_shard[None], qkv_near, qkv_far[None], qkv_far_rest],
        cosine,
        sine_table,
        q_width,
        k_width,
    )
    told("P", queries)
    out_near = jnp.stack([out_shard] + out_near)
    out_far = told("o_ax", over_dp(tied("o_ax", out_near), 1))
    mixed, lse_rows = attend(
        block_of, tied("attn", queries), key_rows, value_rows, place_column, place_row
    )
    told("attn", mixed)
    orders = [[0] + near_steps, [1] + [step ^ 1 for step in near_steps]]
    out_kept, out_sent, out_weight = project_out(
        word, tied("out", mixed), orders, [out_near, out_far]
    )

    def ctx_sum(name, summed):
        other = told(name, over_ctx(tied(name, summed.astype(bf16))))
        return summed + jnp.concatenate([other[run:], other[:run]], axis=0).astype(f32)

    source = own_half[:half].astype(f32)
    middle = source + ctx_sum("ar1", out_kept + over_core(out_sent).astype(f32))
    gain_two = gains[1]
    normed_two, unit_two, factor_two = norm_forward(middle, gain_two)
    normed_two = normed_two.astype(bf16)
    normed_other = over_core(normed_two)
    hidden, grad_gate_up, grad_kept, grad_sent = feed(
        word, tied("mlp", normed_two), normed_other, own_half, core_half, mlp_weight
    )

    def halves(block):
        size = block.shape[0] // 2
        kept = lax.dynamic_slice_in_dim(block, side * size, size, 0)
        sent = lax.dynamic_slice_in_dim(block, (1 - side) * size, size, 0)
        return kept, sent

    def summed(name, kept, sent, bit):
        received = told(name, over_dp(tied(name, sent.astype(bf16)), bit))
        return kept.astype(f32) + received.astype(f32)

    def summed_half(name, total, bit):
        count = total.shape[0] // 2
        return summed(name, total[:count], total[count:], bit)

    grad_other = told("mid_core", over_core(grad_sent))
    hidden, grad_gate_up, grad_other = lax.optimization_barrier((hidden, grad_gate_up, grad_other))
    grad_normed_two = grad_kept + grad_other.astype(f32)
    def m_grads(name, upper):
        pair = weight_grad(
            word,
            dp_size,
            [
                ([normed_two, normed_other], 0, [tied(name, grad_gate_up)]),
                ([own_half, core_half], 1, [hidden]),
            ],
            upper,
        )
        told(name, pair[1])
        return pair

    m_high = summed("m_x1", *m_grads("m_w1", 1), 1)
    m_pair = m_grads("m_w", 0)
    mlp_kept, mlp_sent = feed_out(word, tied("mo", hidden), mlp_weight)
    told("mo", mlp_sent)
    mlp_event = told("mo_core", over_core(tied("mo_core", mlp_sent)))
    grad_normed_two = ctx_sum("ar2", grad_normed_two)
    grad_source_two, _ = norm_backward(grad_normed_two, unit_two, factor_two, gain_two)
    grad_gain_two = jnp.sum(grad_normed_two[:run] * unit_two[:run], axis=0)
    grad_middle = own_half[half:].astype(f32) + grad_source_two
    branch = grad_middle.astype(bf16)
    branches = [branch, told("branch", over_core(tied("branch", branch)))]
    def back(name, group):
        result = attend_back(
            group,
            block_of,
            tied(name, queries),
            key_rows,
            value_rows,
            branches,
            out_weight,
            lse_rows,
            place_column,
            place_row,
            raw,
            cosine,
            sine_table,
            gains,
        )
        told(name, result[0])
        return result

    first_back = back("g0", 0)
    m_low = summed("m_x", *m_pair, 1)
    m_sum = summed("m_z1", m_low, m_high, z_bits[0])
    second_back = back("g1", 1)
    back_grads = [grads[part] for part in range(3) for grads in (first_back, second_back)]

    def a_grads(name, upper):
        pair = weight_grad(
            word,
            dp_size,
            [(branches, 0, [tied(name, mixed)]), ([normed_one], 0, back_grads)],
            upper,
        )
        told(name, pair[1])
        return pair

    a_high = summed("a_x1", *a_grads("a_w1", 1), 1)
    a_pair = a_grads("a_w", 0)
    m_sum = summed("m_z2", m_sum[0], m_sum[1], z_bits[1])
    q_half, k_half = q_width // 2, k_width // 2
    starts = [0, q_half, q_width, q_width + k_half, q_width + k_width, q_width + k_width + k_half]
    back_grads[0] = tied("pb", back_grads[0])
    one_kept, one_sent, grad_gain_one = project_back(
        word, own_half, core_half, starts, back_grads, qkv_weight
    )
    told("pb", one_sent)
    a_low = summed("a_x2", *a_pair, 1)
    one_event = told("one_core", over_core(tied("one_core", one_sent)))
    gain_grads = jnp.concatenate(
        [
            grad_gain_one[0],
            grad_gain_two,
            (first_back[3] + second_back[3])[0],
            (first_back[4] + second_back[4])[0],
        ]
    )
    gain_count = gain_grads.shape[0]
    gain_grads = gain_grads + told("gain_core", over_core(tied("gain_core", gain_grads)))
    gain_grads = gain_grads + told("gain_x", over_dp(tied("gain_x", gain_grads), 1))
    gain_grads = gain_grads + told("gain_z", over_dp(tied("gain_z", gain_grads), z_bits[0]))
    a_sum = summed("a_z1", a_low, a_high, z_bits[0])
    one_sum = one_kept + one_event.astype(f32)
    one_other = told("one_y", over_ctx(tied("one_y", one_sum[run:].astype(bf16))))
    grad_normed_one = one_sum[:run] + one_other.astype(f32)
    _, unit_one, factor_one = norm_forward(tokens[0].astype(f32), gains[0])
    grad_source_one, _ = norm_backward(grad_normed_one, unit_one, factor_one, gains[0])
    grad_tokens = grad_middle[:run] + grad_source_one

    mlp_part = tied("oth", mlp_kept) + mlp_event.astype(f32)
    other_part = told("oth", over_ctx(mlp_part[run:].astype(bf16)))
    layer_out = middle[:run] + mlp_part[:run] + tied("lo", other_part).astype(f32)

    def with_gains(blocks, gains):
        columns = blocks.shape[-1]
        return jnp.concatenate(
            [blocks.astype(bf16).reshape(-1, columns), as_rows(gains, columns)], axis=0
        )

    rows = a_sum.shape[1]
    mlp_kept, mlp_sent = halves(m_sum)
    mlp_other = told("m_y", over_ctx(tied("m_y", mlp_sent.astype(bf16))))
    received = told("a_z2", over_dp(tied("a_z2", with_gains(a_sum[1], gain_grads)), z_bits[1]))
    a_sum = a_sum[0] + received[:rows].astype(f32)
    gain_grads = gain_grads + from_rows(received[rows:], gain_count)
    attn_kept, attn_sent = halves(a_sum)
    received = over_ctx(tied("f_y", with_gains(attn_sent, gain_grads)))
    gain_grads = gain_grads + from_rows(received[rows // 2 :], gain_count)
    gate_grad, up_grad, down_grad = finish(
        side[None],
        mlp_kept,
        mlp_other,
        [(place * hidden_width, hidden_width) for place in range(3)],
    )
    out_grad, query_grad, key_grad, value_grad = finish(
        side[None],
        attn_kept,
        received,
        [
            (0, q_width),
            (q_width, q_width),
            (2 * q_width, k_width),
            (2 * q_width + k_width, k_width),
        ],
    )
    return (
        layer_out[None],
        grad_tokens[None],
        gain_grads[:width],
        query_grad,
        key_grad,
        value_grad,
        gain_grads[2 * width : 2 * width + HD],
        gain_grads[2 * width + HD :],
        out_grad.T,
        gain_grads[width : 2 * width],
        gate_grad,
        up_grad,
        down_grad.T,
    )


def plan(mesh):
    sizes = dict(mesh.shape)
    if sizes["ctx"] == 2 and sizes["tensor"] == 2 and sizes["dp"] == 8:
        return functools.partial(group_body, sizes["dp"])
    return split_body


def solution(mesh):
    in_specs = (
        P("dp", ("ctx", "tensor"), None),
        P("dp", "ctx"),
        P("dp"),
        P("dp", "tensor"),
        P("dp", "tensor"),
        P("dp", "tensor"),
        P("dp"),
        P("dp"),
        P("tensor", "dp"),
        P("dp"),
        P("dp", "tensor"),
        P("dp", "tensor"),
        P("tensor", "dp"),
        P("dp", ("ctx", "tensor"), None),
    )
    out_specs = (
        P("dp", ("ctx", "tensor"), None),
        P("dp", ("ctx", "tensor"), None),
        P(),
        P(("dp", "ctx"), "tensor"),
        P(("dp", "ctx"), "tensor"),
        P(("dp", "ctx"), "tensor"),
        P(),
        P(),
        P("tensor", ("dp", "ctx")),
        P(),
        P(("dp", "ctx"), "tensor"),
        P(("dp", "ctx"), "tensor"),
        P("tensor", ("dp", "ctx")),
    )
    return jax.shard_map(plan(mesh), mesh=mesh, in_specs=in_specs, out_specs=out_specs, check_vma=False)
```
